32 devices in a mesh: groups: 2 (over y), seq: 4 (over z), head: 2 (over x), side: 2 (over core).
Axes of the slice: x: 2, y: 2, z: 4, core: 2. Of those that a mesh axis runs over, the one named last changes fastest.
Arguments:
- hidden: bfloat16 [32, 8192], P('groups', ('seq', 'side')), parts along dimension 0
- gain: float32 [8192], P(('seq', 'side')), may hold values from 0.25 to 1.75
- w_query: bfloat16 [8192, 8192], P(('seq', 'side'), 'head')
- w_key: bfloat16 [8192, 1024], P(('seq', 'side'), 'head')
- w_value: bfloat16 [8192, 1024], P(('seq', 'side'), 'head'), may hold values from -0.0625 to 0.0625
- w_out: bfloat16 [8192, 8192], P('head', ('seq', 'side')), may hold values from -0.0625 to 0.0625
- prefix_keys: bfloat16 [2, 8, 32768, 128], P('groups', 'head', ('seq', 'side')), parts along dimension 0, may hold values from -6 to 6
- prefix_values: bfloat16 [2, 8, 32768, 128], P('groups', 'head', ('seq', 'side')), parts along dimension 0
- suffix_keys: bfloat16 [256, 8, 128, 128], P(('groups', 'seq', 'side'), 'head'), parts along dimension 0, may hold values from -15 to 15
- suffix_values: bfloat16 [256, 8, 128, 128], P(('groups', 'seq', 'side'), 'head'), parts along dimension 0, may hold values from -6 to 6
- suffix_lengths: int32 [32], P('groups'), parts along dimension 0, may hold values from 1 to 1024, 8192 in all
- page_table: int32 [32, 8], P('groups'), parts along dimension 0, may hold values from 0 to 15, as said below
Outputs:
- hidden_out: bfloat16 [32, 8192], P('groups', ('seq', 'side')), parts along dimension 0
- update: float32 [32, 8192], P('groups', ('seq', 'side')), parts along dimension 0
The draws below stay inside these ranges and needn't reach their ends.
There are 2 independent parts, one for each index of `groups`. The reference program is written for one: setup_inputs(seed, part) draws one part's arguments, and reference() takes and returns one part's arrays. A program takes and returns all parts, laid end to end along the dimension named above; an argument that names none is the same for every part. Nothing has to cross between parts.
Inputs may be any that keep to these rules, and one draw needn't show every extreme that they name: `suffix_lengths`: the lengths sum to 8192 and the longest is exactly 1024. `page_table`: entries are slots within the holding block (s // 2) xor 1; the 2 samples of one block of sample rows use every slot of their holding block exactly once.
All inputs are finite; a program needn't handle non-finite values.
Results may differ from the reference program's by a relative error of at most 0.0081.
Values may be sent and summed in bfloat16 or wider, within the bound.
No kernel may reach another device: no remote copies, remote signals or barrier semaphores. Data moves between devices by JAX's collectives and lax.ppermute only.
A program may use at most 128 MiB of HBM per device.

```python
import math
import jax
import jax.numpy as jnp
import numpy as np
from jax import lax

D = 8192
QH = 64
KVH = 8
HD = 128
GROUP = 8
SAMP_DEV = 2
GEN = 16
SAMPLES = 16
PROMPTS = 1
PREFIX = 32768
SUFFIX = 1024
PAGE = 128
PAGES = 8
SLOTS_DEV = 16
POOL = 128
STEPS = 3


def draw_hidden(key, part):
    base = jnp.clip(jax.random.normal(key, (SAMPLES, D), jnp.float32), -6.0, 6.0)
    column = jnp.arange(D, dtype=jnp.float32) / D
    ramp = 1.0 + 2.0 * column
    return (base * ramp).astype(jnp.bfloat16)


def head_ranks(key):
    return jax.random.permutation(jax.random.fold_in(key, 13), KVH)


def head_signs(key):
    rank = head_ranks(key)
    return jnp.where(rank % 2 == 0, -1.0, 1.0).astype(jnp.float32)


def projection_pair(key):
    query = jax.random.normal(jax.random.fold_in(key, 11), (D, QH * HD), jnp.float32) / math.sqrt(D)
    noise = jax.random.normal(jax.random.fold_in(key, 12), (D, KVH * HD), jnp.float32) / math.sqrt(D)
    grouped = query.reshape(D, KVH, GROUP, HD).mean(axis=2).reshape(D, KVH * HD)
    signs = jnp.repeat(head_signs(key), HD)[None, :]
    keyed = 6.0 * signs * grouped + noise
    return (query, keyed)


def draw_w_query(key, part):
    return projection_pair(key)[0].astype(jnp.bfloat16)


def draw_w_key(key, part):
    return projection_pair(key)[1].astype(jnp.bfloat16)


def draw_prefix_values(key, part):
    shape = (PROMPTS, KVH, PREFIX, HD)
    center = 0.5 * jax.random.normal(jax.random.fold_in(key, 21), (PROMPTS, KVH, 1, HD), jnp.float32)
    noise = jnp.clip(jax.random.normal(jax.random.fold_in(key, 22), shape, jnp.float32), -5.0, 5.0)
    return jnp.clip(center + noise, -6.0, 6.0).astype(jnp.bfloat16)


def draw_page_table(key, part):
    blocks = SAMPLES // SAMP_DEV
    keys = jax.random.split(key, blocks)
    perms = jax.vmap(lambda one: jax.random.permutation(one, SLOTS_DEV))(keys)
    return perms.reshape(SAMPLES, PAGES).astype(jnp.int32)


def block_scale(stream_key, dims, shards, least, top_value):
    def one(dim, parts):
        draws = jax.random.uniform(jax.random.fold_in(jax.random.fold_in(stream_key, 6), dim), (parts,), jnp.float32, least / len(shards), top_value / len(shards))
        return jnp.repeat(jnp.exp(draws), dims[dim] // parts).reshape((-1,) + (1,) * (len(dims) - dim - 1))

    level = one(*shards[0])
    for cut in shards[1:]:
        level = level * one(*cut)
    return level


def split_up(amount, total, most, skew):
    weights = [(1 << 20) // math.isqrt(standing ** skew) + 1 for standing in range(2, amount + 1)]
    surplus, counts = total - most - (amount - 1), [1] * (amount - 1)
    while surplus > 0:
        candidates = [i for i in range(amount - 1) if counts[i] < most]
        mass, left = sum([weights[i] for i in candidates]), surplus
        for i in candidates:
            addition = min(most - counts[i], max(1, left * weights[i] // mass), surplus)
            counts[i] = counts[i] + addition
            surplus = surplus - addition
    return np.array([most] + counts)


def ragged_sizes(own_key, count, total, reach, slope):
    if count == 2:
        one = jax.random.randint(own_key, (), max(1, total - reach), min(reach, total - 1) + 1)
        return jnp.stack([one, total - one])
    sizes = jnp.asarray(split_up(count, total, reach, slope), jnp.int32)
    twos = (count - 1) // 2
    donor, taker = sizes[1:1 + 2 * twos:2], sizes[2:2 + 2 * twos:2]
    margin = jnp.minimum(donor - 1, reach - taker)
    shifted = jax.random.randint(jax.random.fold_in(own_key, 1), (twos,), 0, 1 << 20) % (margin + 1)
    sizes = sizes.at[1:1 + 2 * twos:2].set(donor - shifted).at[2:2 + 2 * twos:2].set(taker + shifted)
    return sizes[jax.random.permutation(jax.random.fold_in(own_key, 2), count)]


def bell_draw(rng, dims, deviation, limit, cuts=(), kind=jnp.bfloat16):
    level = block_scale(rng, dims, cuts, -0.22, 0.18) if cuts else 1.0
    values = jax.random.normal(rng, dims, jnp.float32) * deviation * level
    return jnp.minimum(jnp.maximum(values, -limit), limit).astype(kind)


def setup_inputs(seed: int = 0, part: int = 0) -> dict:
    seeds = jax.random.split(jax.random.key(seed), 13)
    part_splits = jax.random.split(jax.random.fold_in(seeds[12], part), 13)
    hidden = draw_hidden(jax.random.fold_in(jax.random.fold_in(seeds[12], part), 71), part)
    gain = jnp.clip(1.0 + 0.15 * jax.random.normal(seeds[1], (D,), jnp.float32), 0.25, 1.75)
    w_query = draw_w_query(jax.random.fold_in(seeds[12], 71), part)
    w_key = draw_w_key(jax.random.fold_in(seeds[12], 71), part)
    w_value = bell_draw(seeds[4], (D, KVH * HD), D ** -0.5, 0.0625, ((0, 8), (1, 2)))
    w_out = bell_draw(seeds[5], (QH * HD, D), (QH * HD) ** -0.5, 0.0625, ((0, 2), (1, 8)))
    prefix_keys = bell_draw(part_splits[6], (PROMPTS, KVH, PREFIX, HD), 1.0, 6.0, ((1, 2), (2, 8)))
    prefix_values = draw_prefix_values(jax.random.fold_in(jax.random.fold_in(seeds[12], part), 71), part)
    suffix_keys = bell_draw(part_splits[8], (POOL, KVH, PAGE, HD), 2.5, 15.0, ((0, 8), (1, 2)))
    suffix_values = bell_draw(part_splits[9], (POOL, KVH, PAGE, HD), 1.0, 6.0, ((0, 8), (1, 2)))
    suffix_lengths = ragged_sizes(part_splits[10], SAMPLES, SAMPLES * SUFFIX // 2, SUFFIX, 2).astype(jnp.int32)
    page_table = draw_page_table(jax.random.fold_in(jax.random.fold_in(seeds[12], part), 71), part)
    return dict(hidden=hidden, gain=gain, w_query=w_query, w_key=w_key, w_value=w_value, w_out=w_out, prefix_keys=prefix_keys, prefix_values=prefix_values, suffix_keys=suffix_keys, suffix_values=suffix_values, suffix_lengths=suffix_lengths, page_table=page_table)


def rotate(vectors, position):
    half = vectors.shape[-1] // 2
    freq = 500000.0 ** (-(jnp.arange(half, dtype=jnp.float32) * 2.0 / vectors.shape[-1]))
    angle = position[..., None] * freq
    cosine = jnp.cos(angle)
    sine = jnp.sin(angle)
    lower = vectors[..., :half]
    upper = vectors[..., half:]
    return jnp.concatenate([lower * cosine - upper * sine, upper * cosine + lower * sine], axis=-1)

def rounded(weights):
    return lax.optimization_barrier(weights.astype(jnp.bfloat16)).astype(jnp.float32)

def reference(hidden, gain, w_query, w_key, w_value, w_out, prefix_keys, prefix_values, suffix_keys, suffix_values, suffix_lengths, page_table):
    scale = 1.0 / math.sqrt(HD)
    holder = jnp.bitwise_xor(jnp.arange(SAMPLES, dtype=jnp.int32) // SAMP_DEV, 1)
    slots = (holder[:, None] * SLOTS_DEV + page_table).astype(jnp.int32)
    page_keys = suffix_keys[slots].reshape(PROMPTS, GEN, PAGES, KVH, PAGE, HD)
    page_values = suffix_values[slots].reshape(PROMPTS, GEN, PAGES, KVH, PAGE, HD)
    lengths = suffix_lengths.reshape(PROMPTS, GEN)
    w_proj = jnp.concatenate([w_query, w_key, w_value], axis=1)
    query_width = QH * HD
    key_width = KVH * HD
    state = hidden
    update = jnp.zeros((SAMPLES, D), jnp.float32)
    new_keys = []
    new_values = []
    for step in range(STEPS):
        wide = state.astype(jnp.float32)
        scaled = (wide * gain).astype(jnp.bfloat16)
        proj = jnp.dot(scaled, w_proj, preferred_element_type=jnp.float32)
        inverse = lax.rsqrt(lax.optimization_barrier(jnp.mean(wide * wide, axis=1)) + 1e-05)[:, None]
        position = (PREFIX + suffix_lengths + step).astype(jnp.float32)
        query = rotate((proj[:, :query_width] * inverse).reshape(SAMPLES, KVH, GROUP, HD), position[:, None, None]).astype(jnp.bfloat16)
        new_keys.append(rotate((proj[:, query_width:query_width + key_width] * inverse).reshape(SAMPLES, KVH, HD), position[:, None]).astype(jnp.bfloat16))
        new_values.append((proj[:, query_width + key_width:] * inverse).reshape(SAMPLES, KVH, HD).astype(jnp.bfloat16))
        fresh_k = jnp.stack(new_keys, axis=1).reshape(PROMPTS, GEN, step + 1, KVH, HD)
        fresh_v = jnp.stack(new_values, axis=1).reshape(PROMPTS, GEN, step + 1, KVH, HD)

        def one_prompt(items):
            query_p, pre_k, pre_v, suf_k, suf_v, length_p, new_k, new_v = items
            qf = query_p.astype(jnp.float32)
            s_pre = jnp.einsum('gkhd,kld->gkhl', qf, pre_k.astype(jnp.float32)) * scale
            s_suf = jnp.einsum('gkhd,gpkjd->gkhpj', qf, suf_k.astype(jnp.float32)).reshape(GEN, KVH, GROUP, SUFFIX) * scale
            live = (jnp.arange(SUFFIX, dtype=jnp.int32)[None, :] < length_p[:, None])[:, None, None, :]
            s_suf = jnp.where(live, s_suf, -jnp.inf)
            s_new = jnp.einsum('gkhd,gukd->gkhu', qf, new_k.astype(jnp.float32)) * scale
            top = jnp.maximum(jnp.maximum(lax.optimization_barrier(jnp.max(s_pre, axis=-1)), lax.optimization_barrier(jnp.max(s_suf, axis=-1))), lax.optimization_barrier(jnp.max(s_new, axis=-1)))
            e_pre = jnp.exp(s_pre - top[..., None])
            e_suf = jnp.exp(s_suf - top[..., None])
            e_new = jnp.exp(s_new - top[..., None])
            total = lax.optimization_barrier(jnp.sum(e_pre, axis=-1)) + lax.optimization_barrier(jnp.sum(e_suf, axis=-1)) + lax.optimization_barrier(jnp.sum(e_new, axis=-1))
            acc = jnp.einsum('gkhl,kld->gkhd', rounded(e_pre), pre_v.astype(jnp.float32))
            acc = acc + jnp.einsum('gkhpj,gpkjd->gkhd', rounded(e_suf).reshape(GEN, KVH, GROUP, PAGES, PAGE), suf_v.astype(jnp.float32))
            acc = acc + jnp.einsum('gkhu,gukd->gkhd', rounded(e_new), new_v.astype(jnp.float32))
            return (acc / total[..., None]).astype(jnp.bfloat16)
        mixed = lax.map(one_prompt, (query.reshape(PROMPTS, GEN, KVH, GROUP, HD), prefix_keys, prefix_values, page_keys, page_values, lengths, fresh_k, fresh_v))
        mixed = mixed.reshape(SAMPLES, query_width)
        delta = jnp.dot(mixed, w_out, preferred_element_type=jnp.float32)
        update = update + delta
        state = (wide + delta).astype(jnp.bfloat16)
    return (state, update)
```

```python
import functools
import math

import jax
import jax.numpy as jnp
from jax import lax
from jax.experimental import pallas as pl
from jax.experimental.pallas import tpu as pltpu
from jax.sharding import PartitionSpec as P

D = 8192
HD = 128
GROUP = 8
SAMP_DEV = 2
PREFIX = 32768
STEPS = 3


def combined_all(array, axis, combine):
    everything = jax.tree.map(lambda part: lax.all_gather(part, axis), array)
    first = jax.tree.map(lambda part: part[0], everything)

    def lap(k, so_far):
        return combine(so_far, jax.tree.map(lambda part: part[k], everything))

    return lax.fori_loop(1, lax.axis_size(axis), lap, first)


def rotate(vectors, position):
    half = vectors.shape[-1] // 2
    freq = 500000.0 ** (-(jnp.arange(half, dtype=jnp.float32) * 2.0 / vectors.shape[-1]))
    angle = position[..., None] * freq
    cosine = jnp.cos(angle)
    sine = jnp.sin(angle)
    lower = vectors[..., :half]
    upper = vectors[..., half:]
    return jnp.concatenate([lower * cosine - upper * sine, upper * cosine + lower * sine], axis=-1)


def combine(first, second):
    acc_a, top_a, total_a = first
    acc_b, top_b, total_b = second
    top = jnp.maximum(top_a, top_b)
    weight_a = jnp.exp(top_a - top)
    weight_b = jnp.exp(top_b - top)
    return (
        acc_a * weight_a[..., None] + acc_b * weight_b[..., None],
        top,
        total_a * weight_a + total_b * weight_b,
    )


def local_any(
    hidden,
    gain,
    w_query,
    w_key,
    w_value,
    w_out,
    prefix_keys,
    prefix_values,
    suffix_keys,
    suffix_values,
    suffix_lengths,
    page_table,
):
    samples = hidden.shape[0]
    kv_local = w_key.shape[1] // HD
    query_width = kv_local * GROUP * HD
    key_width = kv_local * HD
    prompts = prefix_keys.shape[0]
    scale = 1.0 / math.sqrt(HD)
    rank = lax.axis_index(("seq", "side"))
    w_proj = jnp.concatenate([w_query, w_key, w_value], axis=1)
    pool_keys, pool_values = (suffix_keys, suffix_values)
    start = jnp.bitwise_xor(rank, 1) * SAMP_DEV
    table_rows = lax.dynamic_slice_in_dim(page_table, start, SAMP_DEV, 0)
    page_keys = pool_keys[table_rows]
    page_values = pool_values[table_rows]
    length_rows = lax.dynamic_slice_in_dim(suffix_lengths, start, SAMP_DEV, 0)
    page_count = page_keys.shape[1]
    page_size = page_keys.shape[3]
    suffix_span = page_count * page_size
    live = (jnp.arange(suffix_span, dtype=jnp.int32)[None, :] < length_rows[:, None])[
        :, None, None, :
    ]
    state = hidden
    update = jnp.zeros(hidden.shape, jnp.float32)
    new_keys = []
    new_values = []
    for step in range(STEPS):
        wide = state.astype(jnp.float32)
        scaled = (wide * gain).astype(jnp.bfloat16)
        partial_value = jnp.dot(scaled, w_proj, preferred_element_type=jnp.float32)
        squares = jnp.sum(wide * wide, axis=1)
        proj, total_sq = lax.psum((partial_value, squares), ("seq", "side"))
        inverse = lax.rsqrt(total_sq / D + 1e-05)[:, None]
        position = (PREFIX + suffix_lengths + step).astype(jnp.float32)
        query = rotate(
            (proj[:, :query_width] * inverse).reshape(samples, kv_local, GROUP, HD),
            position[:, None, None],
        ).astype(jnp.bfloat16)
        new_keys.append(
            rotate(
                (proj[:, query_width : query_width + key_width] * inverse).reshape(
                    samples, kv_local, HD
                ),
                position[:, None],
            ).astype(jnp.bfloat16)
        )
        new_values.append(
            (proj[:, query_width + key_width :] * inverse)
            .reshape(samples, kv_local, HD)
            .astype(jnp.bfloat16)
        )
        stacked_keys = jnp.stack(new_keys, axis=1)
        stacked_values = jnp.stack(new_values, axis=1)
        grouped = query.reshape(prompts, samples // prompts, kv_local, GROUP, HD)
        scores = (
            jnp.einsum(
                "pgkhd,pkld->pgkhl", grouped, prefix_keys, preferred_element_type=jnp.float32
            )
            * scale
        )
        top = jnp.max(scores, axis=-1)
        expo = jnp.exp(scores - top[..., None])
        total = jnp.sum(expo, axis=-1)
        acc = jnp.einsum(
            "pgkhl,pkld->pgkhd",
            expo.astype(jnp.bfloat16),
            prefix_values,
            preferred_element_type=jnp.float32,
        )
        acc = acc.reshape(samples, kv_local, GROUP, HD)
        top = top.reshape(samples, kv_local, GROUP)
        total = total.reshape(samples, kv_local, GROUP)
        own_query = lax.dynamic_slice_in_dim(query, start, SAMP_DEV, 0)
        own_keys = lax.dynamic_slice_in_dim(stacked_keys, start, SAMP_DEV, 0)
        own_values = lax.dynamic_slice_in_dim(stacked_values, start, SAMP_DEV, 0)
        suffix_scores = jnp.einsum(
            "skhd,spkjd->skhpj", own_query, page_keys, preferred_element_type=jnp.float32
        )
        suffix_scores = suffix_scores.reshape(SAMP_DEV, kv_local, GROUP, suffix_span) * scale
        suffix_scores = jnp.where(live, suffix_scores, -jnp.inf)
        fresh_scores = (
            jnp.einsum("skhd,sukd->skhu", own_query, own_keys, preferred_element_type=jnp.float32)
            * scale
        )
        peak = jnp.maximum(jnp.max(suffix_scores, axis=-1), jnp.max(fresh_scores, axis=-1))
        suffix_expo = jnp.exp(suffix_scores - peak[..., None])
        fresh_expo = jnp.exp(fresh_scores - peak[..., None])
        near_total = jnp.sum(suffix_expo, axis=-1) + jnp.sum(fresh_expo, axis=-1)
        near_acc = jnp.einsum(
            "skhpj,spkjd->skhd",
            suffix_expo.astype(jnp.bfloat16).reshape(
                SAMP_DEV, kv_local, GROUP, page_count, page_size
            ),
            page_values,
            preferred_element_type=jnp.float32,
        )
        near_acc = near_acc + jnp.einsum(
            "skhu,sukd->skhd",
            fresh_expo.astype(jnp.bfloat16),
            own_values,
            preferred_element_type=jnp.float32,
        )
        rows_now = (
            lax.dynamic_slice_in_dim(acc, start, SAMP_DEV, 0),
            lax.dynamic_slice_in_dim(top, start, SAMP_DEV, 0),
            lax.dynamic_slice_in_dim(total, start, SAMP_DEV, 0),
        )
        joined = combine(rows_now, (near_acc, peak, near_total))
        acc = lax.dynamic_update_slice_in_dim(acc, joined[0], start, 0)
        top = lax.dynamic_update_slice_in_dim(top, joined[1], start, 0)
        total = lax.dynamic_update_slice_in_dim(total, joined[2], start, 0)
        acc, top, total = combined_all((acc, top, total), ("seq", "side"), combine)
        mixed = (acc / total[..., None]).astype(jnp.bfloat16).reshape(samples, query_width)
        part = jnp.dot(mixed, w_out, preferred_element_type=jnp.float32)
        delta = lax.psum(part, "head")
        update = update + delta
        state = (wide + delta).astype(jnp.bfloat16)
    return (state, update)


LANES = 128
LOG2E = 1.4426950408889634
BF16 = jnp.bfloat16
F32 = jnp.float32
VMEM_SPEC = pl.BlockSpec(memory_space=pltpu.VMEM)
SMEM_SPEC = pl.BlockSpec(memory_space=pltpu.SMEM)
PARAMS = pltpu.CompilerParams(vmem_limit_bytes=20 * 1024 * 1024)


def resident(array):
    return pltpu.with_memory_space_constraint(array, pltpu.VMEM)


def lanes(rows):
    return lax.broadcasted_iota(jnp.int32, (rows, LANES), 1)


def pieces(values):
    high = values.astype(BF16).astype(F32)
    middle = (values - high).astype(BF16).astype(F32)
    return high, middle, values - high - middle


def bias_kernel(place, lengths, table, bias):
    pages = table.shape[1]
    page = bias.shape[2] // (SAMP_DEV * pages)
    row = lax.broadcasted_iota(jnp.int32, (bias.shape[1], page), 0)
    column = lax.broadcasted_iota(jnp.int32, (bias.shape[1], page), 1)
    for pool in range(2):
        for j in range(SAMP_DEV):
            sample = place[2 + pool] + j
            mine = row % SAMP_DEV == j
            for p in range(pages):
                live = mine & (column < lengths[sample] - p * page)
                spot = pl.ds(pl.multiple_of(table[sample, p] * page, page), page)
                bias[pool, :, spot] = jnp.where(live, 0.0, -jnp.inf)


def live_bias(place, lengths, table, page):
    tokens = SAMP_DEV * table.shape[1] * page
    return pl.pallas_call(
        bias_kernel,
        out_shape=jax.ShapeDtypeStruct((2, SAMP_DEV * GROUP, tokens), F32),
        in_specs=[SMEM_SPEC] * 3,
        out_specs=VMEM_SPEC,
        compiler_params=PARAMS,
    )(place, lengths, table)


def project_kernel(first, place, *refs):
    if first:
        x_ref, gain, w_query, w_key, w_value, keep, give = refs
        wide = x_ref[...].astype(F32)
    else:
        x_ref, gain, w_query, w_key, w_value, sum_ref, mine, other = refs[:8]
        keep, give, new_x, new_sum = refs[8:]
        delta = mine[...] + other[...]
        new_sum[...] = sum_ref[...] + delta
        state = (x_ref[...].astype(F32) + delta).astype(BF16)
        new_x[...] = state
        wide = state.astype(F32)
    scaled = (wide * gain[...]).astype(BF16)
    squares = jnp.sum(wide * wide, axis=1, keepdims=True)
    column = lanes(wide.shape[0])
    query = w_query.shape[1] // 2
    key = w_key.shape[1] // 2
    side = place[0]
    for out, who in ((give, 1 - side), (keep, side)):
        tile = min(1024, query)
        for at in range(0, query, tile):
            columns = pl.ds(pl.multiple_of(who * query + at, tile), tile)
            out[:, at : at + tile] = jnp.dot(
                scaled, w_query[:, columns], preferred_element_type=F32
            )
        columns = pl.ds(pl.multiple_of(who * key, key), key)
        out[:, query : query + key] = jnp.dot(
            scaled, w_key[:, columns], preferred_element_type=F32
        )
        out[:, query + key : query + 2 * key] = jnp.dot(
            scaled, w_value[:, columns], preferred_element_type=F32
        )
        out[:, query + 2 * key :] = jnp.where(column == 0, squares, 0.0)


def project(place, x, gain, weights, rest):
    rows = x.shape[0]
    width = sum(w.shape[1] for w in weights) // 2 + LANES
    halves = [jax.ShapeDtypeStruct((rows, width), F32)] * 2
    out_shape = halves if not rest else halves + [
        jax.ShapeDtypeStruct(x.shape, BF16),
        jax.ShapeDtypeStruct(x.shape, F32),
    ]
    return pl.pallas_call(
        functools.partial(project_kernel, not rest),
        out_shape=out_shape,
        in_specs=[SMEM_SPEC] + [VMEM_SPEC] * (5 + len(rest)),
        out_specs=[VMEM_SPEC] * len(out_shape),
        compiler_params=PARAMS,
    )(place, x, gain, *weights, *rest)


def pair_sum_kernel(keep, got, total, sent):
    both = keep[...] + got[...]
    total[...] = both
    main = both.shape[1] - LANES
    sent[:, :main] = both[:, :main].astype(BF16)
    column = lanes(both.shape[0])
    high, middle, low = pieces(both[:, main : main + 1])
    sent[:, main:] = jnp.where(
        column == 0, high, jnp.where(column == 1, middle, jnp.where(column == 2, low, 0.0))
    ).astype(BF16)


def pair_sum(keep, got):
    return pl.pallas_call(
        pair_sum_kernel,
        out_shape=[
            jax.ShapeDtypeStruct(keep.shape, F32),
            jax.ShapeDtypeStruct(keep.shape, BF16),
        ],
        in_specs=[VMEM_SPEC] * 2,
        out_specs=[VMEM_SPEC] * 2,
        compiler_params=PARAMS,
    )(keep, got)


def attend_kernel(features, step, others, place, *refs):
    total_ref = refs[0]
    got = refs[1 : 1 + others]
    cos_ref, sin_ref, bias_ref = refs[1 + others : 4 + others]
    pk, pv, sk, sv, got_pk, got_pv, got_sk, got_sv = refs[4 + others : 12 + others]
    old = refs[12 + others : 12 + others + step]
    sent, stat, fresh = refs[12 + others + step :]
    rows = total_ref.shape[0]
    heads = got_pk.shape[1]
    width = total_ref.shape[1] - LANES
    query_width = width - 2 * heads * HD
    side, base, first_own, first_got = place[0], place[1], place[2], place[3]
    span = 2 * SAMP_DEV
    scale = LOG2E / math.sqrt(HD)

    stats = total_ref[:, width : width + 1]
    for ref in got:
        stats = stats + jnp.sum(ref[:, width:].astype(F32), axis=1, keepdims=True)
    inverse = lax.rsqrt(stats / features + 1e-05)
    cosine = cos_ref[...]
    sine = sin_ref[...]

    def block(at):
        value = total_ref[:, at : at + HD]
        for ref in got:
            value = value + ref[:, at : at + HD].astype(F32)
        return value * inverse

    def turned(at):
        value = block(at)
        return (value * cosine + pltpu.roll(value, HD // 2, 1) * sine).astype(BF16)

    sample = lax.broadcasted_iota(jnp.int32, (rows, 1), 0)
    owned = (sample >= base) & (sample < base + span)
    pick_row = lax.broadcasted_iota(jnp.int32, (SAMP_DEV * GROUP, GROUP * rows), 0)
    pick_column = lax.broadcasted_iota(jnp.int32, (SAMP_DEV * GROUP, GROUP * rows), 1)
    spot = (pick_row // SAMP_DEV) * rows + pick_row % SAMP_DEV
    stat_value = jnp.zeros((rows, LANES), F32)
    column = lanes(rows)

    for head in range(heads):
        queries = [turned((head * GROUP + g) * HD) for g in range(GROUP)]
        packed = jnp.concatenate(queries, axis=0)
        new_key = turned(query_width + head * HD)
        new_value = block(query_width + (heads + head) * HD).astype(BF16)
        fresh[:, head * HD : (head + 1) * HD] = new_key
        fresh[:, (heads + head) * HD : (heads + head + 1) * HD] = new_value
        keys = [ref[:, head * HD : (head + 1) * HD].astype(F32) for ref in old]
        values = [
            ref[:, (heads + head) * HD : (heads + head + 1) * HD].astype(F32) for ref in old
        ]
        keys.append(new_key.astype(F32))
        values.append(new_value.astype(F32))

        near = []
        for pool, (key_pool, value_pool, at, start) in enumerate(
            (
                (sk, sv, side * heads + head, first_own),
                (got_sk, got_sv, head, first_got),
            )
        ):
            tokens = key_pool.shape[0] * key_pool.shape[2]
            pick = (pick_column == spot + start).astype(F32).astype(BF16)
            few = jnp.dot(pick, packed, preferred_element_type=F32).astype(BF16)
            score = lax.dot_general(
                few,
                key_pool[:, at].reshape(tokens, HD),
                (((1,), (1,)), ((), ())),
                preferred_element_type=F32,
            )
            score = score * scale + bias_ref[pool]
            top = jnp.max(score, axis=1, keepdims=True)
            expo = jnp.exp2(score - top)
            near.append(
                (
                    start,
                    top,
                    jnp.sum(expo, axis=1, keepdims=True),
                    jnp.dot(
                        expo.astype(BF16),
                        value_pool[:, at].reshape(tokens, HD),
                        preferred_element_type=F32,
                    ),
                )
            )
        tops, totals, sums = [], [], []
        for g in range(GROUP):
            top = jnp.full((rows, 1), -1e30, F32)
            total = jnp.zeros((rows, 1), F32)
            acc = jnp.zeros((rows, HD), F32)
            for start, near_top, near_total, near_acc in near:
                for j in range(SAMP_DEV):
                    line = slice(g * SAMP_DEV + j, g * SAMP_DEV + j + 1)
                    here = sample == start + j
                    top = jnp.where(here, near_top[line], top)
                    total = jnp.where(here, near_total[line], total)
                    acc = jnp.where(here, near_acc[line], acc)
            wide_query = queries[g].astype(F32)
            scores = [
                jnp.sum(wide_query * key, axis=1, keepdims=True) * scale for key in keys
            ]
            peak = top
            for score in scores:
                peak = jnp.maximum(peak, score)
            peak = jnp.where(owned, peak, top)
            shrink = jnp.exp2(top - peak)
            total = total * shrink
            acc = acc * shrink
            for score, value in zip(scores, values):
                expo = jnp.where(owned, jnp.exp2(jnp.where(owned, score - peak, 0.0)), 0.0)
                total = total + expo
                acc = acc + expo.astype(BF16).astype(F32) * value
            tops.append(peak)
            totals.append(total)
            sums.append(acc)
        top = jnp.concatenate(tops, axis=0)
        total = jnp.concatenate(totals, axis=0)
        acc = jnp.concatenate(sums, axis=0)

        length = pk.shape[2]
        chunk = min(2048, length)
        for key_ref, value_ref, at in ((pk, pv, side * heads + head), (got_pk, got_pv, head)):
            for begin in range(0, length, chunk):
                score = lax.dot_general(
                    packed,
                    key_ref[0, at, begin : begin + chunk],
                    (((1,), (1,)), ((), ())),
                    preferred_element_type=F32,
                )
                score = score * scale
                peak = jnp.maximum(top, jnp.max(score, axis=1, keepdims=True))
                shrink = jnp.exp2(top - peak)
                expo = jnp.exp2(score - peak)
                total = total * shrink + jnp.sum(expo, axis=1, keepdims=True)
                acc = acc * shrink + jnp.dot(
                    expo.astype(BF16),
                    value_ref[0, at, begin : begin + chunk],
                    preferred_element_type=F32,
                )
                top = peak
        mean = acc / total
        level = top + jnp.log2(total)
        for g in range(GROUP):
            index = head * GROUP + g
            part = slice(g * rows, (g + 1) * rows)
            sent[:, index * HD : (index + 1) * HD] = mean[part].astype(BF16)
            stat_value = jnp.where(column == index, level[part], stat_value)
    high, middle, low = pieces(stat_value)
    many = heads * GROUP
    stat[...] = stat_value
    shifted = high + pltpu.roll(middle, many, 1) + pltpu.roll(low, 2 * many, 1)
    sent[:, many * HD :] = shifted.astype(BF16)


def attend(features, step, place, total, got, tables, pools, old):
    rows = total.shape[0]
    heads = pools[4].shape[1]
    operands = [total, *got, *tables, *pools, *old]
    return pl.pallas_call(
        functools.partial(attend_kernel, features, step, len(got)),
        out_shape=[
            jax.ShapeDtypeStruct((rows, heads * GROUP * HD + LANES), BF16),
            jax.ShapeDtypeStruct((rows, LANES), F32),
            jax.ShapeDtypeStruct((rows, 2 * heads * HD), BF16),
        ],
        in_specs=[SMEM_SPEC] + [VMEM_SPEC] * len(operands),
        out_specs=[VMEM_SPEC] * 3,
        compiler_params=PARAMS,
    )(place, *operands)


def merge_kernel(own, stat, *refs):
    got, out = refs[:-1], refs[-1]
    many = out.shape[1] // HD
    levels = [stat[...]]
    for ref in got:
        packed = ref[:, many * HD :].astype(F32)
        levels.append(
            packed
            + pltpu.roll(packed, LANES - many, 1)
            + pltpu.roll(packed, LANES - 2 * many, 1)
        )
    top = functools.reduce(jnp.maximum, levels)
    weights = [jnp.exp2(level - top) for level in levels]
    share = 1.0 / functools.reduce(jnp.add, weights)
    weights = [weight * share for weight in weights]
    for index in range(many):
        part = slice(index * HD, (index + 1) * HD)
        value = own[:, part].astype(F32) * weights[0][:, index : index + 1]
        for ref, weight in zip(got, weights[1:]):
            value = value + ref[:, part].astype(F32) * weight[:, index : index + 1]
        out[:, part] = value.astype(BF16)


def merge(own, stat, got):
    return pl.pallas_call(
        merge_kernel,
        out_shape=jax.ShapeDtypeStruct((own.shape[0], own.shape[1] - LANES), BF16),
        in_specs=[VMEM_SPEC] * (2 + len(got)),
        out_specs=VMEM_SPEC,
        compiler_params=PARAMS,
    )(own, stat, *got)


def output_kernel(place, mine, other, weight, out):
    half = mine.shape[1]
    side = place[0]
    here = pl.ds(pl.multiple_of(side * half, half), half)
    there = pl.ds(pl.multiple_of((1 - side) * half, half), half)
    out[...] = jnp.dot(mine[...], weight[here], preferred_element_type=F32) + jnp.dot(
        other[...], weight[there], preferred_element_type=F32
    )


def output(place, mine, other, weight):
    return pl.pallas_call(
        output_kernel,
        out_shape=jax.ShapeDtypeStruct((mine.shape[0], weight.shape[1]), F32),
        in_specs=[SMEM_SPEC] + [VMEM_SPEC] * 3,
        out_specs=VMEM_SPEC,
        compiler_params=PARAMS,
    )(place, mine, other, weight)


def swapped(array, axis):
    return lax.ppermute(array, axis, [(0, 1), (1, 0)])


def from_others(array, axis):
    size = lax.axis_size(axis)
    return [
        lax.ppermute(array, axis, [(i, (i + hop) % size) for i in range(size)])
        for hop in range(1, size)
    ]


def local_split(
    hidden,
    gain,
    w_query,
    w_key,
    w_value,
    w_out,
    prefix_keys,
    prefix_values,
    suffix_keys,
    suffix_values,
    suffix_lengths,
    page_table,
):
    samples, width = hidden.shape
    features = width * lax.axis_size(("seq", "side"))
    seq = lax.axis_index("seq")
    side = lax.axis_index("side")
    base = seq * (2 * SAMP_DEV)
    first_own = base + (1 - side) * SAMP_DEV
    first_got = base + side * SAMP_DEV
    place = jnp.stack([side, base, first_own, first_got]).astype(jnp.int32)
    own_pools = (prefix_keys, prefix_values, suffix_keys, suffix_values)
    heads = prefix_keys.shape[1] // 2
    got_pools = [
        swapped(lax.dynamic_slice_in_dim(pool, (1 - side) * heads, heads, 1), "side")
        for pool in own_pools
    ]
    pools = [resident(pool) for pool in (*own_pools, *got_pools)]
    weights = [resident(weight) for weight in (w_query, w_key, w_value)]
    out_weight = resident(w_out)
    bias = live_bias(place, suffix_lengths, page_table, suffix_keys.shape[2])
    half = HD // 2
    freq = 500000.0 ** (-(jnp.arange(half, dtype=F32) * 2.0 / HD))
    position = (
        PREFIX + suffix_lengths[None, :] + jnp.arange(STEPS, dtype=jnp.int32)[:, None]
    ).astype(F32)
    angle = position[..., None] * freq
    cosine, sine = jnp.cos(angle), jnp.sin(angle)
    cosine = jnp.concatenate([cosine, cosine], axis=-1)
    sine = jnp.concatenate([-sine, sine], axis=-1)
    gain_row = gain[None, :]

    state = hidden
    update = jnp.zeros(hidden.shape, F32)
    rest = ()
    old = []
    for step in range(STEPS):
        outs = project(place, state, gain_row, weights, rest)
        keep, give = outs[:2]
        if rest:
            state, update = outs[2:]
        total, sent = pair_sum(keep, swapped(give, "side"))
        got = from_others(sent, "seq")
        sent, stat, fresh = attend(
            features, step, place, total, got, (cosine[step], sine[step], bias), pools, old
        )
        old.append(fresh)
        mixed = merge(sent, stat, from_others(sent, "seq"))
        part = output(place, mixed, swapped(mixed, "side"), out_weight)
        rest = (update, part, swapped(part, "head"))
    delta = rest[1] + rest[2]
    return ((state.astype(F32) + delta).astype(BF16), update + delta)


def fits(mesh, args):
    heads = args[4].shape[1] // HD // mesh.shape["head"]
    return (
        mesh.shape["head"] == 2
        and mesh.shape["side"] == 2
        and heads % 2 == 0
        and args[6].shape[0] == mesh.shape["groups"]
        and heads // 2 * GROUP * 3 <= LANES
    )


def solution(mesh):
    placed = (
        P("groups", ("seq", "side")),
        P(("seq", "side")),
        P(("seq", "side"), "head"),
        P(("seq", "side"), "head"),
        P(("seq", "side"), "head"),
        P("head", ("seq", "side")),
        P("groups", "head", ("seq", "side"), None),
        P("groups", "head", ("seq", "side"), None),
        P(("groups", "seq", "side"), "head", None, None),
        P(("groups", "seq", "side"), "head", None, None),
        P("groups"),
        P("groups", None),
    )

    def whole(*args):
        return jax.shard_map(
            local_split if fits(mesh, args) else local_any,
            mesh=mesh,
            in_specs=placed,
            out_specs=(P("groups", ("seq", "side")), P("groups", ("seq", "side"))),
            check_vma=False,
        )(*args)

    return whole
```

```python
import functools
import math

import jax
import jax.numpy as jnp
from jax import lax
from jax.experimental import pallas as pl
from jax.experimental.pallas import tpu as pltpu
from jax.sharding import PartitionSpec as P

D = 8192
HD = 128
GROUP = 8
SAMP_DEV = 2
PREFIX = 32768
STEPS = 3


def combined_all(array, axis, combine):
    everything = jax.tree.map(lambda part: lax.all_gather(part, axis), array)
    first = jax.tree.map(lambda part: part[0], everything)

    def lap(k, so_far):
        return combine(so_far, jax.tree.map(lambda part: part[k], everything))

    return lax.fori_loop(1, lax.axis_size(axis), lap, first)


def rotate(vectors, position):
    half = vectors.shape[-1] // 2
    freq = 500000.0 ** (-(jnp.arange(half, dtype=jnp.float32) * 2.0 / vectors.shape[-1]))
    angle = position[..., None] * freq
    cosine = jnp.cos(angle)
    sine = jnp.sin(angle)
    lower = vectors[..., :half]
    upper = vectors[..., half:]
    return jnp.concatenate([lower * cosine - upper * sine, upper * cosine + lower * sine], axis=-1)


def combine(first, second):
    acc_a, top_a, total_a = first
    acc_b, top_b, total_b = second
    top = jnp.maximum(top_a, top_b)
    weight_a = jnp.exp(top_a - top)
    weight_b = jnp.exp(top_b - top)
    return (
        acc_a * weight_a[..., None] + acc_b * weight_b[..., None],
        top,
        total_a * weight_a + total_b * weight_b,
    )


def local_any(
    hidden,
    gain,
    w_query,
    w_key,
    w_value,
    w_out,
    prefix_keys,
    prefix_values,
    suffix_keys,
    suffix_values,
    suffix_lengths,
    page_table,
):
    samples = hidden.shape[0]
    kv_local = w_key.shape[1] // HD
    query_width = kv_local * GROUP * HD
    key_width = kv_local * HD
    prompts = prefix_keys.shape[0]
    scale = 1.0 / math.sqrt(HD)
    rank = lax.axis_index(("seq", "side"))
    w_proj = jnp.concatenate([w_query, w_key, w_value], axis=1)
    pool_keys, pool_values = (suffix_keys, suffix_values)
    start = jnp.bitwise_xor(rank, 1) * SAMP_DEV
    table_rows = lax.dynamic_slice_in_dim(page_table, start, SAMP_DEV, 0)
    page_keys = pool_keys[table_rows]
    page_values = pool_values[table_rows]
    length_rows = lax.dynamic_slice_in_dim(suffix_lengths, start, SAMP_DEV, 0)
    page_count = page_keys.shape[1]
    page_size = page_keys.shape[3]
    suffix_span = page_count * page_size
    live = (jnp.arange(suffix_span, dtype=jnp.int32)[None, :] < length_rows[:, None])[
        :, None, None, :
    ]
    state = hidden
    update = jnp.zeros(hidden.shape, jnp.float32)
    new_keys = []
    new_values = []
    for step in range(STEPS):
        wide = state.astype(jnp.float32)
        scaled = (wide * gain).astype(jnp.bfloat16)
        partial_value = jnp.dot(scaled, w_proj, preferred_element_type=jnp.float32)
        squares = jnp.sum(wide * wide, axis=1)
        proj, total_sq = lax.psum((partial_value, squares), ("seq", "side"))
        inverse = lax.rsqrt(total_sq / D + 1e-05)[:, None]
        position = (PREFIX + suffix_lengths + step).astype(jnp.float32)
        query = rotate(
            (proj[:, :query_width] * inverse).reshape(samples, kv_local, GROUP, HD),
            position[:, None, None],
        ).astype(jnp.bfloat16)
        new_keys.append(
            rotate(
                (proj[:, query_width : query_width + key_width] * inverse).reshape(
                    samples, kv_local, HD
                ),
                position[:, None],
            ).astype(jnp.bfloat16)
        )
        new_values.append(
            (proj[:, query_width + key_width :] * inverse)
            .reshape(samples, kv_local, HD)
            .astype(jnp.bfloat16)
        )
        stacked_keys = jnp.stack(new_keys, axis=1)
        stacked_values = jnp.stack(new_values, axis=1)
        grouped = query.reshape(prompts, samples // prompts, kv_local, GROUP, HD)
        scores = (
            jnp.einsum(
                "pgkhd,pkld->pgkhl", grouped, prefix_keys, preferred_element_type=jnp.float32
            )
            * scale
        )
        top = jnp.max(scores, axis=-1)
        expo = jnp.exp(scores - top[..., None])
        total = jnp.sum(expo, axis=-1)
        acc = jnp.einsum(
            "pgkhl,pkld->pgkhd",
            expo.astype(jnp.bfloat16),
            prefix_values,
            preferred_element_type=jnp.float32,
        )
        acc = acc.reshape(samples, kv_local, GROUP, HD)
        top = top.reshape(samples, kv_local, GROUP)
        total = total.reshape(samples, kv_local, GROUP)
        own_query = lax.dynamic_slice_in_dim(query, start, SAMP_DEV, 0)
        own_keys = lax.dynamic_slice_in_dim(stacked_keys, start, SAMP_DEV, 0)
        own_values = lax.dynamic_slice_in_dim(stacked_values, start, SAMP_DEV, 0)
        suffix_scores = jnp.einsum(
            "skhd,spkjd->skhpj", own_query, page_keys, preferred_element_type=jnp.float32
        )
        suffix_scores = suffix_scores.reshape(SAMP_DEV, kv_local, GROUP, suffix_span) * scale
        suffix_scores = jnp.where(live, suffix_scores, -jnp.inf)
        fresh_scores = (
            jnp.einsum("skhd,sukd->skhu", own_query, own_keys, preferred_element_type=jnp.float32)
            * scale
        )
        peak = jnp.maximum(jnp.max(suffix_scores, axis=-1), jnp.max(fresh_scores, axis=-1))
        suffix_expo = jnp.exp(suffix_scores - peak[..., None])
        fresh_expo = jnp.exp(fresh_scores - peak[..., None])
        near_total = jnp.sum(suffix_expo, axis=-1) + jnp.sum(fresh_expo, axis=-1)
        near_acc = jnp.einsum(
            "skhpj,spkjd->skhd",
            suffix_expo.astype(jnp.bfloat16).reshape(
                SAMP_DEV, kv_local, GROUP, page_count, page_size
            ),
            page_values,
            preferred_element_type=jnp.float32,
        )
        near_acc = near_acc + jnp.einsum(
            "skhu,sukd->skhd",
            fresh_expo.astype(jnp.bfloat16),
            own_values,
            preferred_element_type=jnp.float32,
        )
        rows_now = (
            lax.dynamic_slice_in_dim(acc, start, SAMP_DEV, 0),
            lax.dynamic_slice_in_dim(top, start, SAMP_DEV, 0),
            lax.dynamic_slice_in_dim(total, start, SAMP_DEV, 0),
        )
        joined = combine(rows_now, (near_acc, peak, near_total))
        acc = lax.dynamic_update_slice_in_dim(acc, joined[0], start, 0)
        top = lax.dynamic_update_slice_in_dim(top, joined[1], start, 0)
        total = lax.dynamic_update_slice_in_dim(total, joined[2], start, 0)
        acc, top, total = combined_all((acc, top, total), ("seq", "side"), combine)
        mixed = (acc / total[..., None]).astype(jnp.bfloat16).reshape(samples, query_width)
        part = jnp.dot(mixed, w_out, preferred_element_type=jnp.float32)
        delta = lax.psum(part, "head")
        update = update + delta
        state = (wide + delta).astype(jnp.bfloat16)
    return (state, update)


LANES = 128
LOG2E = 1.4426950408889634
BF16 = jnp.bfloat16
F32 = jnp.float32
VMEM_SPEC = pl.BlockSpec(memory_space=pltpu.VMEM)
SMEM_SPEC = pl.BlockSpec(memory_space=pltpu.SMEM)
HBM_SPEC = pl.BlockSpec(memory_space=pltpu.HBM)
PARAMS = pltpu.CompilerParams(vmem_limit_bytes=13 * 1024 * 1024)


def resident(array):
    return pltpu.with_memory_space_constraint(array, pltpu.VMEM)


def in_hbm(array):
    return pltpu.with_memory_space_constraint(array, pltpu.HBM)


def lanes(rows):
    return lax.broadcasted_iota(jnp.int32, (rows, LANES), 1)


def pieces(values):
    high = values.astype(BF16).astype(F32)
    middle = (values - high).astype(BF16).astype(F32)
    return high, middle, values - high - middle


def move(copies):
    for copy in copies:
        copy.start()
    for copy in copies:
        copy.wait()


def split_kernel(place, pk, pv, sk, sv, prefix, suffix, sems):
    heads = prefix.shape[1]
    away = pl.ds((1 - place[0]) * heads, heads)
    move(
        [
            pltpu.make_async_copy(pk.at[0, away], prefix.at[0], sems.at[0]),
            pltpu.make_async_copy(pv.at[0, away], prefix.at[1], sems.at[1]),
            pltpu.make_async_copy(sk.at[:, away], suffix.at[0], sems.at[2]),
            pltpu.make_async_copy(sv.at[:, away], suffix.at[1], sems.at[3]),
        ]
    )


def split_heads(place, pools):
    pk, sk = pools[0], pools[2]
    return pl.pallas_call(
        split_kernel,
        out_shape=[
            pltpu.VMEM((2, pk.shape[1] // 2) + pk.shape[2:], pk.dtype),
            pltpu.VMEM((2, sk.shape[0], sk.shape[1] // 2) + sk.shape[2:], sk.dtype),
        ],
        in_specs=[SMEM_SPEC] + [HBM_SPEC] * 4,
        out_specs=[VMEM_SPEC] * 2,
        scratch_shapes=[pltpu.SemaphoreType.DMA((4,))],
        compiler_params=PARAMS,
    )(place, *pools)


def bias_kernel(place, lengths, table, bias):
    pages = table.shape[1]
    page = bias.shape[2] // (SAMP_DEV * pages)
    row = lax.broadcasted_iota(jnp.int32, (bias.shape[1], page), 0)
    column = lax.broadcasted_iota(jnp.int32, (bias.shape[1], page), 1)
    for pool in range(2):
        for j in range(SAMP_DEV):
            sample = place[2 + pool] + j
            mine = row % SAMP_DEV == j
            for p in range(pages):
                live = mine & (column < lengths[sample] - p * page)
                spot = pl.ds(pl.multiple_of(table[sample, p] * page, page), page)
                bias[pool, :, spot] = jnp.where(live, 0.0, -jnp.inf)


def live_bias(place, lengths, table, page):
    tokens = SAMP_DEV * table.shape[1] * page
    return pl.pallas_call(
        bias_kernel,
        out_shape=jax.ShapeDtypeStruct((2, SAMP_DEV * GROUP, tokens), F32),
        in_specs=[SMEM_SPEC] * 3,
        out_specs=VMEM_SPEC,
        compiler_params=PARAMS,
    )(place, lengths, table)


def project_kernel(first, place, *refs):
    if first:
        x_ref, gain, w_query, w_key, w_value, keep, give = refs
        wide = x_ref[...].astype(F32)
    else:
        x_ref, gain, w_query, w_key, w_value, sum_ref, mine, other = refs[:8]
        keep, give, new_x, new_sum = refs[8:]
        delta = mine[...] + other[...]
        new_sum[...] = sum_ref[...] + delta
        state = (x_ref[...].astype(F32) + delta).astype(BF16)
        new_x[...] = state
        wide = state.astype(F32)
    scaled = (wide * gain[...]).astype(BF16)
    squares = jnp.sum(wide * wide, axis=1, keepdims=True)
    column = lanes(wide.shape[0])
    query = w_query.shape[1] // 2
    key = w_key.shape[1] // 2
    side = place[0]
    for out, who in ((give, 1 - side), (keep, side)):
        tile = min(1024, query)
        for at in range(0, query, tile):
            columns = pl.ds(pl.multiple_of(who * query + at, tile), tile)
            out[:, at : at + tile] = jnp.dot(
                scaled, w_query[:, columns], preferred_element_type=F32
            )
        columns = pl.ds(pl.multiple_of(who * key, key), key)
        out[:, query : query + key] = jnp.dot(
            scaled, w_key[:, columns], preferred_element_type=F32
        )
        out[:, query + key : query + 2 * key] = jnp.dot(
            scaled, w_value[:, columns], preferred_element_type=F32
        )
        out[:, query + 2 * key :] = jnp.where(column == 0, squares, 0.0)


def project(place, x, gain, weights, rest):
    rows = x.shape[0]
    width = sum(w.shape[1] for w in weights) // 2 + LANES
    halves = [jax.ShapeDtypeStruct((rows, width), F32)] * 2
    out_shape = halves if not rest else halves + [
        jax.ShapeDtypeStruct(x.shape, BF16),
        jax.ShapeDtypeStruct(x.shape, F32),
    ]
    return pl.pallas_call(
        functools.partial(project_kernel, not rest),
        out_shape=out_shape,
        in_specs=[SMEM_SPEC] + [VMEM_SPEC] * (5 + len(rest)),
        out_specs=[VMEM_SPEC] * len(out_shape),
        compiler_params=PARAMS,
    )(place, x, gain, *weights, *rest)


def pair_sum_kernel(keep, got, total, sent):
    both = keep[...] + got[...]
    total[...] = both
    main = both.shape[1] - LANES
    sent[:, :main] = both[:, :main].astype(BF16)
    column = lanes(both.shape[0])
    high, middle, low = pieces(both[:, main : main + 1])
    sent[:, main:] = jnp.where(
        column == 0, high, jnp.where(column == 1, middle, jnp.where(column == 2, low, 0.0))
    ).astype(BF16)


def pair_sum(keep, got):
    return pl.pallas_call(
        pair_sum_kernel,
        out_shape=[
            jax.ShapeDtypeStruct(keep.shape, F32),
            jax.ShapeDtypeStruct(keep.shape, BF16),
        ],
        in_specs=[VMEM_SPEC] * 2,
        out_specs=[VMEM_SPEC] * 2,
        compiler_params=PARAMS,
    )(keep, got)


def lane_fold(fold, array):
    parts = [array[:, at : at + LANES] for at in range(0, array.shape[1], LANES)]
    return functools.reduce(fold, parts)


def row_max(arrays):
    folded = [lane_fold(jnp.maximum, array) for array in arrays]
    return jnp.max(functools.reduce(jnp.maximum, folded), axis=1, keepdims=True)


def against(rows, keys):
    return lax.dot_general(
        rows, keys, (((1,), (1,)), ((), ())), preferred_element_type=F32
    )


def weigh(scores, top, values, scale):
    total, acc = None, None
    for score, value in zip(scores, values):
        expo = jnp.exp2((score - top) * scale)
        part = lane_fold(jnp.add, expo)
        term = jnp.dot(expo.astype(BF16), value, preferred_element_type=F32)
        total = part if total is None else total + part
        acc = term if acc is None else acc + term
    return jnp.sum(total, axis=1, keepdims=True), acc


def attend_kernel(features, step, others, place, *refs):
    total_ref = refs[0]
    got = refs[1 : 1 + others]
    cos_ref, sin_ref, bias_ref = refs[1 + others : 4 + others]
    if step == 0:
        pk, pv, sk, sv, got_prefix, got_suffix = refs[4 + others : 10 + others]
        sent, stat, fresh, prefix, suffix, sems = refs[10 + others :]
        old = ()
        heads = got_prefix.shape[1]
        own = pl.ds(place[0] * heads, heads)
        waits = [
            pltpu.make_async_copy(got_suffix.at[0], suffix.at[0, 1], sems.at[0]),
            pltpu.make_async_copy(sk.at[:, own], suffix.at[0, 0], sems.at[1]),
            pltpu.make_async_copy(got_prefix.at[0], prefix.at[0, 1], sems.at[2]),
            pltpu.make_async_copy(pk.at[0, own], prefix.at[0, 0], sems.at[3]),
            pltpu.make_async_copy(got_suffix.at[1], suffix.at[1, 1], sems.at[4]),
            pltpu.make_async_copy(sv.at[:, own], suffix.at[1, 0], sems.at[5]),
            pltpu.make_async_copy(got_prefix.at[1], prefix.at[1, 1], sems.at[6]),
            pltpu.make_async_copy(pv.at[0, own], prefix.at[1, 0], sems.at[7]),
        ]
        for copy in waits:
            copy.start()
    else:
        prefix, suffix = refs[4 + others : 6 + others]
        old = refs[6 + others : 6 + others + step]
        sent, stat, fresh = refs[6 + others + step :]
        waits = []
    rows = total_ref.shape[0]
    heads = prefix.shape[2]
    width = total_ref.shape[1] - LANES
    query_width = width - 2 * heads * HD
    base, starts = place[1], (place[2], place[3])
    scale = LOG2E / math.sqrt(HD)

    stats = total_ref[:, width : width + 1]
    for ref in got:
        stats = stats + jnp.sum(ref[:, width:].astype(F32), axis=1, keepdims=True)
    inverse = lax.rsqrt(stats / features + 1e-05)
    cosine = cos_ref[...]
    sine = sin_ref[...]

    def block(at):
        value = total_ref[:, at : at + HD]
        for ref in got:
            value = value + ref[:, at : at + HD].astype(F32)
        return value * inverse

    def turned(at):
        value = block(at)
        return (value * cosine + pltpu.roll(value, HD // 2, 1) * sine).astype(BF16)

    sample = lax.broadcasted_iota(jnp.int32, (rows, 1), 0)
    owned = (sample >= base) & (sample < base + 2 * SAMP_DEV)
    few_rows = SAMP_DEV * GROUP
    pick_row = lax.broadcasted_iota(jnp.int32, (few_rows, GROUP * rows), 0)
    pick_column = lax.broadcasted_iota(jnp.int32, (few_rows, GROUP * rows), 1)
    spot = (pick_row // SAMP_DEV) * rows + pick_row % SAMP_DEV
    picks = [(pick_column == spot + start).astype(F32).astype(BF16) for start in starts]
    column = lanes(rows)

    queries = [
        [turned((head * GROUP + g) * HD) for g in range(GROUP)] for head in range(heads)
    ]
    packed = [jnp.concatenate(query, axis=0) for query in queries]
    keys, values = [], []
    for head in range(heads):
        new_key = turned(query_width + head * HD)
        new_value = block(query_width + (heads + head) * HD).astype(BF16)
        key_part = slice(head * HD, (head + 1) * HD)
        value_part = slice((heads + head) * HD, (heads + head + 1) * HD)
        fresh[:, key_part] = new_key
        fresh[:, value_part] = new_value
        keys.append([ref[:, key_part].astype(F32) for ref in old] + [new_key.astype(F32)])
        values.append([ref[:, value_part].astype(F32) for ref in old] + [new_value.astype(F32)])
    few = [
        [jnp.dot(pick, packed[head], preferred_element_type=F32).astype(BF16) for pick in picks]
        for head in range(heads)
    ]
    fresh_scores = [
        [
            [
                jnp.sum(query.astype(F32) * key, axis=1, keepdims=True)
                for key in keys[head]
            ]
            for query in queries[head]
        ]
        for head in range(heads)
    ]

    slots, page = suffix.shape[2], suffix.shape[4]
    length = prefix.shape[3]
    chunk = min(2048, length)
    pieces_of = [(src, at) for src in range(2) for at in range(0, length, chunk)]

    def pool(kind, src, head):
        return suffix[kind, src, :, head].reshape(slots * page, HD)

    for copy in waits[:4]:
        copy.wait()
    near_scores = [
        [against(few[head][src], pool(0, src, head)) + bias_ref[src] for src in range(2)]
        for head in range(heads)
    ]
    far_scores = [
        [
            against(packed[head], prefix[0, src, head, at : at + chunk])
            for src, at in pieces_of
        ]
        for head in range(heads)
    ]
    near_tops = [[row_max([score]) for score in scores] for scores in near_scores]
    far_tops = [row_max(scores) for scores in far_scores]
    for copy in waits[4:]:
        copy.wait()
    near = [
        [
            weigh([near_scores[head][src]], near_tops[head][src], [pool(1, src, head)], scale)
            for src in range(2)
        ]
        for head in range(heads)
    ]

    stat_value = jnp.zeros((rows, LANES), F32)
    for head in range(heads):
        far_total, far_acc = weigh(
            far_scores[head],
            far_tops[head],
            [prefix[1, src, head, at : at + chunk] for src, at in pieces_of],
            scale,
        )
        for g in range(GROUP):
            part = slice(g * rows, (g + 1) * rows)
            far_top = far_tops[head][part]
            near_top = jnp.full((rows, 1), -1e30, F32)
            total = jnp.zeros((rows, 1), F32)
            acc = jnp.zeros((rows, HD), F32)
            for src in range(2):
                for j in range(SAMP_DEV):
                    line = slice(g * SAMP_DEV + j, g * SAMP_DEV + j + 1)
                    here = sample == starts[src] + j
                    near_top = jnp.where(here, near_tops[head][src][line], near_top)
                    total = jnp.where(here, near[head][src][0][line], total)
                    acc = jnp.where(here, near[head][src][1][line], acc)
            top = jnp.maximum(far_top, near_top)
            scores = fresh_scores[head][g]
            for score in scores:
                top = jnp.where(owned, jnp.maximum(top, score), top)
            far_weight = jnp.exp2((far_top - top) * scale)
            near_weight = jnp.exp2((near_top - top) * scale)
            total = total * near_weight + far_total[part] * far_weight
            acc = acc * near_weight + far_acc[part] * far_weight
            for score, value in zip(scores, values[head]):
                expo = jnp.where(owned, jnp.exp2(jnp.where(owned, score - top, 0.0) * scale), 0.0)
                total = total + expo
                acc = acc + expo.astype(BF16).astype(F32) * value
            index = head * GROUP + g
            sent[:, index * HD : (index + 1) * HD] = (acc / total).astype(BF16)
            level = top * scale + jnp.log2(total)
            stat_value = jnp.where(column == index, level, stat_value)
    high, middle, low = pieces(stat_value)
    many = heads * GROUP
    stat[...] = stat_value
    shifted = high + pltpu.roll(middle, many, 1) + pltpu.roll(low, 2 * many, 1)
    sent[:, many * HD :] = shifted.astype(BF16)


def attend(features, step, place, total, got, tables, caches, old):
    rows = total.shape[0]
    out_shape, scratch = [], []
    if step == 0:
        pools, (got_prefix, got_suffix) = caches
        heads = got_prefix.shape[1]
        out_shape = [
            pltpu.VMEM((2, 2) + part.shape[1:], BF16) for part in (got_prefix, got_suffix)
        ]
        scratch = [pltpu.SemaphoreType.DMA((8,))]
        inputs = [in_hbm(array) for array in (*pools, got_prefix, got_suffix)]
        specs = [HBM_SPEC] * len(inputs)
    else:
        heads = caches[0].shape[2]
        inputs = [resident(array) for array in caches]
        specs = [VMEM_SPEC] * len(inputs)
    small = [total, *got, *tables]
    return pl.pallas_call(
        functools.partial(attend_kernel, features, step, len(got)),
        out_shape=[
            jax.ShapeDtypeStruct((rows, heads * GROUP * HD + LANES), BF16),
            jax.ShapeDtypeStruct((rows, LANES), F32),
            jax.ShapeDtypeStruct((rows, 2 * heads * HD), BF16),
            *out_shape,
        ],
        in_specs=[SMEM_SPEC] + [VMEM_SPEC] * len(small) + specs + [VMEM_SPEC] * len(old),
        out_specs=[VMEM_SPEC] * (3 + len(out_shape)),
        scratch_shapes=scratch,
        compiler_params=PARAMS,
    )(place, *small, *inputs, *old)


def merge_kernel(own, stat, *refs):
    got, out = refs[:-1], refs[-1]
    many = out.shape[1] // HD
    levels = [stat[...]]
    for ref in got:
        packed = ref[:, many * HD :].astype(F32)
        levels.append(
            packed
            + pltpu.roll(packed, LANES - many, 1)
            + pltpu.roll(packed, LANES - 2 * many, 1)
        )
    top = functools.reduce(jnp.maximum, levels)
    weights = [jnp.exp2(level - top) for level in levels]
    share = 1.0 / functools.reduce(jnp.add, weights)
    weights = [weight * share for weight in weights]
    for index in range(many):
        part = slice(index * HD, (index + 1) * HD)
        value = own[:, part].astype(F32) * weights[0][:, index : index + 1]
        for ref, weight in zip(got, weights[1:]):
            value = value + ref[:, part].astype(F32) * weight[:, index : index + 1]
        out[:, part] = value.astype(BF16)


def merge(own, stat, got):
    return pl.pallas_call(
        merge_kernel,
        out_shape=jax.ShapeDtypeStruct((own.shape[0], own.shape[1] - LANES), BF16),
        in_specs=[VMEM_SPEC] * (2 + len(got)),
        out_specs=VMEM_SPEC,
        compiler_params=PARAMS,
    )(own, stat, *got)


def output_kernel(place, mine, other, weight, out):
    half = mine.shape[1]
    side = place[0]
    here = pl.ds(pl.multiple_of(side * half, half), half)
    there = pl.ds(pl.multiple_of((1 - side) * half, half), half)
    out[...] = jnp.dot(mine[...], weight[here], preferred_element_type=F32) + jnp.dot(
        other[...], weight[there], preferred_element_type=F32
    )


def output(place, mine, other, weight):
    return pl.pallas_call(
        output_kernel,
        out_shape=jax.ShapeDtypeStruct((mine.shape[0], weight.shape[1]), F32),
        in_specs=[SMEM_SPEC] + [VMEM_SPEC] * 3,
        out_specs=VMEM_SPEC,
        compiler_params=PARAMS,
    )(place, mine, other, weight)


def swapped(array, axis):
    return lax.ppermute(array, axis, [(0, 1), (1, 0)])


def from_others(array, axis):
    size = lax.axis_size(axis)
    return [
        lax.ppermute(array, axis, [(i, (i + hop) % size) for i in range(size)])
        for hop in range(1, size)
    ]


def local_split(
    hidden,
    gain,
    w_query,
    w_key,
    w_value,
    w_out,
    prefix_keys,
    prefix_values,
    suffix_keys,
    suffix_values,
    suffix_lengths,
    page_table,
):
    samples, width = hidden.shape
    features = width * lax.axis_size(("seq", "side"))
    seq = lax.axis_index("seq")
    side = lax.axis_index("side")
    base = seq * (2 * SAMP_DEV)
    first_own = base + (1 - side) * SAMP_DEV
    first_got = base + side * SAMP_DEV
    place = jnp.stack([side, base, first_own, first_got]).astype(jnp.int32)
    pools = (prefix_keys, prefix_values, suffix_keys, suffix_values)
    given = split_heads(place, [in_hbm(pool) for pool in pools])
    caches = (pools, [swapped(part, "side") for part in given])
    weights = [resident(weight) for weight in (w_query, w_key, w_value)]
    out_weight = resident(w_out)
    bias = live_bias(place, suffix_lengths, page_table, suffix_keys.shape[2])
    half = HD // 2
    freq = 500000.0 ** (-(jnp.arange(half, dtype=F32) * 2.0 / HD))
    position = (
        PREFIX + suffix_lengths[None, :] + jnp.arange(STEPS, dtype=jnp.int32)[:, None]
    ).astype(F32)
    angle = position[..., None] * freq
    cosine, sine = jnp.cos(angle), jnp.sin(angle)
    cosine = jnp.concatenate([cosine, cosine], axis=-1)
    sine = jnp.concatenate([-sine, sine], axis=-1)
    gain_row = gain[None, :]

    state = hidden
    update = jnp.zeros(hidden.shape, F32)
    rest = ()
    old = []
    for step in range(STEPS):
        outs = project(place, state, gain_row, weights, rest)
        keep, give = outs[:2]
        if rest:
            state, update = outs[2:]
        total, sent = pair_sum(keep, swapped(give, "side"))
        got = from_others(sent, "seq")
        sent, stat, fresh, *kept = attend(
            features, step, place, total, got, (cosine[step], sine[step], bias), caches, old
        )
        caches = kept or caches
        old.append(fresh)
        mixed = merge(sent, stat, from_others(sent, "seq"))
        part = output(place, mixed, swapped(mixed, "side"), out_weight)
        rest = (update, part, swapped(part, "head"))
    delta = rest[1] + rest[2]
    return ((state.astype(F32) + delta).astype(BF16), update + delta)


def fits(mesh, args):
    heads = args[4].shape[1] // HD // mesh.shape["head"]
    return (
        mesh.shape["head"] == 2
        and mesh.shape["side"] == 2
        and heads % 2 == 0
        and args[6].shape[0] == mesh.shape["groups"]
        and heads // 2 * GROUP * 3 <= LANES
    )


def solution(mesh):
    placed = (
        P("groups", ("seq", "side")),
        P(("seq", "side")),
        P(("seq", "side"), "head"),
        P(("seq", "side"), "head"),
        P(("seq", "side"), "head"),
        P("head", ("seq", "side")),
        P("groups", "head", ("seq", "side"), None),
        P("groups", "head", ("seq", "side"), None),
        P(("groups", "seq", "side"), "head", None, None),
        P(("groups", "seq", "side"), "head", None, None),
        P("groups"),
        P("groups", None),
    )

    def whole(*args):
        return jax.shard_map(
            local_split if fits(mesh, args) else local_any,
            mesh=mesh,
            in_specs=placed,
            out_specs=(P("groups", ("seq", "side")), P("groups", ("seq", "side"))),
            check_vma=False,
        )(*args)

    return whole
```

```python
import functools
import math

import jax
import jax.numpy as jnp
from jax import lax
from jax.experimental import pallas as pl
from jax.experimental.pallas import tpu as pltpu
from jax.sharding import PartitionSpec as P

D = 8192
HD = 128
GROUP = 8
SAMP_DEV = 2
PREFIX = 32768
STEPS = 3


def combined_all(array, axis, combine):
    everything = jax.tree.map(lambda part: lax.all_gather(part, axis), array)
    first = jax.tree.map(lambda part: part[0], everything)

    def lap(k, so_far):
        return combine(so_far, jax.tree.map(lambda part: part[k], everything))

    return lax.fori_loop(1, lax.axis_size(axis), lap, first)


def rotate(vectors, position):
    half = vectors.shape[-1] // 2
    freq = 500000.0 ** (-(jnp.arange(half, dtype=jnp.float32) * 2.0 / vectors.shape[-1]))
    angle = position[..., None] * freq
    cosine = jnp.cos(angle)
    sine = jnp.sin(angle)
    lower = vectors[..., :half]
    upper = vectors[..., half:]
    return jnp.concatenate([lower * cosine - upper * sine, upper * cosine + lower * sine], axis=-1)


def combine(first, second):
    acc_a, top_a, total_a = first
    acc_b, top_b, total_b = second
    top = jnp.maximum(top_a, top_b)
    weight_a = jnp.exp(top_a - top)
    weight_b = jnp.exp(top_b - top)
    return (
        acc_a * weight_a[..., None] + acc_b * weight_b[..., None],
        top,
        total_a * weight_a + total_b * weight_b,
    )


def local_any(
    hidden,
    gain,
    w_query,
    w_key,
    w_value,
    w_out,
    prefix_keys,
    prefix_values,
    suffix_keys,
    suffix_values,
    suffix_lengths,
    page_table,
):
    samples = hidden.shape[0]
    kv_local = w_key.shape[1] // HD
    query_width = kv_local * GROUP * HD
    key_width = kv_local * HD
    prompts = prefix_keys.shape[0]
    scale = 1.0 / math.sqrt(HD)
    rank = lax.axis_index(("seq", "side"))
    w_proj = jnp.concatenate([w_query, w_key, w_value], axis=1)
    pool_keys, pool_values = (suffix_keys, suffix_values)
    start = jnp.bitwise_xor(rank, 1) * SAMP_DEV
    table_rows = lax.dynamic_slice_in_dim(page_table, start, SAMP_DEV, 0)
    page_keys = pool_keys[table_rows]
    page_values = pool_values[table_rows]
    length_rows = lax.dynamic_slice_in_dim(suffix_lengths, start, SAMP_DEV, 0)
    page_count = page_keys.shape[1]
    page_size = page_keys.shape[3]
    suffix_span = page_count * page_size
    live = (jnp.arange(suffix_span, dtype=jnp.int32)[None, :] < length_rows[:, None])[
        :, None, None, :
    ]
    state = hidden
    update = jnp.zeros(hidden.shape, jnp.float32)
    new_keys = []
    new_values = []
    for step in range(STEPS):
        wide = state.astype(jnp.float32)
        scaled = (wide * gain).astype(jnp.bfloat16)
        partial_value = jnp.dot(scaled, w_proj, preferred_element_type=jnp.float32)
        squares = jnp.sum(wide * wide, axis=1)
        proj, total_sq = lax.psum((partial_value, squares), ("seq", "side"))
        inverse = lax.rsqrt(total_sq / D + 1e-05)[:, None]
        position = (PREFIX + suffix_lengths + step).astype(jnp.float32)
        query = rotate(
            (proj[:, :query_width] * inverse).reshape(samples, kv_local, GROUP, HD),
            position[:, None, None],
        ).astype(jnp.bfloat16)
        new_keys.append(
            rotate(
                (proj[:, query_width : query_width + key_width] * inverse).reshape(
                    samples, kv_local, HD
                ),
                position[:, None],
            ).astype(jnp.bfloat16)
        )
        new_values.append(
            (proj[:, query_width + key_width :] * inverse)
            .reshape(samples, kv_local, HD)
            .astype(jnp.bfloat16)
        )
        stacked_keys = jnp.stack(new_keys, axis=1)
        stacked_values = jnp.stack(new_values, axis=1)
        grouped = query.reshape(prompts, samples // prompts, kv_local, GROUP, HD)
        scores = (
            jnp.einsum(
                "pgkhd,pkld->pgkhl", grouped, prefix_keys, preferred_element_type=jnp.float32
            )
            * scale
        )
        top = jnp.max(scores, axis=-1)
        expo = jnp.exp(scores - top[..., None])
        total = jnp.sum(expo, axis=-1)
        acc = jnp.einsum(
            "pgkhl,pkld->pgkhd",
            expo.astype(jnp.bfloat16),
            prefix_values,
            preferred_element_type=jnp.float32,
        )
        acc = acc.reshape(samples, kv_local, GROUP, HD)
        top = top.reshape(samples, kv_local, GROUP)
        total = total.reshape(samples, kv_local, GROUP)
        own_query = lax.dynamic_slice_in_dim(query, start, SAMP_DEV, 0)
        own_keys = lax.dynamic_slice_in_dim(stacked_keys, start, SAMP_DEV, 0)
        own_values = lax.dynamic_slice_in_dim(stacked_values, start, SAMP_DEV, 0)
        suffix_scores = jnp.einsum(
            "skhd,spkjd->skhpj", own_query, page_keys, preferred_element_type=jnp.float32
        )
        suffix_scores = suffix_scores.reshape(SAMP_DEV, kv_local, GROUP, suffix_span) * scale
        suffix_scores = jnp.where(live, suffix_scores, -jnp.inf)
        fresh_scores = (
            jnp.einsum("skhd,sukd->skhu", own_query, own_keys, preferred_element_type=jnp.float32)
            * scale
        )
        peak = jnp.maximum(jnp.max(suffix_scores, axis=-1), jnp.max(fresh_scores, axis=-1))
        suffix_expo = jnp.exp(suffix_scores - peak[..., None])
        fresh_expo = jnp.exp(fresh_scores - peak[..., None])
        near_total = jnp.sum(suffix_expo, axis=-1) + jnp.sum(fresh_expo, axis=-1)
        near_acc = jnp.einsum(
            "skhpj,spkjd->skhd",
            suffix_expo.astype(jnp.bfloat16).reshape(
                SAMP_DEV, kv_local, GROUP, page_count, page_size
            ),
            page_values,
            preferred_element_type=jnp.float32,
        )
        near_acc = near_acc + jnp.einsum(
            "skhu,sukd->skhd",
            fresh_expo.astype(jnp.bfloat16),
            own_values,
            preferred_element_type=jnp.float32,
        )
        rows_now = (
            lax.dynamic_slice_in_dim(acc, start, SAMP_DEV, 0),
            lax.dynamic_slice_in_dim(top, start, SAMP_DEV, 0),
            lax.dynamic_slice_in_dim(total, start, SAMP_DEV, 0),
        )
        joined = combine(rows_now, (near_acc, peak, near_total))
        acc = lax.dynamic_update_slice_in_dim(acc, joined[0], start, 0)
        top = lax.dynamic_update_slice_in_dim(top, joined[1], start, 0)
        total = lax.dynamic_update_slice_in_dim(total, joined[2], start, 0)
        acc, top, total = combined_all((acc, top, total), ("seq", "side"), combine)
        mixed = (acc / total[..., None]).astype(jnp.bfloat16).reshape(samples, query_width)
        part = jnp.dot(mixed, w_out, preferred_element_type=jnp.float32)
        delta = lax.psum(part, "head")
        update = update + delta
        state = (wide + delta).astype(jnp.bfloat16)
    return (state, update)


LANES = 128
LOG2E = 1.4426950408889634
BF16 = jnp.bfloat16
F32 = jnp.float32
VMEM_SPEC = pl.BlockSpec(memory_space=pltpu.VMEM)
SMEM_SPEC = pl.BlockSpec(memory_space=pltpu.SMEM)
HBM_SPEC = pl.BlockSpec(memory_space=pltpu.HBM)
PARAMS = pltpu.CompilerParams(vmem_limit_bytes=4 * 1024 * 1024)
LARGE_PARAMS = pltpu.CompilerParams(vmem_limit_bytes=13 * 1024 * 1024)


def resident(array):
    return pltpu.with_memory_space_constraint(array, pltpu.VMEM)


def in_hbm(array):
    return pltpu.with_memory_space_constraint(array, pltpu.HBM)


def lanes(rows):
    return lax.broadcasted_iota(jnp.int32, (rows, LANES), 1)


def pieces(values):
    high = values.astype(BF16).astype(F32)
    middle = (values - high).astype(BF16).astype(F32)
    return high, middle, values - high - middle


def move(copies):
    for copy in copies:
        copy.start()
    for copy in copies:
        copy.wait()


def copied(pairs, sems):
    copies = [
        pltpu.make_async_copy(source, target, sems.at[n])
        for n, (source, target) in enumerate(pairs)
    ]
    for copy in copies:
        copy.start()
    return copies


def halves(place, pools, prefix, suffix):
    heads = prefix.shape[1]
    part = pl.ds(place[0] * heads, heads)
    pk, pv, sk, sv = pools
    return [
        (sk.at[:, part], suffix.at[0]),
        (pk.at[0, part], prefix.at[0]),
        (sv.at[:, part], suffix.at[1]),
        (pv.at[0, part], prefix.at[1]),
    ]


def half_shapes(pools):
    pk, sk = pools[0], pools[2]
    return [
        pltpu.VMEM((2, pk.shape[1] // 2) + pk.shape[2:], pk.dtype),
        pltpu.VMEM((2, sk.shape[0], sk.shape[1] // 2) + sk.shape[2:], sk.dtype),
    ]


def load_kernel(pools, place, *refs):
    count = (len(refs) - 2 + 2 * (pools > 0)) // 2
    sources, outs, sems = refs[:count], refs[count + 1 : -1], refs[-1]
    pairs = list(zip(sources[pools:], outs[2 * (pools > 0) :]))
    if pools:
        pairs = halves(place, sources[:pools], *outs[:2]) + pairs
    for copy in copied(pairs, sems):
        copy.wait()


def load(place, pools, weights, after):
    sources = [in_hbm(array) for array in (*pools, *weights)]
    shapes = half_shapes(pools) if pools else []
    shapes = shapes + [pltpu.VMEM(w.shape, w.dtype) for w in weights]
    return pl.pallas_call(
        functools.partial(load_kernel, len(pools)),
        out_shape=shapes,
        in_specs=[SMEM_SPEC] + [HBM_SPEC] * len(sources) + [VMEM_SPEC],
        out_specs=[VMEM_SPEC] * len(shapes),
        scratch_shapes=[pltpu.SemaphoreType.DMA((len(sources),))],
        compiler_params=PARAMS,
        cost_estimate=pl.CostEstimate(flops=0, bytes_accessed=1 << 25, transcendentals=0),
    )(place, *sources, after)


def bias_kernel(place, lengths, table, bias):
    pages = table.shape[1]
    page = bias.shape[2] // (SAMP_DEV * pages)
    row = lax.broadcasted_iota(jnp.int32, (bias.shape[1], page), 0)
    column = lax.broadcasted_iota(jnp.int32, (bias.shape[1], page), 1)
    for pool in range(2):
        for j in range(SAMP_DEV):
            sample = place[2 + pool] + j
            mine = row % SAMP_DEV == j
            for p in range(pages):
                live = mine & (column < lengths[sample] - p * page)
                spot = pl.ds(pl.multiple_of(table[sample, p] * page, page), page)
                bias[pool, :, spot] = jnp.where(live, 0.0, -jnp.inf)


def live_bias(place, lengths, table, page):
    tokens = SAMP_DEV * table.shape[1] * page
    return pl.pallas_call(
        bias_kernel,
        out_shape=jax.ShapeDtypeStruct((2, SAMP_DEV * GROUP, tokens), F32),
        in_specs=[SMEM_SPEC] * 3,
        out_specs=VMEM_SPEC,
        compiler_params=PARAMS,
    )(place, lengths, table)


def project_kernel(first, place, *refs):
    x_ref, gain, *weights = refs[:5]
    if first:
        keep, give, *buffers, sems = refs[5:]
    else:
        sum_ref, mine, other, keep, give, new_x, new_sum = refs[5:]
        delta = mine[...] + other[...]
        new_sum[...] = sum_ref[...] + delta
        state = (x_ref[...].astype(F32) + delta).astype(BF16)
        new_x[...] = state
        wide = state.astype(F32)
    tiles = []
    for out, who in ((give, 1 - place[0]), (keep, place[0])):
        at = 0
        for index, weight in enumerate(weights):
            half = weight.shape[1] // 2
            tile = min(1024, half)
            for begin in range(0, half, tile):
                columns = pl.ds(pl.multiple_of(who * half + begin, tile), tile)
                tiles.append((out, at + begin, tile, index, columns))
            at += half
    copies = []
    if first:
        copies = copied(
            [(x_ref, buffers[3]), (gain, buffers[4])]
            + [
                (weights[index].at[:, columns], buffers[index].at[:, columns])
                for _, _, _, index, columns in tiles
            ],
            sems,
        )
        weights = buffers
        copies[0].wait()
        copies[1].wait()
        wide = buffers[3][...].astype(F32)
        gain = buffers[4]
    scaled = (wide * gain[...]).astype(BF16)
    squares = jnp.sum(wide * wide, axis=1, keepdims=True)
    column = lanes(wide.shape[0])
    for out in (give, keep):
        out[:, out.shape[1] - LANES :] = jnp.where(column == 0, squares, 0.0)
    for n, (out, at, tile, index, columns) in enumerate(tiles):
        if copies:
            copies[n + 2].wait()
        out[:, at : at + tile] = jnp.dot(
            scaled, weights[index][:, columns], preferred_element_type=F32
        )


def project(place, x, gain, weights, rest):
    rows = x.shape[0]
    width = sum(w.shape[1] for w in weights) // 2 + LANES
    out_shape = [jax.ShapeDtypeStruct((rows, width), F32)] * 2
    if rest:
        weights = [resident(weight) for weight in weights]
        scratch = []
        out_shape = out_shape + [
            jax.ShapeDtypeStruct(x.shape, BF16),
            jax.ShapeDtypeStruct(x.shape, F32),
        ]
    else:
        weights = [in_hbm(weight) for weight in weights]
        x, gain = in_hbm(x), in_hbm(gain)
        count = 2 + 2 * sum(max(1, w.shape[1] // 2048) for w in weights)
        scratch = [pltpu.VMEM(w.shape, w.dtype) for w in (*weights, x, gain)]
        scratch.append(pltpu.SemaphoreType.DMA((count,)))
    return pl.pallas_call(
        functools.partial(project_kernel, not rest),
        out_shape=out_shape,
        in_specs=[SMEM_SPEC]
        + [VMEM_SPEC if rest else HBM_SPEC] * 5
        + [VMEM_SPEC] * len(rest),
        out_specs=[VMEM_SPEC] * len(out_shape),
        scratch_shapes=scratch,
        compiler_params=PARAMS if rest else LARGE_PARAMS,
    )(place, x, gain, *weights, *rest)


def pair_sum_kernel(keep, got, total, sent):
    both = keep[...] + got[...]
    total[...] = both
    main = both.shape[1] - LANES
    sent[:, :main] = both[:, :main].astype(BF16)
    column = lanes(both.shape[0])
    high, middle, low = pieces(both[:, main : main + 1])
    sent[:, main:] = jnp.where(
        column == 0, high, jnp.where(column == 1, middle, jnp.where(column == 2, low, 0.0))
    ).astype(BF16)


def pair_sum(keep, got):
    return pl.pallas_call(
        pair_sum_kernel,
        out_shape=[
            jax.ShapeDtypeStruct(keep.shape, F32),
            jax.ShapeDtypeStruct(keep.shape, BF16),
        ],
        in_specs=[VMEM_SPEC] * 2,
        out_specs=[VMEM_SPEC] * 2,
        compiler_params=PARAMS,
    )(keep, got)


def lane_fold(fold, array):
    parts = [array[:, at : at + LANES] for at in range(0, array.shape[1], LANES)]
    return functools.reduce(fold, parts)


def row_max(arrays):
    folded = [lane_fold(jnp.maximum, array) for array in arrays]
    return jnp.max(functools.reduce(jnp.maximum, folded), axis=1, keepdims=True)


def against(rows, keys):
    return lax.dot_general(
        rows, keys, (((1,), (1,)), ((), ())), preferred_element_type=F32
    )


def weigh(scores, top, values, scale):
    total, acc = None, None
    for score, value in zip(scores, values):
        expo = jnp.exp2((score - top) * scale)
        part = lane_fold(jnp.add, expo)
        term = jnp.dot(expo.astype(BF16), value, preferred_element_type=F32)
        total = part if total is None else total + part
        acc = term if acc is None else acc + term
    return jnp.sum(total, axis=1, keepdims=True), acc


def attend_kernel(features, step, others, place, *refs):
    total_ref = refs[0]
    got = refs[1 : 1 + others]
    cos_ref, sin_ref, bias_ref = refs[1 + others : 4 + others]
    own_prefix, own_suffix, *far = refs[4 + others : (10 if step == 0 else 8) + others]
    refs = refs[(10 if step == 0 else 8) + others :]
    old, (sent, stat, fresh) = refs[:step], refs[step : 3 + step]
    heads = own_prefix.shape[1]
    waits = []
    if step == 0:
        got_prefix, got_suffix, sems = refs[3:]
        waits = copied(halves(place, far, got_prefix, got_suffix), sems)
    else:
        got_prefix, got_suffix = far
    prefix = (own_prefix, got_prefix)
    suffix = (own_suffix, got_suffix)
    rows = total_ref.shape[0]
    width = total_ref.shape[1] - LANES
    query_width = width - 2 * heads * HD
    base, starts = place[1], (place[2], place[3])
    scale = LOG2E / math.sqrt(HD)

    stats = total_ref[:, width : width + 1]
    for ref in got:
        stats = stats + jnp.sum(ref[:, width:].astype(F32), axis=1, keepdims=True)
    inverse = lax.rsqrt(stats / features + 1e-05)
    cosine = cos_ref[...]
    sine = sin_ref[...]

    def block(at):
        value = total_ref[:, at : at + HD]
        for ref in got:
            value = value + ref[:, at : at + HD].astype(F32)
        return value * inverse

    def turned(at):
        value = block(at)
        return (value * cosine + pltpu.roll(value, HD // 2, 1) * sine).astype(BF16)

    sample = lax.broadcasted_iota(jnp.int32, (rows, 1), 0)
    owned = (sample >= base) & (sample < base + 2 * SAMP_DEV)
    few_rows = SAMP_DEV * GROUP
    pick_row = lax.broadcasted_iota(jnp.int32, (few_rows, GROUP * rows), 0)
    pick_column = lax.broadcasted_iota(jnp.int32, (few_rows, GROUP * rows), 1)
    spot = (pick_row // SAMP_DEV) * rows + pick_row % SAMP_DEV
    picks = [(pick_column == spot + start).astype(F32).astype(BF16) for start in starts]
    column = lanes(rows)

    queries = [
        [turned((head * GROUP + g) * HD) for g in range(GROUP)] for head in range(heads)
    ]
    packed = [jnp.concatenate(query, axis=0) for query in queries]
    keys, values = [], []
    for head in range(heads):
        new_key = turned(query_width + head * HD)
        new_value = block(query_width + (heads + head) * HD).astype(BF16)
        key_part = slice(head * HD, (head + 1) * HD)
        value_part = slice((heads + head) * HD, (heads + head + 1) * HD)
        fresh[:, key_part] = new_key
        fresh[:, value_part] = new_value
        keys.append([ref[:, key_part].astype(F32) for ref in old] + [new_key.astype(F32)])
        values.append([ref[:, value_part].astype(F32) for ref in old] + [new_value.astype(F32)])
    few = [
        [jnp.dot(pick, packed[head], preferred_element_type=F32).astype(BF16) for pick in picks]
        for head in range(heads)
    ]
    fresh_scores = [
        [
            [
                jnp.sum(query.astype(F32) * key, axis=1, keepdims=True)
                for key in keys[head]
            ]
            for query in queries[head]
        ]
        for head in range(heads)
    ]

    slots, page = own_suffix.shape[1], own_suffix.shape[3]
    length = own_prefix.shape[2]
    chunk = min(2048, length)
    pieces_of = [(src, at) for src in range(2) for at in range(0, length, chunk)]

    def pool(kind, src, head):
        return suffix[src][kind, :, head].reshape(slots * page, HD)

    near_scores = [[None] * 2 for _ in range(heads)]
    far_scores = [[None] * len(pieces_of) for _ in range(heads)]
    for src in range(2):
        if src == 1:
            for copy in waits[:2]:
                copy.wait()
        for head in range(heads):
            near_scores[head][src] = against(few[head][src], pool(0, src, head)) + bias_ref[src]
            for n, (whose, at) in enumerate(pieces_of):
                if whose == src:
                    far_scores[head][n] = against(
                        packed[head], prefix[src][0, head, at : at + chunk]
                    )
    near_tops = [[row_max([score]) for score in scores] for scores in near_scores]
    far_tops = [row_max(scores) for scores in far_scores]
    for copy in waits[2:]:
        copy.wait()
    near = [
        [
            weigh([near_scores[head][src]], near_tops[head][src], [pool(1, src, head)], scale)
            for src in range(2)
        ]
        for head in range(heads)
    ]

    stat_value = jnp.zeros((rows, LANES), F32)
    for head in range(heads):
        far_total, far_acc = weigh(
            far_scores[head],
            far_tops[head],
            [prefix[src][1, head, at : at + chunk] for src, at in pieces_of],
            scale,
        )
        for g in range(GROUP):
            part = slice(g * rows, (g + 1) * rows)
            far_top = far_tops[head][part]
            near_top = jnp.full((rows, 1), -1e30, F32)
            total = jnp.zeros((rows, 1), F32)
            acc = jnp.zeros((rows, HD), F32)
            for src in range(2):
                for j in range(SAMP_DEV):
                    line = slice(g * SAMP_DEV + j, g * SAMP_DEV + j + 1)
                    here = sample == starts[src] + j
                    near_top = jnp.where(here, near_tops[head][src][line], near_top)
                    total = jnp.where(here, near[head][src][0][line], total)
                    acc = jnp.where(here, near[head][src][1][line], acc)
            top = jnp.maximum(far_top, near_top)
            scores = fresh_scores[head][g]
            for score in scores:
                top = jnp.where(owned, jnp.maximum(top, score), top)
            far_weight = jnp.exp2((far_top - top) * scale)
            near_weight = jnp.exp2((near_top - top) * scale)
            total = total * near_weight + far_total[part] * far_weight
            acc = acc * near_weight + far_acc[part] * far_weight
            for score, value in zip(scores, values[head]):
                expo = jnp.where(owned, jnp.exp2(jnp.where(owned, score - top, 0.0) * scale), 0.0)
                total = total + expo
                acc = acc + expo.astype(BF16).astype(F32) * value
            index = head * GROUP + g
            sent[:, index * HD : (index + 1) * HD] = (acc / total).astype(BF16)
            level = top * scale + jnp.log2(total)
            stat_value = jnp.where(column == index, level, stat_value)
    high, middle, low = pieces(stat_value)
    many = heads * GROUP
    stat[...] = stat_value
    shifted = high + pltpu.roll(middle, many, 1) + pltpu.roll(low, 2 * many, 1)
    sent[:, many * HD :] = shifted.astype(BF16)


def attend(features, step, place, total, got, tables, caches, old):
    rows = total.shape[0]
    own, far = caches
    heads = own[0].shape[1]
    if step == 0:
        inputs = [resident(array) for array in own] + [in_hbm(array) for array in far]
        specs = [VMEM_SPEC] * 2 + [HBM_SPEC] * 4
        out_shape = [pltpu.VMEM(part.shape, BF16) for part in own]
        scratch = [pltpu.SemaphoreType.DMA((4,))]
    else:
        inputs = [resident(array) for array in (*own, *far)]
        specs = [VMEM_SPEC] * 4
        out_shape, scratch = [], []
    small = [total, *got, *tables]
    return pl.pallas_call(
        functools.partial(attend_kernel, features, step, len(got)),
        out_shape=[
            jax.ShapeDtypeStruct((rows, heads * GROUP * HD + LANES), BF16),
            jax.ShapeDtypeStruct((rows, LANES), F32),
            jax.ShapeDtypeStruct((rows, 2 * heads * HD), BF16),
            *out_shape,
        ],
        in_specs=[SMEM_SPEC] + [VMEM_SPEC] * len(small) + specs + [VMEM_SPEC] * len(old),
        out_specs=[VMEM_SPEC] * (3 + len(out_shape)),
        scratch_shapes=scratch,
        compiler_params=LARGE_PARAMS,
    )(place, *small, *inputs, *old)


def merge_kernel(own, stat, *refs):
    got, out = refs[:-1], refs[-1]
    many = out.shape[1] // HD
    levels = [stat[...]]
    for ref in got:
        packed = ref[:, many * HD :].astype(F32)
        levels.append(
            packed
            + pltpu.roll(packed, LANES - many, 1)
            + pltpu.roll(packed, LANES - 2 * many, 1)
        )
    top = functools.reduce(jnp.maximum, levels)
    weights = [jnp.exp2(level - top) for level in levels]
    share = 1.0 / functools.reduce(jnp.add, weights)
    weights = [weight * share for weight in weights]
    for index in range(many):
        part = slice(index * HD, (index + 1) * HD)
        value = own[:, part].astype(F32) * weights[0][:, index : index + 1]
        for ref, weight in zip(got, weights[1:]):
            value = value + ref[:, part].astype(F32) * weight[:, index : index + 1]
        out[:, part] = value.astype(BF16)


def merge(own, stat, got):
    return pl.pallas_call(
        merge_kernel,
        out_shape=jax.ShapeDtypeStruct((own.shape[0], own.shape[1] - LANES), BF16),
        in_specs=[VMEM_SPEC] * (2 + len(got)),
        out_specs=VMEM_SPEC,
        compiler_params=PARAMS,
    )(own, stat, *got)


def output_kernel(place, mine, other, weight, out):
    half = mine.shape[1]
    side = place[0]
    here = pl.ds(pl.multiple_of(side * half, half), half)
    there = pl.ds(pl.multiple_of((1 - side) * half, half), half)
    out[...] = jnp.dot(mine[...], weight[here], preferred_element_type=F32) + jnp.dot(
        other[...], weight[there], preferred_element_type=F32
    )


def output(place, mine, other, weight):
    return pl.pallas_call(
        output_kernel,
        out_shape=jax.ShapeDtypeStruct((mine.shape[0], weight.shape[1]), F32),
        in_specs=[SMEM_SPEC] + [VMEM_SPEC] * 3,
        out_specs=VMEM_SPEC,
        compiler_params=PARAMS,
    )(place, mine, other, weight)


def swapped(array, axis):
    return lax.ppermute(array, axis, [(0, 1), (1, 0)])


def from_others(array, axis):
    size = lax.axis_size(axis)
    return [
        lax.ppermute(array, axis, [(i, (i + hop) % size) for i in range(size)])
        for hop in range(1, size)
    ]


def local_split(
    hidden,
    gain,
    w_query,
    w_key,
    w_value,
    w_out,
    prefix_keys,
    prefix_values,
    suffix_keys,
    suffix_values,
    suffix_lengths,
    page_table,
):
    samples, width = hidden.shape
    features = width * lax.axis_size(("seq", "side"))
    seq = lax.axis_index("seq")
    side = lax.axis_index("side")
    base = seq * (2 * SAMP_DEV)
    first_own = base + (1 - side) * SAMP_DEV
    first_got = base + side * SAMP_DEV
    place = jnp.stack([side, base, first_own, first_got]).astype(jnp.int32)
    pools = (prefix_keys, prefix_values, suffix_keys, suffix_values)
    weights = (w_query, w_key, w_value)
    far = [swapped(pool, "side") for pool in pools[2:]]
    bias = live_bias(place, suffix_lengths, page_table, suffix_keys.shape[2])
    half = HD // 2
    freq = 500000.0 ** (-(jnp.arange(half, dtype=F32) * 2.0 / HD))
    position = (
        PREFIX + suffix_lengths[None, :] + jnp.arange(STEPS, dtype=jnp.int32)[:, None]
    ).astype(F32)
    angle = position[..., None] * freq
    cosine, sine = jnp.cos(angle), jnp.sin(angle)
    cosine = jnp.concatenate([cosine, cosine], axis=-1)
    sine = jnp.concatenate([-sine, sine], axis=-1)
    gain_row = gain[None, :]

    state = hidden
    update = jnp.zeros(hidden.shape, F32)
    rest = ()
    old = []
    for step in range(STEPS):
        keep, give, *more = project(place, state, gain_row, weights, rest)
        got_sum = swapped(give, "side")
        if rest:
            state, update = more
        else:
            got_sum, *given = lax.optimization_barrier((got_sum, *far, *pools[:2]))
            far = [swapped(pool, "side") for pool in given[2:]] + given[:2]
        total, sent = pair_sum(keep, got_sum)
        if not rest:
            *own, out_weight = load(place, pools, [w_out], sent)
        got = from_others(sent, "seq")
        sent, stat, fresh, *kept = attend(
            features, step, place, total, got, (cosine[step], sine[step], bias), (own, far), old
        )
        far = kept or far
        got = from_others(sent, "seq")
        if not rest:
            weights = load(place, (), weights, stat)
            got, weights = lax.optimization_barrier((got, weights))
        old.append(fresh)
        mixed = merge(sent, stat, got)
        part = output(place, mixed, swapped(mixed, "side"), resident(out_weight))
        rest = (update, part, swapped(part, "head"))
    delta = rest[1] + rest[2]
    return ((state.astype(F32) + delta).astype(BF16), update + delta)


def fits(mesh, args):
    heads = args[4].shape[1] // HD // mesh.shape["head"]
    return (
        mesh.shape["head"] == 2
        and mesh.shape["side"] == 2
        and heads % 2 == 0
        and args[6].shape[0] == mesh.shape["groups"]
        and heads // 2 * GROUP * 3 <= LANES
    )


def solution(mesh):
    placed = (
        P("groups", ("seq", "side")),
        P(("seq", "side")),
        P(("seq", "side"), "head"),
        P(("seq", "side"), "head"),
        P(("seq", "side"), "head"),
        P("head", ("seq", "side")),
        P("groups", "head", ("seq", "side"), None),
        P("groups", "head", ("seq", "side"), None),
        P(("groups", "seq", "side"), "head", None, None),
        P(("groups", "seq", "side"), "head", None, None),
        P("groups"),
        P("groups", None),
    )

    def whole(*args):
        return jax.shard_map(
            local_split if fits(mesh, args) else local_any,
            mesh=mesh,
            in_specs=placed,
            out_specs=(P("groups", ("seq", "side")), P("groups", ("seq", "side"))),
            check_vma=False,
        )(*args)

    return whole
```

```python
import functools
import math

import jax
import jax.numpy as jnp
from jax import lax
from jax.experimental import pallas as pl
from jax.experimental.pallas import tpu as pltpu
from jax.sharding import PartitionSpec as P

D = 8192
HD = 128
GROUP = 8
SAMP_DEV = 2
PREFIX = 32768
STEPS = 3


def combined_all(array, axis, combine):
    everything = jax.tree.map(lambda part: lax.all_gather(part, axis), array)
    first = jax.tree.map(lambda part: part[0], everything)

    def lap(k, so_far):
        return combine(so_far, jax.tree.map(lambda part: part[k], everything))

    return lax.fori_loop(1, lax.axis_size(axis), lap, first)


def rotate(vectors, position):
    half = vectors.shape[-1] // 2
    freq = 500000.0 ** (-(jnp.arange(half, dtype=jnp.float32) * 2.0 / vectors.shape[-1]))
    angle = position[..., None] * freq
    cosine = jnp.cos(angle)
    sine = jnp.sin(angle)
    lower = vectors[..., :half]
    upper = vectors[..., half:]
    return jnp.concatenate([lower * cosine - upper * sine, upper * cosine + lower * sine], axis=-1)


def combine(first, second):
    acc_a, top_a, total_a = first
    acc_b, top_b, total_b = second
    top = jnp.maximum(top_a, top_b)
    weight_a = jnp.exp(top_a - top)
    weight_b = jnp.exp(top_b - top)
    return (
        acc_a * weight_a[..., None] + acc_b * weight_b[..., None],
        top,
        total_a * weight_a + total_b * weight_b,
    )


def local_any(
    hidden,
    gain,
    w_query,
    w_key,
    w_value,
    w_out,
    prefix_keys,
    prefix_values,
    suffix_keys,
    suffix_values,
    suffix_lengths,
    page_table,
):
    samples = hidden.shape[0]
    kv_local = w_key.shape[1] // HD
    query_width = kv_local * GROUP * HD
    key_width = kv_local * HD
    prompts = prefix_keys.shape[0]
    scale = 1.0 / math.sqrt(HD)
    rank = lax.axis_index(("seq", "side"))
    w_proj = jnp.concatenate([w_query, w_key, w_value], axis=1)
    pool_keys, pool_values = (suffix_keys, suffix_values)
    start = jnp.bitwise_xor(rank, 1) * SAMP_DEV
    table_rows = lax.dynamic_slice_in_dim(page_table, start, SAMP_DEV, 0)
    page_keys = pool_keys[table_rows]
    page_values = pool_values[table_rows]
    length_rows = lax.dynamic_slice_in_dim(suffix_lengths, start, SAMP_DEV, 0)
    page_count = page_keys.shape[1]
    page_size = page_keys.shape[3]
    suffix_span = page_count * page_size
    live = (jnp.arange(suffix_span, dtype=jnp.int32)[None, :] < length_rows[:, None])[
        :, None, None, :
    ]
    state = hidden
    update = jnp.zeros(hidden.shape, jnp.float32)
    new_keys = []
    new_values = []
    for step in range(STEPS):
        wide = state.astype(jnp.float32)
        scaled = (wide * gain).astype(jnp.bfloat16)
        partial_value = jnp.dot(scaled, w_proj, preferred_element_type=jnp.float32)
        squares = jnp.sum(wide * wide, axis=1)
        proj, total_sq = lax.psum((partial_value, squares), ("seq", "side"))
        inverse = lax.rsqrt(total_sq / D + 1e-05)[:, None]
        position = (PREFIX + suffix_lengths + step).astype(jnp.float32)
        query = rotate(
            (proj[:, :query_width] * inverse).reshape(samples, kv_local, GROUP, HD),
            position[:, None, None],
        ).astype(jnp.bfloat16)
        new_keys.append(
            rotate(
                (proj[:, query_width : query_width + key_width] * inverse).reshape(
                    samples, kv_local, HD
                ),
                position[:, None],
            ).astype(jnp.bfloat16)
        )
        new_values.append(
            (proj[:, query_width + key_width :] * inverse)
            .reshape(samples, kv_local, HD)
            .astype(jnp.bfloat16)
        )
        stacked_keys = jnp.stack(new_keys, axis=1)
        stacked_values = jnp.stack(new_values, axis=1)
        grouped = query.reshape(prompts, samples // prompts, kv_local, GROUP, HD)
        scores = (
            jnp.einsum(
                "pgkhd,pkld->pgkhl", grouped, prefix_keys, preferred_element_type=jnp.float32
            )
            * scale
        )
        top = jnp.max(scores, axis=-1)
        expo = jnp.exp(scores - top[..., None])
        total = jnp.sum(expo, axis=-1)
        acc = jnp.einsum(
            "pgkhl,pkld->pgkhd",
            expo.astype(jnp.bfloat16),
            prefix_values,
            preferred_element_type=jnp.float32,
        )
        acc = acc.reshape(samples, kv_local, GROUP, HD)
        top = top.reshape(samples, kv_local, GROUP)
        total = total.reshape(samples, kv_local, GROUP)
        own_query = lax.dynamic_slice_in_dim(query, start, SAMP_DEV, 0)
        own_keys = lax.dynamic_slice_in_dim(stacked_keys, start, SAMP_DEV, 0)
        own_values = lax.dynamic_slice_in_dim(stacked_values, start, SAMP_DEV, 0)
        suffix_scores = jnp.einsum(
            "skhd,spkjd->skhpj", own_query, page_keys, preferred_element_type=jnp.float32
        )
        suffix_scores = suffix_scores.reshape(SAMP_DEV, kv_local, GROUP, suffix_span) * scale
        suffix_scores = jnp.where(live, suffix_scores, -jnp.inf)
        fresh_scores = (
            jnp.einsum("skhd,sukd->skhu", own_query, own_keys, preferred_element_type=jnp.float32)
            * scale
        )
        peak = jnp.maximum(jnp.max(suffix_scores, axis=-1), jnp.max(fresh_scores, axis=-1))
        suffix_expo = jnp.exp(suffix_scores - peak[..., None])
        fresh_expo = jnp.exp(fresh_scores - peak[..., None])
        near_total = jnp.sum(suffix_expo, axis=-1) + jnp.sum(fresh_expo, axis=-1)
        near_acc = jnp.einsum(
            "skhpj,spkjd->skhd",
            suffix_expo.astype(jnp.bfloat16).reshape(
                SAMP_DEV, kv_local, GROUP, page_count, page_size
            ),
            page_values,
            preferred_element_type=jnp.float32,
        )
        near_acc = near_acc + jnp.einsum(
            "skhu,sukd->skhd",
            fresh_expo.astype(jnp.bfloat16),
            own_values,
            preferred_element_type=jnp.float32,
        )
        rows_now = (
            lax.dynamic_slice_in_dim(acc, start, SAMP_DEV, 0),
            lax.dynamic_slice_in_dim(top, start, SAMP_DEV, 0),
            lax.dynamic_slice_in_dim(total, start, SAMP_DEV, 0),
        )
        joined = combine(rows_now, (near_acc, peak, near_total))
        acc = lax.dynamic_update_slice_in_dim(acc, joined[0], start, 0)
        top = lax.dynamic_update_slice_in_dim(top, joined[1], start, 0)
        total = lax.dynamic_update_slice_in_dim(total, joined[2], start, 0)
        acc, top, total = combined_all((acc, top, total), ("seq", "side"), combine)
        mixed = (acc / total[..., None]).astype(jnp.bfloat16).reshape(samples, query_width)
        part = jnp.dot(mixed, w_out, preferred_element_type=jnp.float32)
        delta = lax.psum(part, "head")
        update = update + delta
        state = (wide + delta).astype(jnp.bfloat16)
    return (state, update)


LANES = 128
LOG2E = 1.4426950408889634
BF16 = jnp.bfloat16
F32 = jnp.float32
VMEM_SPEC = pl.BlockSpec(memory_space=pltpu.VMEM)
SMEM_SPEC = pl.BlockSpec(memory_space=pltpu.SMEM)
HBM_SPEC = pl.BlockSpec(memory_space=pltpu.HBM)
PARAMS = pltpu.CompilerParams(vmem_limit_bytes=4 * 1024 * 1024)
LARGE_PARAMS = pltpu.CompilerParams(vmem_limit_bytes=13 * 1024 * 1024)
COST = pl.CostEstimate(flops=1 << 28, bytes_accessed=1 << 22, transcendentals=0)


def resident(array):
    return pltpu.with_memory_space_constraint(array, pltpu.VMEM)


def in_hbm(array):
    return pltpu.with_memory_space_constraint(array, pltpu.HBM)


def lanes(rows):
    return lax.broadcasted_iota(jnp.int32, (rows, LANES), 1)


def pieces(values):
    high = values.astype(BF16).astype(F32)
    middle = (values - high).astype(BF16).astype(F32)
    return high, middle, values - high - middle


def move(copies):
    for copy in copies:
        copy.start()
    for copy in copies:
        copy.wait()


def copied(pairs, sems):
    copies = [
        pltpu.make_async_copy(source, target, sems.at[n])
        for n, (source, target) in enumerate(pairs)
    ]
    for copy in copies:
        copy.start()
    return copies


def halves(place, pools, prefix, suffix):
    heads = prefix.shape[1]
    part = pl.ds(place[0] * heads, heads)
    pk, pv, sk, sv = pools
    return [
        (sk.at[:, part], suffix.at[0]),
        (pk.at[0, part], prefix.at[0]),
        (sv.at[:, part], suffix.at[1]),
        (pv.at[0, part], prefix.at[1]),
    ]


def half_shapes(pools):
    pk, sk = pools[0], pools[2]
    return [
        pltpu.VMEM((2, pk.shape[1] // 2) + pk.shape[2:], pk.dtype),
        pltpu.VMEM((2, sk.shape[0], sk.shape[1] // 2) + sk.shape[2:], sk.dtype),
    ]


def live_bias(place, lengths, table, bias):
    pages = table.shape[1]
    page = bias.shape[2] // (SAMP_DEV * pages)
    row = lax.broadcasted_iota(jnp.int32, (bias.shape[1], page), 0)
    column = lax.broadcasted_iota(jnp.int32, (bias.shape[1], page), 1)
    for pool in range(2):
        for j in range(SAMP_DEV):
            sample = place[2 + pool] + j
            mine = row % SAMP_DEV == j
            for p in range(pages):
                live = mine & (column < lengths[sample] - p * page)
                spot = pl.ds(pl.multiple_of(table[sample, p] * page, page), page)
                bias[pool, :, spot] = jnp.where(live, 0.0, -jnp.inf)


def load_caches_kernel(
    place, lengths, table, pk, pv, sk, sv, w_out, after, prefix, suffix, kept_out, bias, sems
):
    pairs = halves(place, (pk, pv, sk, sv), prefix, suffix) + [(w_out, kept_out)]
    copies = copied(pairs, sems)
    live_bias(place, lengths, table, bias)
    for copy in copies:
        copy.wait()


def load_caches(place, lengths, table, pools, w_out, after):
    page = pools[2].shape[2]
    tokens = SAMP_DEV * table.shape[1] * page
    sources = [in_hbm(array) for array in (*pools, w_out)]
    return pl.pallas_call(
        load_caches_kernel,
        out_shape=half_shapes(pools)
        + [
            pltpu.VMEM(w_out.shape, w_out.dtype),
            jax.ShapeDtypeStruct((2, SAMP_DEV * GROUP, tokens), F32),
        ],
        in_specs=[SMEM_SPEC] * 3 + [HBM_SPEC] * 5 + [VMEM_SPEC],
        out_specs=[VMEM_SPEC] * 4,
        scratch_shapes=[pltpu.SemaphoreType.DMA((5,))],
        compiler_params=PARAMS,
        cost_estimate=pl.CostEstimate(flops=0, bytes_accessed=1 << 25, transcendentals=0),
    )(place, lengths, table, *sources, after)


def load_kernel(*refs):
    count = len(refs) // 2 - 1
    for copy in copied(zip(refs[:count], refs[count + 1 : -1]), refs[-1]):
        copy.wait()


def load(weights, after):
    return pl.pallas_call(
        load_kernel,
        out_shape=[pltpu.VMEM(w.shape, w.dtype) for w in weights],
        in_specs=[HBM_SPEC] * len(weights) + [VMEM_SPEC],
        out_specs=[VMEM_SPEC] * len(weights),
        scratch_shapes=[pltpu.SemaphoreType.DMA((len(weights),))],
        compiler_params=PARAMS,
        cost_estimate=pl.CostEstimate(flops=0, bytes_accessed=1 << 25, transcendentals=0),
    )(*[in_hbm(weight) for weight in weights], after)


def column_tiles(place, weights, who):
    tiles, at = [], 0
    for index, weight in enumerate(weights):
        half = weight.shape[1] // 2
        tile = min(1024, half)
        for begin in range(0, half, tile):
            columns = pl.ds(pl.multiple_of(who * half + begin, tile), tile)
            tiles.append((index, columns, slice(at + begin, at + begin + tile)))
        at += half
    return tiles


def first_project_kernel(place, *refs):
    sources, (keep, give, *buffers, sems) = refs[:5], refs[5:]
    weights, (x_ref, gain) = buffers[:3], buffers[3:]
    outs = ((give, 1 - place[0]), (keep, place[0]))
    tiles = [
        (out, *tile) for out, who in outs for tile in column_tiles(place, weights, who)
    ]
    pairs = list(zip(sources[3:], buffers[3:]))
    for _, index, columns, _ in tiles:
        pairs.append((sources[index].at[:, columns], weights[index].at[:, columns]))
    copies = copied(pairs, sems)
    copies[0].wait()
    copies[1].wait()
    wide = x_ref[...].astype(F32)
    scaled = (wide * gain[...]).astype(BF16)
    squares = jnp.sum(wide * wide, axis=1, keepdims=True)
    column = lanes(wide.shape[0])
    for out in (give, keep):
        out[:, out.shape[1] - LANES :] = jnp.where(column == 0, squares, 0.0)
    for copy, (out, index, columns, to) in zip(copies[2:], tiles):
        copy.wait()
        out[:, to] = jnp.dot(
            scaled, weights[index][:, columns], preferred_element_type=F32
        )


def first_project(place, x, gain, weights):
    rows = x.shape[0]
    width = sum(w.shape[1] for w in weights) // 2 + LANES
    sources = [in_hbm(array) for array in (*weights, x, gain)]
    count = 2 + 2 * sum(max(1, w.shape[1] // 2048) for w in weights)
    return pl.pallas_call(
        first_project_kernel,
        out_shape=[jax.ShapeDtypeStruct((rows, width), F32)] * 2,
        in_specs=[SMEM_SPEC] + [HBM_SPEC] * 5,
        out_specs=[VMEM_SPEC] * 2,
        scratch_shapes=[pltpu.VMEM(array.shape, array.dtype) for array in sources]
        + [pltpu.SemaphoreType.DMA((count,))],
        compiler_params=LARGE_PARAMS,
    )(place, *sources)


def give_kernel(place, x_ref, gain, sum_ref, mine, other, *refs):
    weights, (give, scaled_ref, new_x, new_sum) = refs[:3], refs[3:]
    delta = mine[...].astype(F32) + other[...].astype(F32)
    new_sum[...] = sum_ref[...] + delta
    state = (x_ref[...].astype(F32) + delta).astype(BF16)
    new_x[...] = state
    wide = state.astype(F32)
    scaled = (wide * gain[...]).astype(BF16)
    scaled_ref[...] = scaled
    squares = jnp.sum(wide * wide, axis=1, keepdims=True)
    column = lanes(wide.shape[0])
    give[:, give.shape[1] - LANES :] = jnp.where(column == 0, squares, 0.0)
    for index, columns, to in column_tiles(place, weights, 1 - place[0]):
        give[:, to] = jnp.dot(
            scaled, weights[index][:, columns], preferred_element_type=F32
        )


def give_project(place, x, gain, weights, rest):
    rows = x.shape[0]
    width = sum(w.shape[1] for w in weights) // 2 + LANES
    return pl.pallas_call(
        give_kernel,
        out_shape=[
            jax.ShapeDtypeStruct((rows, width), F32),
            jax.ShapeDtypeStruct(x.shape, BF16),
            jax.ShapeDtypeStruct(x.shape, BF16),
            jax.ShapeDtypeStruct(x.shape, F32),
        ],
        in_specs=[SMEM_SPEC] + [VMEM_SPEC] * 8,
        out_specs=[VMEM_SPEC] * 4,
        compiler_params=PARAMS,
        cost_estimate=COST,
    )(place, x, gain, *rest, *[resident(weight) for weight in weights])


def keep_kernel(place, scaled_ref, give, *refs):
    weights, keep = refs[:3], refs[3]
    scaled = scaled_ref[...]
    main = keep.shape[1] - LANES
    keep[:, main:] = give[:, main:]
    for index, columns, to in column_tiles(place, weights, place[0]):
        keep[:, to] = jnp.dot(
            scaled, weights[index][:, columns], preferred_element_type=F32
        )


def keep_project(place, scaled, give, weights):
    return pl.pallas_call(
        keep_kernel,
        out_shape=jax.ShapeDtypeStruct(give.shape, F32),
        in_specs=[SMEM_SPEC] + [VMEM_SPEC] * 5,
        out_specs=VMEM_SPEC,
        compiler_params=PARAMS,
        cost_estimate=COST,
    )(place, scaled, give, *[resident(weight) for weight in weights])


def pair_sum_kernel(keep, got, total, sent):
    both = keep[...] + got[...]
    total[...] = both
    main = both.shape[1] - LANES
    sent[:, :main] = both[:, :main].astype(BF16)
    column = lanes(both.shape[0])
    high, middle, low = pieces(both[:, main : main + 1])
    sent[:, main:] = jnp.where(
        column == 0, high, jnp.where(column == 1, middle, jnp.where(column == 2, low, 0.0))
    ).astype(BF16)


def pair_sum(keep, got):
    return pl.pallas_call(
        pair_sum_kernel,
        out_shape=[
            jax.ShapeDtypeStruct(keep.shape, F32),
            jax.ShapeDtypeStruct(keep.shape, BF16),
        ],
        in_specs=[VMEM_SPEC] * 2,
        out_specs=[VMEM_SPEC] * 2,
        compiler_params=PARAMS,
    )(keep, got)


def lane_fold(fold, array):
    parts = [array[:, at : at + LANES] for at in range(0, array.shape[1], LANES)]
    return functools.reduce(fold, parts)


def row_max(arrays):
    folded = [lane_fold(jnp.maximum, array) for array in arrays]
    return jnp.max(functools.reduce(jnp.maximum, folded), axis=1, keepdims=True)


def against(rows, keys):
    return lax.dot_general(
        rows, keys, (((1,), (1,)), ((), ())), preferred_element_type=F32
    )


def weigh(scores, top, values, scale):
    total, acc = None, None
    for score, value in zip(scores, values):
        expo = jnp.exp2((score - top) * scale)
        part = lane_fold(jnp.add, expo)
        term = jnp.dot(expo.astype(BF16), value, preferred_element_type=F32)
        total = part if total is None else total + part
        acc = term if acc is None else acc + term
    return jnp.sum(total, axis=1, keepdims=True), acc


def attend_kernel(features, step, others, place, *refs):
    total_ref = refs[0]
    got = refs[1 : 1 + others]
    cos_ref, sin_ref, bias_ref = refs[1 + others : 4 + others]
    own_prefix, own_suffix, *far = refs[4 + others : (10 if step == 0 else 8) + others]
    refs = refs[(10 if step == 0 else 8) + others :]
    old, (sent, stat, fresh) = refs[:step], refs[step : 3 + step]
    heads = own_prefix.shape[1]
    waits = []
    if step == 0:
        got_prefix, got_suffix, sems = refs[3:]
        waits = copied(halves(place, far, got_prefix, got_suffix), sems)
    else:
        got_prefix, got_suffix = far
    prefix = (own_prefix, got_prefix)
    suffix = (own_suffix, got_suffix)
    rows = total_ref.shape[0]
    width = total_ref.shape[1] - LANES
    query_width = width - 2 * heads * HD
    base, starts = place[1], (place[2], place[3])
    scale = LOG2E / math.sqrt(HD)

    stats = total_ref[:, width : width + 1]
    for ref in got:
        stats = stats + jnp.sum(ref[:, width:].astype(F32), axis=1, keepdims=True)
    inverse = lax.rsqrt(stats / features + 1e-05)
    cosine = cos_ref[...]
    sine = sin_ref[...]

    def block(at):
        value = total_ref[:, at : at + HD]
        for ref in got:
            value = value + ref[:, at : at + HD].astype(F32)
        return value * inverse

    def turned(at):
        value = block(at)
        return (value * cosine + pltpu.roll(value, HD // 2, 1) * sine).astype(BF16)

    sample = lax.broadcasted_iota(jnp.int32, (rows, 1), 0)
    owned = (sample >= base) & (sample < base + 2 * SAMP_DEV)
    few_rows = SAMP_DEV * GROUP
    pick_row = lax.broadcasted_iota(jnp.int32, (few_rows, GROUP * rows), 0)
    pick_column = lax.broadcasted_iota(jnp.int32, (few_rows, GROUP * rows), 1)
    spot = (pick_row // SAMP_DEV) * rows + pick_row % SAMP_DEV
    picks = [(pick_column == spot + start).astype(F32).astype(BF16) for start in starts]
    column = lanes(rows)

    queries = [
        [turned((head * GROUP + g) * HD) for g in range(GROUP)] for head in range(heads)
    ]
    packed = [jnp.concatenate(query, axis=0) for query in queries]
    keys, values = [], []
    for head in range(heads):
        new_key = turned(query_width + head * HD)
        new_value = block(query_width + (heads + head) * HD).astype(BF16)
        key_part = slice(head * HD, (head + 1) * HD)
        value_part = slice((heads + head) * HD, (heads + head + 1) * HD)
        fresh[:, key_part] = new_key
        fresh[:, value_part] = new_value
        keys.append([ref[:, key_part].astype(F32) for ref in old] + [new_key.astype(F32)])
        values.append([ref[:, value_part].astype(F32) for ref in old] + [new_value.astype(F32)])
    few = [
        [jnp.dot(pick, packed[head], preferred_element_type=F32).astype(BF16) for pick in picks]
        for head in range(heads)
    ]
    fresh_scores = [
        [
            [
                jnp.sum(query.astype(F32) * key, axis=1, keepdims=True)
                for key in keys[head]
            ]
            for query in queries[head]
        ]
        for head in range(heads)
    ]

    slots, page = own_suffix.shape[1], own_suffix.shape[3]
    length = own_prefix.shape[2]
    chunk = min(2048, length)
    pieces_of = [(src, at) for src in range(2) for at in range(0, length, chunk)]

    def pool(kind, src, head):
        return suffix[src][kind, :, head].reshape(slots * page, HD)

    near_scores = [[None] * 2 for _ in range(heads)]
    far_scores = [[None] * len(pieces_of) for _ in range(heads)]
    for src in range(2):
        if src == 1:
            for copy in waits[:2]:
                copy.wait()
        for head in range(heads):
            near_scores[head][src] = against(few[head][src], pool(0, src, head)) + bias_ref[src]
            for n, (whose, at) in enumerate(pieces_of):
                if whose == src:
                    far_scores[head][n] = against(
                        packed[head], prefix[src][0, head, at : at + chunk]
                    )
    near_tops = [[row_max([score]) for score in scores] for scores in near_scores]
    far_tops = [row_max(scores) for scores in far_scores]
    for copy in waits[2:]:
        copy.wait()
    near = [
        [
            weigh([near_scores[head][src]], near_tops[head][src], [pool(1, src, head)], scale)
            for src in range(2)
        ]
        for head in range(heads)
    ]

    stat_value = jnp.zeros((rows, LANES), F32)
    for head in range(heads):
        far_total, far_acc = weigh(
            far_scores[head],
            far_tops[head],
            [prefix[src][1, head, at : at + chunk] for src, at in pieces_of],
            scale,
        )
        for g in range(GROUP):
            part = slice(g * rows, (g + 1) * rows)
            far_top = far_tops[head][part]
            near_top = jnp.full((rows, 1), -1e30, F32)
            total = jnp.zeros((rows, 1), F32)
            acc = jnp.zeros((rows, HD), F32)
            for src in range(2):
                for j in range(SAMP_DEV):
                    line = slice(g * SAMP_DEV + j, g * SAMP_DEV + j + 1)
                    here = sample == starts[src] + j
                    near_top = jnp.where(here, near_tops[head][src][line], near_top)
                    total = jnp.where(here, near[head][src][0][line], total)
                    acc = jnp.where(here, near[head][src][1][line], acc)
            top = jnp.maximum(far_top, near_top)
            scores = fresh_scores[head][g]
            for score in scores:
                top = jnp.where(owned, jnp.maximum(top, score), top)
            far_weight = jnp.exp2((far_top - top) * scale)
            near_weight = jnp.exp2((near_top - top) * scale)
            total = total * near_weight + far_total[part] * far_weight
            acc = acc * near_weight + far_acc[part] * far_weight
            for score, value in zip(scores, values[head]):
                expo = jnp.where(owned, jnp.exp2(jnp.where(owned, score - top, 0.0) * scale), 0.0)
                total = total + expo
                acc = acc + expo.astype(BF16).astype(F32) * value
            index = head * GROUP + g
            sent[:, index * HD : (index + 1) * HD] = (acc / total).astype(BF16)
            level = top * scale + jnp.log2(total)
            stat_value = jnp.where(column == index, level, stat_value)
    high, middle, low = pieces(stat_value)
    many = heads * GROUP
    stat[...] = stat_value
    shifted = high + pltpu.roll(middle, many, 1) + pltpu.roll(low, 2 * many, 1)
    sent[:, many * HD :] = shifted.astype(BF16)


def attend(features, step, place, total, got, tables, caches, old):
    rows = total.shape[0]
    own, far = caches
    heads = own[0].shape[1]
    if step == 0:
        inputs = [resident(array) for array in own] + [in_hbm(array) for array in far]
        specs = [VMEM_SPEC] * 2 + [HBM_SPEC] * 4
        out_shape = [pltpu.VMEM(part.shape, BF16) for part in own]
        scratch = [pltpu.SemaphoreType.DMA((4,))]
    else:
        inputs = [resident(array) for array in (*own, *far)]
        specs = [VMEM_SPEC] * 4
        out_shape, scratch = [], []
    small = [total, *got, *tables]
    return pl.pallas_call(
        functools.partial(attend_kernel, features, step, len(got)),
        out_shape=[
            jax.ShapeDtypeStruct((rows, heads * GROUP * HD + LANES), BF16),
            jax.ShapeDtypeStruct((rows, LANES), F32),
            jax.ShapeDtypeStruct((rows, 2 * heads * HD), BF16),
            *out_shape,
        ],
        in_specs=[SMEM_SPEC] + [VMEM_SPEC] * len(small) + specs + [VMEM_SPEC] * len(old),
        out_specs=[VMEM_SPEC] * (3 + len(out_shape)),
        scratch_shapes=scratch,
        compiler_params=LARGE_PARAMS,
    )(place, *small, *inputs, *old)


def merge_kernel(own, stat, *refs):
    got, out = refs[:-1], refs[-1]
    many = out.shape[1] // HD
    levels = [stat[...]]
    for ref in got:
        packed = ref[:, many * HD :].astype(F32)
        levels.append(
            packed
            + pltpu.roll(packed, LANES - many, 1)
            + pltpu.roll(packed, LANES - 2 * many, 1)
        )
    top = functools.reduce(jnp.maximum, levels)
    weights = [jnp.exp2(level - top) for level in levels]
    share = 1.0 / functools.reduce(jnp.add, weights)
    weights = [weight * share for weight in weights]
    for index in range(many):
        part = slice(index * HD, (index + 1) * HD)
        value = own[:, part].astype(F32) * weights[0][:, index : index + 1]
        for ref, weight in zip(got, weights[1:]):
            value = value + ref[:, part].astype(F32) * weight[:, index : index + 1]
        out[:, part] = value.astype(BF16)


def merge(own, stat, got):
    return pl.pallas_call(
        merge_kernel,
        out_shape=jax.ShapeDtypeStruct((own.shape[0], own.shape[1] - LANES), BF16),
        in_specs=[VMEM_SPEC] * (2 + len(got)),
        out_specs=VMEM_SPEC,
        compiler_params=PARAMS,
    )(own, stat, *got)


def near_output_kernel(place, mine, weight, out):
    half = mine.shape[1]
    rows = pl.ds(pl.multiple_of(place[0] * half, half), half)
    out[...] = jnp.dot(mine[...], weight[rows], preferred_element_type=F32)


def far_output_kernel(place, other, weight, near, out):
    half = other.shape[1]
    rows = pl.ds(pl.multiple_of((1 - place[0]) * half, half), half)
    total = near[...] + jnp.dot(other[...], weight[rows], preferred_element_type=F32)
    out[...] = total.astype(BF16)


def output(place, mine, weight):
    other = swapped(mine, "side")
    shape = (mine.shape[0], weight.shape[1])
    near = pl.pallas_call(
        near_output_kernel,
        out_shape=jax.ShapeDtypeStruct(shape, F32),
        in_specs=[SMEM_SPEC] + [VMEM_SPEC] * 2,
        out_specs=VMEM_SPEC,
        compiler_params=PARAMS,
        cost_estimate=COST,
    )(place, mine, resident(weight))
    return pl.pallas_call(
        far_output_kernel,
        out_shape=jax.ShapeDtypeStruct(shape, BF16),
        in_specs=[SMEM_SPEC] + [VMEM_SPEC] * 3,
        out_specs=VMEM_SPEC,
        compiler_params=PARAMS,
    )(place, other, resident(weight), near)


def swapped(array, axis):
    return lax.ppermute(array, axis, [(0, 1), (1, 0)])


def from_others(array, axis):
    size = lax.axis_size(axis)
    return [
        lax.ppermute(array, axis, [(i, (i + hop) % size) for i in range(size)])
        for hop in range(1, size)
    ]


def local_split(
    hidden,
    gain,
    w_query,
    w_key,
    w_value,
    w_out,
    prefix_keys,
    prefix_values,
    suffix_keys,
    suffix_values,
    suffix_lengths,
    page_table,
):
    samples, width = hidden.shape
    features = width * lax.axis_size(("seq", "side"))
    seq = lax.axis_index("seq")
    side = lax.axis_index("side")
    base = seq * (2 * SAMP_DEV)
    first_own = base + (1 - side) * SAMP_DEV
    first_got = base + side * SAMP_DEV
    place = jnp.stack([side, base, first_own, first_got]).astype(jnp.int32)
    pools = (prefix_keys, prefix_values, suffix_keys, suffix_values)
    weights = (w_query, w_key, w_value)
    far = [swapped(pool, "side") for pool in pools[2:]]
    half = HD // 2
    freq = 500000.0 ** (-(jnp.arange(half, dtype=F32) * 2.0 / HD))
    position = (
        PREFIX + suffix_lengths[None, :] + jnp.arange(STEPS, dtype=jnp.int32)[:, None]
    ).astype(F32)
    angle = position[..., None] * freq
    cosine, sine = jnp.cos(angle), jnp.sin(angle)
    cosine = jnp.concatenate([cosine, cosine], axis=-1)
    sine = jnp.concatenate([-sine, sine], axis=-1)
    gain_row = gain[None, :]

    state = hidden
    update = jnp.zeros(hidden.shape, F32)
    rest = ()
    old = []
    for step in range(STEPS):
        if rest:
            give, scaled, state, update = give_project(place, state, gain_row, weights, rest)
            got_sum = swapped(give, "side")
            keep = keep_project(place, scaled, give, weights)
            total, sent = pair_sum(keep, got_sum)
        else:
            keep, give = first_project(place, state, gain_row, weights)
            got_sum = swapped(give, "side")
            got_sum, *given = lax.optimization_barrier((got_sum, *far, *pools[:2]))
            far = [swapped(pool, "side") for pool in given[2:]] + given[:2]
            total, sent = pair_sum(keep, got_sum)
            *own, out_weight, bias = load_caches(
                place, suffix_lengths, page_table, pools, w_out, sent
            )
        got = from_others(sent, "seq")
        sent, stat, fresh, *kept = attend(
            features, step, place, total, got, (cosine[step], sine[step], bias), (own, far), old
        )
        far = kept or far
        got = from_others(sent, "seq")
        if not rest:
            weights = load(weights, stat)
            got, weights = lax.optimization_barrier((got, weights))
        old.append(fresh)
        mixed = merge(sent, stat, got)
        part = output(place, mixed, out_weight)
        rest = (update, part, swapped(part, "head"))
    delta = rest[1].astype(F32) + rest[2].astype(F32)
    return ((state.astype(F32) + delta).astype(BF16), update + delta)


def fits(mesh, args):
    heads = args[4].shape[1] // HD // mesh.shape["head"]
    return (
        mesh.shape["head"] == 2
        and mesh.shape["side"] == 2
        and heads % 2 == 0
        and args[6].shape[0] == mesh.shape["groups"]
        and heads // 2 * GROUP * 3 <= LANES
    )


def solution(mesh):
    placed = (
        P("groups", ("seq", "side")),
        P(("seq", "side")),
        P(("seq", "side"), "head"),
        P(("seq", "side"), "head"),
        P(("seq", "side"), "head"),
        P("head", ("seq", "side")),
        P("groups", "head", ("seq", "side"), None),
        P("groups", "head", ("seq", "side"), None),
        P(("groups", "seq", "side"), "head", None, None),
        P(("groups", "seq", "side"), "head", None, None),
        P("groups"),
        P("groups", None),
    )

    def whole(*args):
        return jax.shard_map(
            local_split if fits(mesh, args) else local_any,
            mesh=mesh,
            in_specs=placed,
            out_specs=(P("groups", ("seq", "side")), P("groups", ("seq", "side"))),
            check_vma=False,
        )(*args)

    return whole
```

```python
import functools
import math

import jax
import jax.numpy as jnp
from jax import lax
from jax.experimental import pallas as pl
from jax.experimental.pallas import tpu as pltpu
from jax.sharding import PartitionSpec as P

D = 8192
HD = 128
GROUP = 8
SAMP_DEV = 2
PREFIX = 32768
STEPS = 3


def combined_all(array, axis, combine):
    everything = jax.tree.map(lambda part: lax.all_gather(part, axis), array)
    first = jax.tree.map(lambda part: part[0], everything)

    def lap(k, so_far):
        return combine(so_far, jax.tree.map(lambda part: part[k], everything))

    return lax.fori_loop(1, lax.axis_size(axis), lap, first)


def rotate(vectors, position):
    half = vectors.shape[-1] // 2
    freq = 500000.0 ** (-(jnp.arange(half, dtype=jnp.float32) * 2.0 / vectors.shape[-1]))
    angle = position[..., None] * freq
    cosine = jnp.cos(angle)
    sine = jnp.sin(angle)
    lower = vectors[..., :half]
    upper = vectors[..., half:]
    return jnp.concatenate([lower * cosine - upper * sine, upper * cosine + lower * sine], axis=-1)


def combine(first, second):
    acc_a, top_a, total_a = first
    acc_b, top_b, total_b = second
    top = jnp.maximum(top_a, top_b)
    weight_a = jnp.exp(top_a - top)
    weight_b = jnp.exp(top_b - top)
    return (
        acc_a * weight_a[..., None] + acc_b * weight_b[..., None],
        top,
        total_a * weight_a + total_b * weight_b,
    )


def local_any(
    hidden,
    gain,
    w_query,
    w_key,
    w_value,
    w_out,
    prefix_keys,
    prefix_values,
    suffix_keys,
    suffix_values,
    suffix_lengths,
    page_table,
):
    samples = hidden.shape[0]
    kv_local = w_key.shape[1] // HD
    query_width = kv_local * GROUP * HD
    key_width = kv_local * HD
    prompts = prefix_keys.shape[0]
    scale = 1.0 / math.sqrt(HD)
    rank = lax.axis_index(("seq", "side"))
    w_proj = jnp.concatenate([w_query, w_key, w_value], axis=1)
    pool_keys, pool_values = (suffix_keys, suffix_values)
    start = jnp.bitwise_xor(rank, 1) * SAMP_DEV
    table_rows = lax.dynamic_slice_in_dim(page_table, start, SAMP_DEV, 0)
    page_keys = pool_keys[table_rows]
    page_values = pool_values[table_rows]
    length_rows = lax.dynamic_slice_in_dim(suffix_lengths, start, SAMP_DEV, 0)
    page_count = page_keys.shape[1]
    page_size = page_keys.shape[3]
    suffix_span = page_count * page_size
    live = (jnp.arange(suffix_span, dtype=jnp.int32)[None, :] < length_rows[:, None])[
        :, None, None, :
    ]
    state = hidden
    update = jnp.zeros(hidden.shape, jnp.float32)
    new_keys = []
    new_values = []
    for step in range(STEPS):
        wide = state.astype(jnp.float32)
        scaled = (wide * gain).astype(jnp.bfloat16)
        partial_value = jnp.dot(scaled, w_proj, preferred_element_type=jnp.float32)
        squares = jnp.sum(wide * wide, axis=1)
        proj, total_sq = lax.psum((partial_value, squares), ("seq", "side"))
        inverse = lax.rsqrt(total_sq / D + 1e-05)[:, None]
        position = (PREFIX + suffix_lengths + step).astype(jnp.float32)
        query = rotate(
            (proj[:, :query_width] * inverse).reshape(samples, kv_local, GROUP, HD),
            position[:, None, None],
        ).astype(jnp.bfloat16)
        new_keys.append(
            rotate(
                (proj[:, query_width : query_width + key_width] * inverse).reshape(
                    samples, kv_local, HD
                ),
                position[:, None],
            ).astype(jnp.bfloat16)
        )
        new_values.append(
            (proj[:, query_width + key_width :] * inverse)
            .reshape(samples, kv_local, HD)
            .astype(jnp.bfloat16)
        )
        stacked_keys = jnp.stack(new_keys, axis=1)
        stacked_values = jnp.stack(new_values, axis=1)
        grouped = query.reshape(prompts, samples // prompts, kv_local, GROUP, HD)
        scores = (
            jnp.einsum(
                "pgkhd,pkld->pgkhl", grouped, prefix_keys, preferred_element_type=jnp.float32
            )
            * scale
        )
        top = jnp.max(scores, axis=-1)
        expo = jnp.exp(scores - top[..., None])
        total = jnp.sum(expo, axis=-1)
        acc = jnp.einsum(
            "pgkhl,pkld->pgkhd",
            expo.astype(jnp.bfloat16),
            prefix_values,
            preferred_element_type=jnp.float32,
        )
        acc = acc.reshape(samples, kv_local, GROUP, HD)
        top = top.reshape(samples, kv_local, GROUP)
        total = total.reshape(samples, kv_local, GROUP)
        own_query = lax.dynamic_slice_in_dim(query, start, SAMP_DEV, 0)
        own_keys = lax.dynamic_slice_in_dim(stacked_keys, start, SAMP_DEV, 0)
        own_values = lax.dynamic_slice_in_dim(stacked_values, start, SAMP_DEV, 0)
        suffix_scores = jnp.einsum(
            "skhd,spkjd->skhpj", own_query, page_keys, preferred_element_type=jnp.float32
        )
        suffix_scores = suffix_scores.reshape(SAMP_DEV, kv_local, GROUP, suffix_span) * scale
        suffix_scores = jnp.where(live, suffix_scores, -jnp.inf)
        fresh_scores = (
            jnp.einsum("skhd,sukd->skhu", own_query, own_keys, preferred_element_type=jnp.float32)
            * scale
        )
        peak = jnp.maximum(jnp.max(suffix_scores, axis=-1), jnp.max(fresh_scores, axis=-1))
        suffix_expo = jnp.exp(suffix_scores - peak[..., None])
        fresh_expo = jnp.exp(fresh_scores - peak[..., None])
        near_total = jnp.sum(suffix_expo, axis=-1) + jnp.sum(fresh_expo, axis=-1)
        near_acc = jnp.einsum(
            "skhpj,spkjd->skhd",
            suffix_expo.astype(jnp.bfloat16).reshape(
                SAMP_DEV, kv_local, GROUP, page_count, page_size
            ),
            page_values,
            preferred_element_type=jnp.float32,
        )
        near_acc = near_acc + jnp.einsum(
            "skhu,sukd->skhd",
            fresh_expo.astype(jnp.bfloat16),
            own_values,
            preferred_element_type=jnp.float32,
        )
        rows_now = (
            lax.dynamic_slice_in_dim(acc, start, SAMP_DEV, 0),
            lax.dynamic_slice_in_dim(top, start, SAMP_DEV, 0),
            lax.dynamic_slice_in_dim(total, start, SAMP_DEV, 0),
        )
        joined = combine(rows_now, (near_acc, peak, near_total))
        acc = lax.dynamic_update_slice_in_dim(acc, joined[0], start, 0)
        top = lax.dynamic_update_slice_in_dim(top, joined[1], start, 0)
        total = lax.dynamic_update_slice_in_dim(total, joined[2], start, 0)
        acc, top, total = combined_all((acc, top, total), ("seq", "side"), combine)
        mixed = (acc / total[..., None]).astype(jnp.bfloat16).reshape(samples, query_width)
        part = jnp.dot(mixed, w_out, preferred_element_type=jnp.float32)
        delta = lax.psum(part, "head")
        update = update + delta
        state = (wide + delta).astype(jnp.bfloat16)
    return (state, update)


LANES = 128
LOG2E = 1.4426950408889634
BF16 = jnp.bfloat16
F32 = jnp.float32
VMEM_SPEC = pl.BlockSpec(memory_space=pltpu.VMEM)
SMEM_SPEC = pl.BlockSpec(memory_space=pltpu.SMEM)
HBM_SPEC = pl.BlockSpec(memory_space=pltpu.HBM)
PARAMS = pltpu.CompilerParams(vmem_limit_bytes=4 * 1024 * 1024)
LARGE_PARAMS = pltpu.CompilerParams(vmem_limit_bytes=13 * 1024 * 1024)
COST = pl.CostEstimate(flops=1 << 28, bytes_accessed=1 << 22, transcendentals=0)


def resident(array):
    return pltpu.with_memory_space_constraint(array, pltpu.VMEM)


def in_hbm(array):
    return pltpu.with_memory_space_constraint(array, pltpu.HBM)


def whereabouts():
    seq, side = lax.axis_index("seq"), lax.axis_index("side")
    base = seq * (2 * SAMP_DEV)
    return side, base, base + (1 - side) * SAMP_DEV, base + side * SAMP_DEV, seq


def lanes(rows):
    return lax.broadcasted_iota(jnp.int32, (rows, LANES), 1)


def pieces(values):
    high = values.astype(BF16).astype(F32)
    middle = (values - high).astype(BF16).astype(F32)
    return high, middle, values - high - middle


def move(copies):
    for copy in copies:
        copy.start()
    for copy in copies:
        copy.wait()


def copied(pairs, sems):
    copies = [
        pltpu.make_async_copy(source, target, sems.at[n])
        for n, (source, target) in enumerate(pairs)
    ]
    for copy in copies:
        copy.start()
    return copies


def halves(place, pools, prefix, suffix):
    heads = prefix.shape[1]
    part = pl.ds(place[0] * heads, heads)
    pk, pv, sk, sv = pools
    return [
        (sk.at[:, part], suffix.at[0]),
        (pk.at[0, part], prefix.at[0]),
        (sv.at[:, part], suffix.at[1]),
        (pv.at[0, part], prefix.at[1]),
    ]


def half_shapes(pools):
    pk, sk = pools[0], pools[2]
    return [
        pltpu.VMEM((2, pk.shape[1] // 2) + pk.shape[2:], pk.dtype),
        pltpu.VMEM((2, sk.shape[0], sk.shape[1] // 2) + sk.shape[2:], sk.dtype),
    ]


def live_bias(place, lengths, table, bias):
    pages = table.shape[1]
    page = bias.shape[2] // (SAMP_DEV * pages)
    row = lax.broadcasted_iota(jnp.int32, (bias.shape[1], page), 0)
    column = lax.broadcasted_iota(jnp.int32, (bias.shape[1], page), 1)
    for pool in range(2):
        for j in range(SAMP_DEV):
            sample = place[2 + pool] + j
            mine = row % SAMP_DEV == j
            for p in range(pages):
                live = mine & (column < lengths[sample] - p * page)
                spot = pl.ds(pl.multiple_of(table[sample, p] * page, page), page)
                bias[pool, :, spot] = jnp.where(live, 0.0, -jnp.inf)


def load_caches_kernel(
    lengths, table, pk, pv, sk, sv, w_out, after, prefix, suffix, kept_out, bias, sems
):
    place = whereabouts()
    pairs = halves(place, (pk, pv, sk, sv), prefix, suffix) + [(w_out, kept_out)]
    copies = copied(pairs, sems)
    live_bias(place, lengths, table, bias)
    for copy in copies:
        copy.wait()


def load_caches(lengths, table, pools, w_out, after):
    page = pools[2].shape[2]
    tokens = SAMP_DEV * table.shape[1] * page
    sources = [in_hbm(array) for array in (*pools, w_out)]
    return pl.pallas_call(
        load_caches_kernel,
        out_shape=half_shapes(pools)
        + [
            pltpu.VMEM(w_out.shape, w_out.dtype),
            jax.ShapeDtypeStruct((2, SAMP_DEV * GROUP, tokens), F32),
        ],
        in_specs=[SMEM_SPEC] * 2 + [HBM_SPEC] * 5 + [VMEM_SPEC],
        out_specs=[VMEM_SPEC] * 4,
        scratch_shapes=[pltpu.SemaphoreType.DMA((5,))],
        compiler_params=PARAMS,
        cost_estimate=pl.CostEstimate(flops=0, bytes_accessed=1 << 25, transcendentals=0),
    )(lengths, table, *sources, after)


def load_kernel(*refs):
    count = len(refs) // 2 - 1
    for copy in copied(zip(refs[:count], refs[count + 1 : -1]), refs[-1]):
        copy.wait()


def load(weights, after):
    return pl.pallas_call(
        load_kernel,
        out_shape=[pltpu.VMEM(w.shape, w.dtype) for w in weights],
        in_specs=[HBM_SPEC] * len(weights) + [VMEM_SPEC],
        out_specs=[VMEM_SPEC] * len(weights),
        scratch_shapes=[pltpu.SemaphoreType.DMA((len(weights),))],
        compiler_params=PARAMS,
        cost_estimate=pl.CostEstimate(flops=0, bytes_accessed=1 << 25, transcendentals=0),
    )(*[in_hbm(weight) for weight in weights], after)


def column_tiles(place, weights, who):
    tiles, at = [], 0
    for index, weight in enumerate(weights):
        half = weight.shape[1] // 2
        tile = min(1024, half)
        for begin in range(0, half, tile):
            columns = pl.ds(pl.multiple_of(who * half + begin, tile), tile)
            tiles.append((index, columns, slice(at + begin, at + begin + tile)))
        at += half
    return tiles


def project_half(scaled, weights, tiles, out, arrive=lambda: None):
    vectors, width = [], 0
    for index, columns, to in tiles:
        arrive()
        part = jnp.dot(scaled, weights[index][:, columns], preferred_element_type=F32)
        if index == 0:
            out[:, to] = part
            width = to.stop
        else:
            vectors += [part[:, at : at + HD] for at in range(0, part.shape[1], HD)]
    span = 2 * SAMP_DEV
    for chip in range(scaled.shape[0] // span):
        part = slice(chip * span, (chip + 1) * span)
        out[:, width + chip * HD : width + (chip + 1) * HD] = jnp.concatenate(
            [vector[part] for vector in vectors], axis=0
        )


def first_project_kernel(*refs):
    place = whereabouts()
    sources, (keep, give, *buffers, sems) = refs[:5], refs[5:]
    weights, (x_ref, gain) = buffers[:3], buffers[3:]
    outs = ((give, 1 - place[0]), (keep, place[0]))
    halves_of = [(out, column_tiles(place, weights, who)) for out, who in outs]
    pairs = list(zip(sources[3:], buffers[3:]))
    for _, tiles in halves_of:
        for index, columns, _ in tiles:
            pairs.append((sources[index].at[:, columns], weights[index].at[:, columns]))
    copies = copied(pairs, sems)
    copies[0].wait()
    copies[1].wait()
    wide = x_ref[...].astype(F32)
    scaled = (wide * gain[...]).astype(BF16)
    squares = jnp.sum(wide * wide, axis=1, keepdims=True)
    column = lanes(wide.shape[0])
    for out in (give, keep):
        out[:, out.shape[1] - LANES :] = jnp.where(column == 0, squares, 0.0)
    waiting = iter(copies[2:])
    for out, tiles in halves_of:
        project_half(scaled, weights, tiles, out, lambda: next(waiting).wait())


def first_project(x, gain, weights):
    rows = x.shape[0]
    width = sum(w.shape[1] for w in weights) // 2 + LANES
    sources = [in_hbm(array) for array in (*weights, x, gain)]
    count = 2 + 2 * sum(max(1, w.shape[1] // 2048) for w in weights)
    return pl.pallas_call(
        first_project_kernel,
        out_shape=[jax.ShapeDtypeStruct((rows, width), F32)] * 2,
        in_specs=[HBM_SPEC] * 5,
        out_specs=[VMEM_SPEC] * 2,
        scratch_shapes=[pltpu.VMEM(array.shape, array.dtype) for array in sources]
        + [pltpu.SemaphoreType.DMA((count,))],
        compiler_params=LARGE_PARAMS,
    )(*sources)


def give_kernel(x_ref, gain, sum_ref, mine, other, *refs):
    place = whereabouts()
    weights, (give, scaled_ref, new_x, new_sum) = refs[:3], refs[3:]
    delta = mine[...].astype(F32) + other[...].astype(F32)
    new_sum[...] = sum_ref[...] + delta
    state = (x_ref[...].astype(F32) + delta).astype(BF16)
    new_x[...] = state
    wide = state.astype(F32)
    scaled = (wide * gain[...]).astype(BF16)
    scaled_ref[...] = scaled
    squares = jnp.sum(wide * wide, axis=1, keepdims=True)
    column = lanes(wide.shape[0])
    give[:, give.shape[1] - LANES :] = jnp.where(column == 0, squares, 0.0)
    project_half(scaled, weights, column_tiles(place, weights, 1 - place[0]), give)


def give_project(x, gain, weights, rest):
    rows = x.shape[0]
    width = sum(w.shape[1] for w in weights) // 2 + LANES
    return pl.pallas_call(
        give_kernel,
        out_shape=[
            jax.ShapeDtypeStruct((rows, width), F32),
            jax.ShapeDtypeStruct(x.shape, BF16),
            jax.ShapeDtypeStruct(x.shape, BF16),
            jax.ShapeDtypeStruct(x.shape, F32),
        ],
        in_specs=[VMEM_SPEC] * 8,
        out_specs=[VMEM_SPEC] * 4,
        compiler_params=PARAMS,
        cost_estimate=COST,
    )(x, gain, *rest, *[resident(weight) for weight in weights])


def keep_kernel(scaled_ref, give, *refs):
    place = whereabouts()
    weights, keep = refs[:3], refs[3]
    scaled = scaled_ref[...]
    main = keep.shape[1] - LANES
    keep[:, main:] = give[:, main:]
    project_half(scaled, weights, column_tiles(place, weights, place[0]), keep)


def keep_project(scaled, give, weights):
    return pl.pallas_call(
        keep_kernel,
        out_shape=jax.ShapeDtypeStruct(give.shape, F32),
        in_specs=[VMEM_SPEC] * 5,
        out_specs=VMEM_SPEC,
        compiler_params=PARAMS,
        cost_estimate=COST,
    )(scaled, give, *[resident(weight) for weight in weights])


def pair_sum_kernel(query_width, keep, got, total, *sent):
    place = whereabouts()
    both = keep[...] + got[...]
    total[...] = both
    rows = both.shape[0]
    main = both.shape[1] - LANES
    chips = (main - query_width) // HD
    column = lanes(rows)
    high, middle, low = pieces(both[:, main : main + 1])
    stats = jnp.where(
        column == 0, high, jnp.where(column == 1, middle, jnp.where(column == 2, low, 0.0))
    ).astype(BF16)
    query = both[:, :query_width].astype(BF16)
    for hop, out in enumerate(sent, 1):
        chip = lax.rem(place[4] + hop, chips)
        block = pl.ds(pl.multiple_of(query_width + chip * HD, HD), HD)
        out[:, :query_width] = query
        out[:, query_width : query_width + HD] = total[:, block].astype(BF16)
        out[:, query_width + HD :] = stats


def pair_sum(keep, got, query_width, hops):
    rows = keep.shape[0]
    sent = jax.ShapeDtypeStruct((rows, query_width + HD + LANES), BF16)
    return pl.pallas_call(
        functools.partial(pair_sum_kernel, query_width),
        out_shape=[jax.ShapeDtypeStruct(keep.shape, F32)] + [sent] * hops,
        in_specs=[VMEM_SPEC] * 2,
        out_specs=[VMEM_SPEC] * (1 + hops),
        compiler_params=PARAMS,
    )(keep, got)


def lane_fold(fold, array):
    parts = [array[:, at : at + LANES] for at in range(0, array.shape[1], LANES)]
    return functools.reduce(fold, parts)


def row_max(arrays):
    folded = [lane_fold(jnp.maximum, array) for array in arrays]
    return jnp.max(functools.reduce(jnp.maximum, folded), axis=1, keepdims=True)


def against(rows, keys):
    return lax.dot_general(
        rows, keys, (((1,), (1,)), ((), ())), preferred_element_type=F32
    )


def weigh(scores, top, values):
    terms = [
        jnp.dot(
            jnp.exp2(score - top).astype(BF16),
            jnp.concatenate([value, jnp.ones_like(value)], axis=1),
            preferred_element_type=F32,
        )
        for score, value in zip(scores, values)
    ]
    both = functools.reduce(jnp.add, terms)
    return both[:, HD : HD + 1], both[:, :HD]


def attend_kernel(features, step, others, *refs):
    place = whereabouts()
    total_ref = refs[0]
    got = refs[1 : 1 + others]
    cos_ref, sin_ref, new_cos, new_sin, bias_ref = refs[1 + others : 6 + others]
    refs = refs[2:]
    own_prefix, own_suffix, *far = refs[4 + others : (10 if step == 0 else 8) + others]
    refs = refs[(10 if step == 0 else 8) + others :]
    old, (sent, stat, fresh) = refs[:step], refs[step : 3 + step]
    heads = own_prefix.shape[1]
    waits = []
    if step == 0:
        got_prefix, got_suffix, sems = refs[3:]
        waits = copied(halves(place, far, got_prefix, got_suffix), sems)
    else:
        got_prefix, got_suffix = far
    prefix = (own_prefix, got_prefix)
    suffix = (own_suffix, got_suffix)
    rows = total_ref.shape[0]
    width = total_ref.shape[1] - LANES
    query_width = width - 2 * heads * HD
    base, starts = place[1], (place[2], place[3])
    scale = LOG2E / math.sqrt(HD)

    stats = total_ref[:, width : width + 1]
    for ref in got:
        stats = stats + jnp.sum(ref[:, query_width + HD :].astype(F32), axis=1, keepdims=True)
    inverse = lax.rsqrt(stats / features + 1e-05)
    cosine = cos_ref[...]
    sine = sin_ref[...]

    def query_block(at):
        value = total_ref[:, at : at + HD]
        for ref in got:
            value = value + ref[:, at : at + HD].astype(F32)
        value = value * (inverse * scale)
        return (value * cosine + pltpu.roll(value, HD // 2, 1) * sine).astype(BF16)

    sample = lax.broadcasted_iota(jnp.int32, (rows, 1), 0)
    few_rows = SAMP_DEV * GROUP
    pick_row = lax.broadcasted_iota(jnp.int32, (few_rows, GROUP * rows), 0)
    pick_column = lax.broadcasted_iota(jnp.int32, (few_rows, GROUP * rows), 1)
    spot = (pick_row // SAMP_DEV) * rows + pick_row % SAMP_DEV
    picks = [(pick_column == spot + start).astype(F32).astype(BF16) for start in starts]
    column = lanes(rows)

    queries = [
        [query_block((head * GROUP + g) * HD) for g in range(GROUP)] for head in range(heads)
    ]
    packed = [jnp.concatenate(query, axis=0) for query in queries]
    span = 2 * SAMP_DEV
    mine = pl.ds(pl.multiple_of(query_width + place[4] * HD, HD), HD)
    new = total_ref[:, mine]
    for ref in got:
        new = new + ref[:, query_width : query_width + HD].astype(F32)
    vector_row = lax.broadcasted_iota(jnp.int32, (rows, 1), 0) % span
    new_inverse = jnp.zeros((rows, 1), F32)
    for i in range(span):
        one = jnp.sum(jnp.where(sample == base + i, inverse, 0.0), axis=0, keepdims=True)
        new_inverse = jnp.where(vector_row == i, one, new_inverse)
    new = new * new_inverse
    new = new * new_cos[...] + pltpu.roll(new, HD // 2, 1) * new_sin[...]
    half = rows // 2
    fresh[:rows] = new.astype(BF16)
    fresh[rows:] = jnp.concatenate([new[half:], new[:half]], axis=0).astype(BF16)
    padding = jnp.zeros((LANES - (step + 1) * rows, HD), BF16)
    new_keys = jnp.concatenate([ref[:rows] for ref in (*old, fresh)] + [padding], axis=0)
    new_values = jnp.concatenate([ref[rows:] for ref in (*old, fresh)] + [padding], axis=0)
    line = lax.broadcasted_iota(jnp.int32, (GROUP * rows, LANES), 0) % rows - base
    token = lax.broadcasted_iota(jnp.int32, (GROUP * rows, LANES), 1)
    new_scores = [
        jnp.where(
            (token < (step + 1) * rows) & (token % rows == line + head * span)
            & (line >= 0) & (line < span),
            against(packed[head], new_keys),
            -jnp.inf,
        )
        for head in range(heads)
    ]
    few = [
        [jnp.dot(pick, packed[head], preferred_element_type=F32).astype(BF16) for pick in picks]
        for head in range(heads)
    ]
    slots, page = own_suffix.shape[1], own_suffix.shape[3]
    length = own_prefix.shape[2]
    chunk = min(2048, length)
    pieces_of = [(src, at) for src in range(2) for at in range(0, length, chunk)]

    def pool(kind, src, head):
        return suffix[src][kind, :, head].reshape(slots * page, HD)

    near_scores = [[None] * 2 for _ in range(heads)]
    far_scores = [[None] * len(pieces_of) for _ in range(heads)]
    for src in range(2):
        if src == 1:
            for copy in waits[:2]:
                copy.wait()
        for head in range(heads):
            near_scores[head][src] = against(few[head][src], pool(0, src, head)) + bias_ref[src]
            for n, (whose, at) in enumerate(pieces_of):
                if whose == src:
                    far_scores[head][n] = against(
                        packed[head], prefix[src][0, head, at : at + chunk]
                    )
    near_tops = [[row_max([score]) for score in scores] for scores in near_scores]
    for head in range(heads):
        far_scores[head].append(new_scores[head])
    far_tops = [row_max(scores) for scores in far_scores]
    for copy in waits[2:]:
        copy.wait()
    near = [
        [
            weigh([near_scores[head][src]], near_tops[head][src], [pool(1, src, head)])
            for src in range(2)
        ]
        for head in range(heads)
    ]

    tops = jnp.zeros((rows, LANES), F32)
    totals = jnp.zeros((rows, LANES), F32)
    for head in range(heads):
        far_total, far_acc = weigh(
            far_scores[head],
            far_tops[head],
            [prefix[src][1, head, at : at + chunk] for src, at in pieces_of] + [new_values],
        )
        for g in range(GROUP):
            part = slice(g * rows, (g + 1) * rows)
            far_top = far_tops[head][part]
            near_top = jnp.full((rows, 1), -1e30, F32)
            total = jnp.zeros((rows, 1), F32)
            acc = jnp.zeros((rows, HD), F32)
            for src in range(2):
                for j in range(SAMP_DEV):
                    line = slice(g * SAMP_DEV + j, g * SAMP_DEV + j + 1)
                    here = sample == starts[src] + j
                    near_top = jnp.where(here, near_tops[head][src][line], near_top)
                    total = jnp.where(here, near[head][src][0][line], total)
                    acc = jnp.where(here, near[head][src][1][line], acc)
            top = jnp.maximum(far_top, near_top)
            far_weight = jnp.exp2(far_top - top)
            near_weight = jnp.exp2(near_top - top)
            total = total * near_weight + far_total[part] * far_weight
            acc = acc * near_weight + far_acc[part] * far_weight
            index = head * GROUP + g
            sent[:, index * HD : (index + 1) * HD] = acc.astype(BF16)
            tops = jnp.where(column == index, top, tops)
            totals = jnp.where(column == index, total, totals)
    many = heads * GROUP
    stat[:, :LANES] = tops
    stat[:, LANES:] = totals
    parts = [*pieces(tops), *pieces(totals)]
    packed_stats = parts[0]
    for n, part in enumerate(parts[1:], 1):
        packed_stats = packed_stats + pltpu.roll(part, n * many, 1)
    sent[:, many * HD :] = packed_stats.astype(BF16)


def attend(features, step, total, got, tables, caches, old):
    rows = total.shape[0]
    own, far = caches
    heads = own[0].shape[1]
    if step == 0:
        inputs = [resident(array) for array in own] + [in_hbm(array) for array in far]
        specs = [VMEM_SPEC] * 2 + [HBM_SPEC] * 4
        out_shape = [pltpu.VMEM(part.shape, BF16) for part in own]
        scratch = [pltpu.SemaphoreType.DMA((4,))]
    else:
        inputs = [resident(array) for array in (*own, *far)]
        specs = [VMEM_SPEC] * 4
        out_shape, scratch = [], []
    small = [total, *got, *tables]
    last = step == STEPS - 1
    if last:
        scratch = [pltpu.VMEM((2 * rows, HD), BF16)]
    else:
        out_shape = [jax.ShapeDtypeStruct((2 * rows, HD), BF16)] + out_shape
    return pl.pallas_call(
        functools.partial(attend_kernel, features, step, len(got)),
        out_shape=[
            jax.ShapeDtypeStruct((rows, heads * GROUP * HD + LANES), BF16),
            jax.ShapeDtypeStruct((rows, 2 * LANES), F32),
            *out_shape,
        ],
        in_specs=[VMEM_SPEC] * len(small) + specs + [VMEM_SPEC] * len(old),
        out_specs=[VMEM_SPEC] * (2 + len(out_shape)),
        scratch_shapes=scratch,
        compiler_params=LARGE_PARAMS,
    )(*small, *inputs, *old)


def merge_kernel(own, stat, *refs):
    got, out = refs[:-1], refs[-1]
    many = out.shape[1] // HD
    tops, totals = [stat[:, :LANES]], [stat[:, LANES:]]
    for ref in got:
        packed = ref[:, many * HD :].astype(F32)
        turns = [packed] + [pltpu.roll(packed, LANES - n * many, 1) for n in range(1, 6)]
        tops.append(turns[0] + turns[1] + turns[2])
        totals.append(turns[3] + turns[4] + turns[5])
    used = lanes(own.shape[0]) < many
    tops = [jnp.where(used, top, 0.0) for top in tops]
    top = functools.reduce(jnp.maximum, tops)
    weights = [jnp.exp2(each - top) for each in tops]
    total = functools.reduce(jnp.add, [w * t for w, t in zip(weights, totals)])
    share = 1.0 / jnp.where(used, total, 1.0)
    weights = [weight * share for weight in weights]
    for index in range(many):
        part = slice(index * HD, (index + 1) * HD)
        value = own[:, part].astype(F32) * weights[0][:, index : index + 1]
        for ref, weight in zip(got, weights[1:]):
            value = value + ref[:, part].astype(F32) * weight[:, index : index + 1]
        out[:, part] = value.astype(BF16)


def merge(own, stat, got):
    return pl.pallas_call(
        merge_kernel,
        out_shape=jax.ShapeDtypeStruct((own.shape[0], own.shape[1] - LANES), BF16),
        in_specs=[VMEM_SPEC] * (2 + len(got)),
        out_specs=VMEM_SPEC,
        compiler_params=PARAMS,
    )(own, stat, *got)


def near_output_kernel(mine, weight, out):
    place = whereabouts()
    half = mine.shape[1]
    rows = pl.ds(pl.multiple_of(place[0] * half, half), half)
    out[...] = jnp.dot(mine[...], weight[rows], preferred_element_type=F32)


def far_output_kernel(other, weight, near, out):
    place = whereabouts()
    half = other.shape[1]
    rows = pl.ds(pl.multiple_of((1 - place[0]) * half, half), half)
    total = near[...] + jnp.dot(other[...], weight[rows], preferred_element_type=F32)
    out[...] = total.astype(BF16)


def output(mine, weight):
    other = swapped(mine, "side")
    shape = (mine.shape[0], weight.shape[1])
    near = pl.pallas_call(
        near_output_kernel,
        out_shape=jax.ShapeDtypeStruct(shape, F32),
        in_specs=[VMEM_SPEC] * 2,
        out_specs=VMEM_SPEC,
        compiler_params=PARAMS,
        cost_estimate=COST,
    )(mine, resident(weight))
    return pl.pallas_call(
        far_output_kernel,
        out_shape=jax.ShapeDtypeStruct(shape, BF16),
        in_specs=[VMEM_SPEC] * 3,
        out_specs=VMEM_SPEC,
        compiler_params=PARAMS,
    )(other, resident(weight), near)


def swapped(array, axis):
    return lax.ppermute(array, axis, [(0, 1), (1, 0)])


def from_others(arrays, axis):
    size = lax.axis_size(axis)
    return [
        lax.ppermute(array, axis, [(i, (i + hop) % size) for i in range(size)])
        for hop, array in enumerate(arrays, 1)
    ]


def rotations(lengths, base):
    half = HD // 2
    freq = 500000.0 ** (-(jnp.arange(half, dtype=F32) * 2.0 / HD))
    position = (
        PREFIX + lengths[None, :] + jnp.arange(STEPS, dtype=jnp.int32)[:, None]
    ).astype(F32)
    angle = position[..., None] * freq
    cosine, sine = jnp.cos(angle), jnp.sin(angle)
    cosine = jnp.concatenate([cosine, cosine], axis=-1)
    sine = jnp.concatenate([-sine, sine], axis=-1)
    span = 2 * SAMP_DEV
    vectors = lengths.shape[0] // span
    new_cosine = lax.dynamic_slice_in_dim(cosine, base, span, 1)
    new_sine = lax.dynamic_slice_in_dim(sine, base, span, 1)
    turns = vectors // 2
    new_cosine = jnp.concatenate(
        [new_cosine] * turns + [jnp.ones_like(new_cosine)] * turns, axis=1
    )
    new_sine = jnp.concatenate([new_sine] * turns + [jnp.zeros_like(new_sine)] * turns, axis=1)
    return cosine, sine, new_cosine, new_sine


def local_split(
    hidden,
    gain,
    w_query,
    w_key,
    w_value,
    w_out,
    prefix_keys,
    prefix_values,
    suffix_keys,
    suffix_values,
    suffix_lengths,
    page_table,
):
    features = hidden.shape[1] * lax.axis_size(("seq", "side"))
    base = lax.axis_index("seq") * (2 * SAMP_DEV)
    pools = (prefix_keys, prefix_values, suffix_keys, suffix_values)
    weights = (w_query, w_key, w_value)
    far = [swapped(pool, "side") for pool in pools[2:]]
    gain_row = gain[None, :]
    query_width = w_query.shape[1] // 2
    hops = lax.axis_size("seq") - 1

    state = hidden
    update = jnp.zeros(hidden.shape, F32)
    rest = ()
    old = []
    for step in range(STEPS):
        if rest:
            give, scaled, state, update = give_project(state, gain_row, weights, rest)
            got_sum = swapped(give, "side")
            keep = keep_project(scaled, give, weights)
            total, *sent = pair_sum(keep, got_sum, query_width, hops)
        else:
            keep, give = first_project(state, gain_row, weights)
            got_sum = swapped(give, "side")
            got_sum, *given = lax.optimization_barrier((got_sum, *far, *pools[:2]))
            far = [swapped(pool, "side") for pool in given[2:]] + given[:2]
            total, *sent = pair_sum(keep, got_sum, query_width, hops)
            *sent, lengths, table = lax.optimization_barrier(
                (*sent, suffix_lengths, page_table)
            )
            turning = rotations(lengths, base)
            *own, out_weight, bias = load_caches(lengths, table, pools, w_out, sent[0])
        got = from_others(sent, "seq")
        tables = (*[each[step] for each in turning], bias)
        sent, stat, *kept = attend(
            features, step, total, got, tables, (own, far), old
        )
        far = kept[1:] or far
        got = from_others([sent] * hops, "seq")
        if not rest:
            weights = load(weights, stat)
            got, weights = lax.optimization_barrier((got, weights))
        old += kept[:1]
        mixed = merge(sent, stat, got)
        part = output(mixed, out_weight)
        rest = (update, part, swapped(part, "head"))
    delta = rest[1].astype(F32) + rest[2].astype(F32)
    return ((state.astype(F32) + delta).astype(BF16), update + delta)


def fits(mesh, args):
    heads = args[4].shape[1] // HD // mesh.shape["head"]
    return (
        mesh.shape["head"] == 2
        and mesh.shape["side"] == 2
        and heads % 2 == 0
        and args[6].shape[0] == mesh.shape["groups"]
        and heads // 2 * GROUP * 6 <= LANES
        and mesh.shape["seq"] == heads
        and args[0].shape[0] // mesh.shape["groups"] * STEPS <= LANES
    )


def solution(mesh):
    placed = (
        P("groups", ("seq", "side")),
        P(("seq", "side")),
        P(("seq", "side"), "head"),
        P(("seq", "side"), "head"),
        P(("seq", "side"), "head"),
        P("head", ("seq", "side")),
        P("groups", "head", ("seq", "side"), None),
        P("groups", "head", ("seq", "side"), None),
        P(("groups", "seq", "side"), "head", None, None),
        P(("groups", "seq", "side"), "head", None, None),
        P("groups"),
        P("groups", None),
    )

    def whole(*args):
        return jax.shard_map(
            local_split if fits(mesh, args) else local_any,
            mesh=mesh,
            in_specs=placed,
            out_specs=(P("groups", ("seq", "side")), P("groups", ("seq", "side"))),
            check_vma=False,
        )(*args)

    return whole
```

```python
import functools
import math

import jax
import jax.numpy as jnp
from jax import lax
from jax.experimental import pallas as pl
from jax.experimental.pallas import tpu as pltpu
from jax.sharding import PartitionSpec as P

D = 8192
HD = 128
GROUP = 8
SAMP_DEV = 2
PREFIX = 32768
STEPS = 3


def combined_all(array, axis, combine):
    everything = jax.tree.map(lambda part: lax.all_gather(part, axis), array)
    first = jax.tree.map(lambda part: part[0], everything)

    def lap(k, so_far):
        return combine(so_far, jax.tree.map(lambda part: part[k], everything))

    return lax.fori_loop(1, lax.axis_size(axis), lap, first)


def rotate(vectors, position):
    half = vectors.shape[-1] // 2
    freq = 500000.0 ** (-(jnp.arange(half, dtype=jnp.float32) * 2.0 / vectors.shape[-1]))
    angle = position[..., None] * freq
    cosine = jnp.cos(angle)
    sine = jnp.sin(angle)
    lower = vectors[..., :half]
    upper = vectors[..., half:]
    return jnp.concatenate([lower * cosine - upper * sine, upper * cosine + lower * sine], axis=-1)


def combine(first, second):
    acc_a, top_a, total_a = first
    acc_b, top_b, total_b = second
    top = jnp.maximum(top_a, top_b)
    weight_a = jnp.exp(top_a - top)
    weight_b = jnp.exp(top_b - top)
    return (
        acc_a * weight_a[..., None] + acc_b * weight_b[..., None],
        top,
        total_a * weight_a + total_b * weight_b,
    )


def local_any(
    hidden,
    gain,
    w_query,
    w_key,
    w_value,
    w_out,
    prefix_keys,
    prefix_values,
    suffix_keys,
    suffix_values,
    suffix_lengths,
    page_table,
):
    samples = hidden.shape[0]
    kv_local = w_key.shape[1] // HD
    query_width = kv_local * GROUP * HD
    key_width = kv_local * HD
    prompts = prefix_keys.shape[0]
    scale = 1.0 / math.sqrt(HD)
    rank = lax.axis_index(("seq", "side"))
    w_proj = jnp.concatenate([w_query, w_key, w_value], axis=1)
    pool_keys, pool_values = (suffix_keys, suffix_values)
    start = jnp.bitwise_xor(rank, 1) * SAMP_DEV
    table_rows = lax.dynamic_slice_in_dim(page_table, start, SAMP_DEV, 0)
    page_keys = pool_keys[table_rows]
    page_values = pool_values[table_rows]
    length_rows = lax.dynamic_slice_in_dim(suffix_lengths, start, SAMP_DEV, 0)
    page_count = page_keys.shape[1]
    page_size = page_keys.shape[3]
    suffix_span = page_count * page_size
    live = (jnp.arange(suffix_span, dtype=jnp.int32)[None, :] < length_rows[:, None])[
        :, None, None, :
    ]
    state = hidden
    update = jnp.zeros(hidden.shape, jnp.float32)
    new_keys = []
    new_values = []
    for step in range(STEPS):
        wide = state.astype(jnp.float32)
        scaled = (wide * gain).astype(jnp.bfloat16)
        partial_value = jnp.dot(scaled, w_proj, preferred_element_type=jnp.float32)
        squares = jnp.sum(wide * wide, axis=1)
        proj, total_sq = lax.psum((partial_value, squares), ("seq", "side"))
        inverse = lax.rsqrt(total_sq / D + 1e-05)[:, None]
        position = (PREFIX + suffix_lengths + step).astype(jnp.float32)
        query = rotate(
            (proj[:, :query_width] * inverse).reshape(samples, kv_local, GROUP, HD),
            position[:, None, None],
        ).astype(jnp.bfloat16)
        new_keys.append(
            rotate(
                (proj[:, query_width : query_width + key_width] * inverse).reshape(
                    samples, kv_local, HD
                ),
                position[:, None],
            ).astype(jnp.bfloat16)
        )
        new_values.append(
            (proj[:, query_width + key_width :] * inverse)
            .reshape(samples, kv_local, HD)
            .astype(jnp.bfloat16)
        )
        stacked_keys = jnp.stack(new_keys, axis=1)
        stacked_values = jnp.stack(new_values, axis=1)
        grouped = query.reshape(prompts, samples // prompts, kv_local, GROUP, HD)
        scores = (
            jnp.einsum(
                "pgkhd,pkld->pgkhl", grouped, prefix_keys, preferred_element_type=jnp.float32
            )
            * scale
        )
        top = jnp.max(scores, axis=-1)
        expo = jnp.exp(scores - top[..., None])
        total = jnp.sum(expo, axis=-1)
        acc = jnp.einsum(
            "pgkhl,pkld->pgkhd",
            expo.astype(jnp.bfloat16),
            prefix_values,
            preferred_element_type=jnp.float32,
        )
        acc = acc.reshape(samples, kv_local, GROUP, HD)
        top = top.reshape(samples, kv_local, GROUP)
        total = total.reshape(samples, kv_local, GROUP)
        own_query = lax.dynamic_slice_in_dim(query, start, SAMP_DEV, 0)
        own_keys = lax.dynamic_slice_in_dim(stacked_keys, start, SAMP_DEV, 0)
        own_values = lax.dynamic_slice_in_dim(stacked_values, start, SAMP_DEV, 0)
        suffix_scores = jnp.einsum(
            "skhd,spkjd->skhpj", own_query, page_keys, preferred_element_type=jnp.float32
        )
        suffix_scores = suffix_scores.reshape(SAMP_DEV, kv_local, GROUP, suffix_span) * scale
        suffix_scores = jnp.where(live, suffix_scores, -jnp.inf)
        fresh_scores = (
            jnp.einsum("skhd,sukd->skhu", own_query, own_keys, preferred_element_type=jnp.float32)
            * scale
        )
        peak = jnp.maximum(jnp.max(suffix_scores, axis=-1), jnp.max(fresh_scores, axis=-1))
        suffix_expo = jnp.exp(suffix_scores - peak[..., None])
        fresh_expo = jnp.exp(fresh_scores - peak[..., None])
        near_total = jnp.sum(suffix_expo, axis=-1) + jnp.sum(fresh_expo, axis=-1)
        near_acc = jnp.einsum(
            "skhpj,spkjd->skhd",
            suffix_expo.astype(jnp.bfloat16).reshape(
                SAMP_DEV, kv_local, GROUP, page_count, page_size
            ),
            page_values,
            preferred_element_type=jnp.float32,
        )
        near_acc = near_acc + jnp.einsum(
            "skhu,sukd->skhd",
            fresh_expo.astype(jnp.bfloat16),
            own_values,
            preferred_element_type=jnp.float32,
        )
        rows_now = (
            lax.dynamic_slice_in_dim(acc, start, SAMP_DEV, 0),
            lax.dynamic_slice_in_dim(top, start, SAMP_DEV, 0),
            lax.dynamic_slice_in_dim(total, start, SAMP_DEV, 0),
        )
        joined = combine(rows_now, (near_acc, peak, near_total))
        acc = lax.dynamic_update_slice_in_dim(acc, joined[0], start, 0)
        top = lax.dynamic_update_slice_in_dim(top, joined[1], start, 0)
        total = lax.dynamic_update_slice_in_dim(total, joined[2], start, 0)
        acc, top, total = combined_all((acc, top, total), ("seq", "side"), combine)
        mixed = (acc / total[..., None]).astype(jnp.bfloat16).reshape(samples, query_width)
        part = jnp.dot(mixed, w_out, preferred_element_type=jnp.float32)
        delta = lax.psum(part, "head")
        update = update + delta
        state = (wide + delta).astype(jnp.bfloat16)
    return (state, update)


LANES = 128
LOG2E = 1.4426950408889634
BF16 = jnp.bfloat16
F32 = jnp.float32
VMEM_SPEC = pl.BlockSpec(memory_space=pltpu.VMEM)
SMEM_SPEC = pl.BlockSpec(memory_space=pltpu.SMEM)
HBM_SPEC = pl.BlockSpec(memory_space=pltpu.HBM)
PARAMS = pltpu.CompilerParams(vmem_limit_bytes=4 * 1024 * 1024)
LARGE_PARAMS = pltpu.CompilerParams(vmem_limit_bytes=13 * 1024 * 1024)
COST = pl.CostEstimate(flops=1 << 28, bytes_accessed=1 << 22, transcendentals=0)


def resident(array):
    return pltpu.with_memory_space_constraint(array, pltpu.VMEM)


def in_hbm(array):
    return pltpu.with_memory_space_constraint(array, pltpu.HBM)


def whereabouts():
    seq, side = lax.axis_index("seq"), lax.axis_index("side")
    base = seq * (2 * SAMP_DEV)
    return side, base, base + (1 - side) * SAMP_DEV, base + side * SAMP_DEV, seq


def lanes(rows):
    return lax.broadcasted_iota(jnp.int32, (rows, LANES), 1)


def pieces(values):
    high = values.astype(BF16).astype(F32)
    middle = (values - high).astype(BF16).astype(F32)
    return high, middle, values - high - middle


def move(copies):
    for copy in copies:
        copy.start()
    for copy in copies:
        copy.wait()


def copied(pairs, sems):
    copies = [
        pltpu.make_async_copy(source, target, sems.at[n])
        for n, (source, target) in enumerate(pairs)
    ]
    for copy in copies:
        copy.start()
    return copies


def halves(place, pools, prefix, suffix):
    heads = prefix.shape[1]
    part = pl.ds(place[0] * heads, heads)
    pk, pv, sk, sv = pools
    return [
        (sk.at[:, part], suffix.at[0]),
        (pk.at[0, part], prefix.at[0]),
        (sv.at[:, part], suffix.at[1]),
        (pv.at[0] if pv.shape[1] == heads else pv.at[0, part], prefix.at[1]),
    ]


def half_shapes(pools):
    pk, sk = pools[0], pools[2]
    return [
        pltpu.VMEM((2, pk.shape[1] // 2) + pk.shape[2:], pk.dtype),
        pltpu.VMEM((2, sk.shape[0], sk.shape[1] // 2) + sk.shape[2:], sk.dtype),
    ]


def cut_kernel(pool, after, out, held, sems):
    place = whereabouts()
    heads, length = out.shape[1:3]
    parts = [(h, pl.ds(at, length // 2)) for h in range(heads) for at in (0, length // 2)]
    source = pool.at[0, pl.ds((1 - place[0]) * heads, heads)]
    reads = copied([(source.at[part], held.at[part]) for part in parts], sems.at[0])
    writes = []
    for n, (read, part) in enumerate(zip(reads, parts)):
        read.wait()
        writes.append(pltpu.make_async_copy(held.at[part], out.at[0].at[part], sems.at[1, n]))
        writes[-1].start()
    for write in writes:
        write.wait()


def cut(pool, after):
    shape = (pool.shape[0], pool.shape[1] // 2) + pool.shape[2:]
    return pl.pallas_call(
        cut_kernel,
        out_shape=jax.ShapeDtypeStruct(shape, pool.dtype),
        in_specs=[HBM_SPEC, VMEM_SPEC],
        out_specs=HBM_SPEC,
        scratch_shapes=[
            pltpu.VMEM(shape[1:], pool.dtype),
            pltpu.SemaphoreType.DMA((2, 2 * shape[1])),
        ],
        compiler_params=PARAMS,
        cost_estimate=pl.CostEstimate(flops=0, bytes_accessed=1 << 23, transcendentals=0),
    )(in_hbm(pool), after)


def live_bias(place, lengths, table, bias):
    pages = table.shape[1]
    page = bias.shape[2] // (SAMP_DEV * pages)
    row = lax.broadcasted_iota(jnp.int32, (bias.shape[1], page), 0)
    column = lax.broadcasted_iota(jnp.int32, (bias.shape[1], page), 1)
    for pool in range(2):
        for j in range(SAMP_DEV):
            sample = place[2 + pool] + j
            mine = row % SAMP_DEV == j
            for p in range(pages):
                live = mine & (column < lengths[sample] - p * page)
                spot = pl.ds(pl.multiple_of(table[sample, p] * page, page), page)
                bias[pool, :, spot] = jnp.where(live, 0.0, -jnp.inf)


def load_caches_kernel(
    lengths, table, pk, pv, sk, sv, w_out, after, prefix, suffix, kept_out, bias, sems
):
    place = whereabouts()
    pairs = halves(place, (pk, pv, sk, sv), prefix, suffix) + [(w_out, kept_out)]
    copies = copied(pairs, sems)
    live_bias(place, lengths, table, bias)
    for copy in copies:
        copy.wait()


def load_caches(lengths, table, pools, w_out, after):
    page = pools[2].shape[2]
    tokens = SAMP_DEV * table.shape[1] * page
    sources = [in_hbm(array) for array in (*pools, w_out)]
    return pl.pallas_call(
        load_caches_kernel,
        out_shape=half_shapes(pools)
        + [
            pltpu.VMEM(w_out.shape, w_out.dtype),
            jax.ShapeDtypeStruct((2, SAMP_DEV * GROUP, tokens), F32),
        ],
        in_specs=[SMEM_SPEC] * 2 + [HBM_SPEC] * 5 + [VMEM_SPEC],
        out_specs=[VMEM_SPEC] * 4,
        scratch_shapes=[pltpu.SemaphoreType.DMA((5,))],
        compiler_params=PARAMS,
        cost_estimate=pl.CostEstimate(flops=0, bytes_accessed=1 << 25, transcendentals=0),
    )(lengths, table, *sources, after)


def load_kernel(*refs):
    count = len(refs) // 2 - 1
    for copy in copied(zip(refs[:count], refs[count + 1 : -1]), refs[-1]):
        copy.wait()


def load(weights, after):
    return pl.pallas_call(
        load_kernel,
        out_shape=[pltpu.VMEM(w.shape, w.dtype) for w in weights],
        in_specs=[HBM_SPEC] * len(weights) + [VMEM_SPEC],
        out_specs=[VMEM_SPEC] * len(weights),
        scratch_shapes=[pltpu.SemaphoreType.DMA((len(weights),))],
        compiler_params=PARAMS,
        cost_estimate=pl.CostEstimate(flops=0, bytes_accessed=1 << 25, transcendentals=0),
    )(*[in_hbm(weight) for weight in weights], after)


def column_tiles(place, weights, who):
    tiles, at = [], 0
    for index, weight in enumerate(weights):
        half = weight.shape[1] // 2
        tile = min(1024, half)
        for begin in range(0, half, tile):
            columns = pl.ds(pl.multiple_of(who * half + begin, tile), tile)
            tiles.append((index, columns, slice(at + begin, at + begin + tile)))
        at += half
    return tiles


def project_half(scaled, weights, tiles, out, arrive=lambda: None):
    vectors, width = [], 0
    for index, columns, to in tiles:
        arrive()
        part = jnp.dot(scaled, weights[index][:, columns], preferred_element_type=F32)
        if index == 0:
            out[:, to] = part
            width = to.stop
        else:
            vectors += [part[:, at : at + HD] for at in range(0, part.shape[1], HD)]
    span = 2 * SAMP_DEV
    for chip in range(scaled.shape[0] // span):
        part = slice(chip * span, (chip + 1) * span)
        out[:, width + chip * HD : width + (chip + 1) * HD] = jnp.concatenate(
            [vector[part] for vector in vectors], axis=0
        )


def first_project_kernel(*refs):
    place = whereabouts()
    sources, (keep, give, *buffers, sems) = refs[:5], refs[5:]
    weights, (x_ref, gain) = buffers[:3], buffers[3:]
    outs = ((give, 1 - place[0]), (keep, place[0]))
    halves_of = [(out, column_tiles(place, weights, who)) for out, who in outs]
    pairs = list(zip(sources[3:], buffers[3:]))
    for _, tiles in halves_of:
        for index, columns, _ in tiles:
            pairs.append((sources[index].at[:, columns], weights[index].at[:, columns]))
    copies = copied(pairs, sems)
    copies[0].wait()
    copies[1].wait()
    wide = x_ref[...].astype(F32)
    scaled = (wide * gain[...]).astype(BF16)
    squares = jnp.sum(wide * wide, axis=1, keepdims=True)
    column = lanes(wide.shape[0])
    for out in (give, keep):
        out[:, out.shape[1] - LANES :] = jnp.where(column == 0, squares, 0.0)
    waiting = iter(copies[2:])
    for out, tiles in halves_of:
        project_half(scaled, weights, tiles, out, lambda: next(waiting).wait())


def first_project(x, gain, weights):
    rows = x.shape[0]
    width = sum(w.shape[1] for w in weights) // 2 + LANES
    sources = [in_hbm(array) for array in (*weights, x, gain)]
    count = 2 + 2 * sum(max(1, w.shape[1] // 2048) for w in weights)
    return pl.pallas_call(
        first_project_kernel,
        out_shape=[jax.ShapeDtypeStruct((rows, width), F32)] * 2,
        in_specs=[HBM_SPEC] * 5,
        out_specs=[VMEM_SPEC] * 2,
        scratch_shapes=[pltpu.VMEM(array.shape, array.dtype) for array in sources]
        + [pltpu.SemaphoreType.DMA((count,))],
        compiler_params=LARGE_PARAMS,
    )(*sources)


def give_kernel(x_ref, gain, sum_ref, mine, other, *refs):
    place = whereabouts()
    weights, (give, scaled_ref, new_x, new_sum) = refs[:3], refs[3:]
    delta = mine[...].astype(F32) + other[...].astype(F32)
    new_sum[...] = sum_ref[...] + delta
    state = (x_ref[...].astype(F32) + delta).astype(BF16)
    new_x[...] = state
    wide = state.astype(F32)
    scaled = (wide * gain[...]).astype(BF16)
    scaled_ref[...] = scaled
    squares = jnp.sum(wide * wide, axis=1, keepdims=True)
    column = lanes(wide.shape[0])
    give[:, give.shape[1] - LANES :] = jnp.where(column == 0, squares, 0.0)
    project_half(scaled, weights, column_tiles(place, weights, 1 - place[0]), give)


def give_project(x, gain, weights, rest):
    rows = x.shape[0]
    width = sum(w.shape[1] for w in weights) // 2 + LANES
    return pl.pallas_call(
        give_kernel,
        out_shape=[
            jax.ShapeDtypeStruct((rows, width), F32),
            jax.ShapeDtypeStruct(x.shape, BF16),
            jax.ShapeDtypeStruct(x.shape, BF16),
            jax.ShapeDtypeStruct(x.shape, F32),
        ],
        in_specs=[VMEM_SPEC] * 8,
        out_specs=[VMEM_SPEC] * 4,
        compiler_params=PARAMS,
        cost_estimate=COST,
    )(x, gain, *rest, *[resident(weight) for weight in weights])


def keep_kernel(scaled_ref, give, *refs):
    place = whereabouts()
    weights, keep = refs[:3], refs[3]
    scaled = scaled_ref[...]
    main = keep.shape[1] - LANES
    keep[:, main:] = give[:, main:]
    project_half(scaled, weights, column_tiles(place, weights, place[0]), keep)


def keep_project(scaled, give, weights):
    return pl.pallas_call(
        keep_kernel,
        out_shape=jax.ShapeDtypeStruct(give.shape, F32),
        in_specs=[VMEM_SPEC] * 5,
        out_specs=VMEM_SPEC,
        compiler_params=PARAMS,
        cost_estimate=COST,
    )(scaled, give, *[resident(weight) for weight in weights])


def pair_sum_kernel(query_width, keep, got, total, *sent):
    place = whereabouts()
    both = keep[...] + got[...]
    total[...] = both
    rows = both.shape[0]
    main = both.shape[1] - LANES
    chips = (main - query_width) // HD
    column = lanes(rows)
    high, middle, low = pieces(both[:, main : main + 1])
    stats = jnp.where(
        column == 0, high, jnp.where(column == 1, middle, jnp.where(column == 2, low, 0.0))
    ).astype(BF16)
    query = both[:, :query_width].astype(BF16)
    for hop, out in enumerate(sent, 1):
        chip = lax.rem(place[4] + hop, chips)
        block = pl.ds(pl.multiple_of(query_width + chip * HD, HD), HD)
        out[:, :query_width] = query
        out[:, query_width : query_width + HD] = total[:, block].astype(BF16)
        out[:, query_width + HD :] = stats


def pair_sum(keep, got, query_width, hops):
    rows = keep.shape[0]
    sent = jax.ShapeDtypeStruct((rows, query_width + HD + LANES), BF16)
    return pl.pallas_call(
        functools.partial(pair_sum_kernel, query_width),
        out_shape=[jax.ShapeDtypeStruct(keep.shape, F32)] + [sent] * hops,
        in_specs=[VMEM_SPEC] * 2,
        out_specs=[VMEM_SPEC] * (1 + hops),
        compiler_params=PARAMS,
    )(keep, got)


def lane_fold(fold, array):
    parts = [array[:, at : at + LANES] for at in range(0, array.shape[1], LANES)]
    return functools.reduce(fold, parts)


def row_max(arrays):
    folded = [lane_fold(jnp.maximum, array) for array in arrays]
    return jnp.max(functools.reduce(jnp.maximum, folded), axis=1, keepdims=True)


def against(rows, keys):
    return lax.dot_general(
        rows, keys, (((1,), (1,)), ((), ())), preferred_element_type=F32
    )


def weigh(scores, top, values):
    terms = [
        jnp.dot(
            jnp.exp2(score - top).astype(BF16),
            jnp.concatenate([value, jnp.ones_like(value)], axis=1),
            preferred_element_type=F32,
        )
        for score, value in zip(scores, values)
    ]
    both = functools.reduce(jnp.add, terms)
    return both[:, HD : HD + 1], both[:, :HD]


def attend_kernel(features, step, others, *refs):
    place = whereabouts()
    total_ref = refs[0]
    got = refs[1 : 1 + others]
    cos_ref, sin_ref, new_cos, new_sin, bias_ref = refs[1 + others : 6 + others]
    refs = refs[2:]
    own_prefix, own_suffix, *far = refs[4 + others : (10 if step == 0 else 8) + others]
    refs = refs[(10 if step == 0 else 8) + others :]
    old, (sent, stat, fresh) = refs[:step], refs[step : 3 + step]
    heads = own_prefix.shape[1]
    waits = []
    if step == 0:
        got_prefix, got_suffix, sems = refs[3:]
        waits = copied(halves(place, far, got_prefix, got_suffix), sems)
    else:
        got_prefix, got_suffix = far
    prefix = (own_prefix, got_prefix)
    suffix = (own_suffix, got_suffix)
    rows = total_ref.shape[0]
    width = total_ref.shape[1] - LANES
    query_width = width - 2 * heads * HD
    base, starts = place[1], (place[2], place[3])
    scale = LOG2E / math.sqrt(HD)

    stats = total_ref[:, width : width + 1]
    for ref in got:
        stats = stats + jnp.sum(ref[:, query_width + HD :].astype(F32), axis=1, keepdims=True)
    inverse = lax.rsqrt(stats / features + 1e-05)
    cosine = cos_ref[...]
    sine = sin_ref[...]

    def query_block(at):
        value = total_ref[:, at : at + HD]
        for ref in got:
            value = value + ref[:, at : at + HD].astype(F32)
        value = value * (inverse * scale)
        return (value * cosine + pltpu.roll(value, HD // 2, 1) * sine).astype(BF16)

    sample = lax.broadcasted_iota(jnp.int32, (rows, 1), 0)
    few_rows = SAMP_DEV * GROUP
    pick_row = lax.broadcasted_iota(jnp.int32, (few_rows, GROUP * rows), 0)
    pick_column = lax.broadcasted_iota(jnp.int32, (few_rows, GROUP * rows), 1)
    spot = (pick_row // SAMP_DEV) * rows + pick_row % SAMP_DEV
    picks = [(pick_column == spot + start).astype(F32).astype(BF16) for start in starts]
    column = lanes(rows)

    queries = [
        [query_block((head * GROUP + g) * HD) for g in range(GROUP)] for head in range(heads)
    ]
    packed = [jnp.concatenate(query, axis=0) for query in queries]
    span = 2 * SAMP_DEV
    mine = pl.ds(pl.multiple_of(query_width + place[4] * HD, HD), HD)
    new = total_ref[:, mine]
    for ref in got:
        new = new + ref[:, query_width : query_width + HD].astype(F32)
    vector_row = lax.broadcasted_iota(jnp.int32, (rows, 1), 0) % span
    new_inverse = jnp.zeros((rows, 1), F32)
    for i in range(span):
        one = jnp.sum(jnp.where(sample == base + i, inverse, 0.0), axis=0, keepdims=True)
        new_inverse = jnp.where(vector_row == i, one, new_inverse)
    new = new * new_inverse
    new = new * new_cos[...] + pltpu.roll(new, HD // 2, 1) * new_sin[...]
    half = rows // 2
    fresh[:rows] = new.astype(BF16)
    fresh[rows:] = jnp.concatenate([new[half:], new[:half]], axis=0).astype(BF16)
    padding = jnp.zeros((LANES - (step + 1) * rows, HD), BF16)
    new_keys = jnp.concatenate([ref[:rows] for ref in (*old, fresh)] + [padding], axis=0)
    new_values = jnp.concatenate([ref[rows:] for ref in (*old, fresh)] + [padding], axis=0)
    line = lax.broadcasted_iota(jnp.int32, (GROUP * rows, LANES), 0) % rows - base
    token = lax.broadcasted_iota(jnp.int32, (GROUP * rows, LANES), 1)
    new_scores = [
        jnp.where(
            (token < (step + 1) * rows) & (token % rows == line + head * span)
            & (line >= 0) & (line < span),
            against(packed[head], new_keys),
            -jnp.inf,
        )
        for head in range(heads)
    ]
    few = [
        [jnp.dot(pick, packed[head], preferred_element_type=F32).astype(BF16) for pick in picks]
        for head in range(heads)
    ]
    slots, page = own_suffix.shape[1], own_suffix.shape[3]
    length = own_prefix.shape[2]
    chunk = min(2048, length)
    pieces_of = [(src, at) for src in range(2) for at in range(0, length, chunk)]

    def pool(kind, src, head):
        return suffix[src][kind, :, head].reshape(slots * page, HD)

    near_scores = [[None] * 2 for _ in range(heads)]
    far_scores = [[None] * len(pieces_of) for _ in range(heads)]
    for src in range(2):
        if src == 1:
            for copy in waits[:2]:
                copy.wait()
        for head in range(heads):
            near_scores[head][src] = against(few[head][src], pool(0, src, head)) + bias_ref[src]
            for n, (whose, at) in enumerate(pieces_of):
                if whose == src:
                    far_scores[head][n] = against(
                        packed[head], prefix[src][0, head, at : at + chunk]
                    )
    near_tops = [[row_max([score]) for score in scores] for scores in near_scores]
    for head in range(heads):
        far_scores[head].append(new_scores[head])
    far_tops = [row_max(scores) for scores in far_scores]
    for copy in waits[2:]:
        copy.wait()
    near = [
        [
            weigh([near_scores[head][src]], near_tops[head][src], [pool(1, src, head)])
            for src in range(2)
        ]
        for head in range(heads)
    ]

    tops = jnp.zeros((rows, LANES), F32)
    totals = jnp.zeros((rows, LANES), F32)
    for head in range(heads):
        far_total, far_acc = weigh(
            far_scores[head],
            far_tops[head],
            [prefix[src][1, head, at : at + chunk] for src, at in pieces_of] + [new_values],
        )
        for g in range(GROUP):
            part = slice(g * rows, (g + 1) * rows)
            far_top = far_tops[head][part]
            near_top = jnp.full((rows, 1), -1e30, F32)
            total = jnp.zeros((rows, 1), F32)
            acc = jnp.zeros((rows, HD), F32)
            for src in range(2):
                for j in range(SAMP_DEV):
                    line = slice(g * SAMP_DEV + j, g * SAMP_DEV + j + 1)
                    here = sample == starts[src] + j
                    near_top = jnp.where(here, near_tops[head][src][line], near_top)
                    total = jnp.where(here, near[head][src][0][line], total)
                    acc = jnp.where(here, near[head][src][1][line], acc)
            top = jnp.maximum(far_top, near_top)
            far_weight = jnp.exp2(far_top - top)
            near_weight = jnp.exp2(near_top - top)
            total = total * near_weight + far_total[part] * far_weight
            acc = acc * near_weight + far_acc[part] * far_weight
            index = head * GROUP + g
            sent[:, index * HD : (index + 1) * HD] = acc.astype(BF16)
            tops = jnp.where(column == index, top, tops)
            totals = jnp.where(column == index, total, totals)
    many = heads * GROUP
    stat[:, :LANES] = tops
    stat[:, LANES:] = totals
    parts = [*pieces(tops), *pieces(totals)]
    packed_stats = parts[0]
    for n, part in enumerate(parts[1:], 1):
        packed_stats = packed_stats + pltpu.roll(part, n * many, 1)
    sent[:, many * HD :] = packed_stats.astype(BF16)


def attend(features, step, total, got, tables, caches, old):
    rows = total.shape[0]
    own, far = caches
    heads = own[0].shape[1]
    if step == 0:
        inputs = [resident(array) for array in own] + [in_hbm(array) for array in far]
        specs = [VMEM_SPEC] * 2 + [HBM_SPEC] * 4
        out_shape = [pltpu.VMEM(part.shape, BF16) for part in own]
        scratch = [pltpu.SemaphoreType.DMA((4,))]
    else:
        inputs = [resident(array) for array in (*own, *far)]
        specs = [VMEM_SPEC] * 4
        out_shape, scratch = [], []
    small = [total, *got, *tables]
    last = step == STEPS - 1
    if last:
        scratch = [pltpu.VMEM((2 * rows, HD), BF16)]
    else:
        out_shape = [jax.ShapeDtypeStruct((2 * rows, HD), BF16)] + out_shape
    return pl.pallas_call(
        functools.partial(attend_kernel, features, step, len(got)),
        out_shape=[
            jax.ShapeDtypeStruct((rows, heads * GROUP * HD + LANES), BF16),
            jax.ShapeDtypeStruct((rows, 2 * LANES), F32),
            *out_shape,
        ],
        in_specs=[VMEM_SPEC] * len(small) + specs + [VMEM_SPEC] * len(old),
        out_specs=[VMEM_SPEC] * (2 + len(out_shape)),
        scratch_shapes=scratch,
        compiler_params=LARGE_PARAMS,
    )(*small, *inputs, *old)


def merge_kernel(own, stat, *refs):
    got, out = refs[:-1], refs[-1]
    many = out.shape[1] // HD
    tops, totals = [stat[:, :LANES]], [stat[:, LANES:]]
    for ref in got:
        packed = ref[:, many * HD :].astype(F32)
        turns = [packed] + [pltpu.roll(packed, LANES - n * many, 1) for n in range(1, 6)]
        tops.append(turns[0] + turns[1] + turns[2])
        totals.append(turns[3] + turns[4] + turns[5])
    used = lanes(own.shape[0]) < many
    tops = [jnp.where(used, top, 0.0) for top in tops]
    top = functools.reduce(jnp.maximum, tops)
    weights = [jnp.exp2(each - top) for each in tops]
    total = functools.reduce(jnp.add, [w * t for w, t in zip(weights, totals)])
    share = 1.0 / jnp.where(used, total, 1.0)
    weights = [weight * share for weight in weights]
    for index in range(many):
        part = slice(index * HD, (index + 1) * HD)
        value = own[:, part].astype(F32) * weights[0][:, index : index + 1]
        for ref, weight in zip(got, weights[1:]):
            value = value + ref[:, part].astype(F32) * weight[:, index : index + 1]
        out[:, part] = value.astype(BF16)


def merge(own, stat, got):
    return pl.pallas_call(
        merge_kernel,
        out_shape=jax.ShapeDtypeStruct((own.shape[0], own.shape[1] - LANES), BF16),
        in_specs=[VMEM_SPEC] * (2 + len(got)),
        out_specs=VMEM_SPEC,
        compiler_params=PARAMS,
    )(own, stat, *got)


def near_output_kernel(mine, weight, out):
    place = whereabouts()
    half = mine.shape[1]
    rows = pl.ds(pl.multiple_of(place[0] * half, half), half)
    out[...] = jnp.dot(mine[...], weight[rows], preferred_element_type=F32)


def far_output_kernel(other, weight, near, out):
    place = whereabouts()
    half = other.shape[1]
    rows = pl.ds(pl.multiple_of((1 - place[0]) * half, half), half)
    total = near[...] + jnp.dot(other[...], weight[rows], preferred_element_type=F32)
    out[...] = total.astype(BF16)


def output(mine, weight):
    other = swapped(mine, "side")
    shape = (mine.shape[0], weight.shape[1])
    near = pl.pallas_call(
        near_output_kernel,
        out_shape=jax.ShapeDtypeStruct(shape, F32),
        in_specs=[VMEM_SPEC] * 2,
        out_specs=VMEM_SPEC,
        compiler_params=PARAMS,
        cost_estimate=COST,
    )(mine, resident(weight))
    return pl.pallas_call(
        far_output_kernel,
        out_shape=jax.ShapeDtypeStruct(shape, BF16),
        in_specs=[VMEM_SPEC] * 3,
        out_specs=VMEM_SPEC,
        compiler_params=PARAMS,
    )(other, resident(weight), near)


def swapped(array, axis):
    return lax.ppermute(array, axis, [(0, 1), (1, 0)])


def from_others(arrays, axis):
    size = lax.axis_size(axis)
    return [
        lax.ppermute(array, axis, [(i, (i + hop) % size) for i in range(size)])
        for hop, array in enumerate(arrays, 1)
    ]


def rotations(lengths, base):
    half = HD // 2
    freq = 500000.0 ** (-(jnp.arange(half, dtype=F32) * 2.0 / HD))
    position = (
        PREFIX + lengths[None, :] + jnp.arange(STEPS, dtype=jnp.int32)[:, None]
    ).astype(F32)
    angle = position[..., None] * freq
    cosine, sine = jnp.cos(angle), jnp.sin(angle)
    cosine = jnp.concatenate([cosine, cosine], axis=-1)
    sine = jnp.concatenate([-sine, sine], axis=-1)
    span = 2 * SAMP_DEV
    vectors = lengths.shape[0] // span
    new_cosine = lax.dynamic_slice_in_dim(cosine, base, span, 1)
    new_sine = lax.dynamic_slice_in_dim(sine, base, span, 1)
    turns = vectors // 2
    new_cosine = jnp.concatenate(
        [new_cosine] * turns + [jnp.ones_like(new_cosine)] * turns, axis=1
    )
    new_sine = jnp.concatenate([new_sine] * turns + [jnp.zeros_like(new_sine)] * turns, axis=1)
    return cosine, sine, new_cosine, new_sine


def local_split(
    hidden,
    gain,
    w_query,
    w_key,
    w_value,
    w_out,
    prefix_keys,
    prefix_values,
    suffix_keys,
    suffix_values,
    suffix_lengths,
    page_table,
):
    features = hidden.shape[1] * lax.axis_size(("seq", "side"))
    base = lax.axis_index("seq") * (2 * SAMP_DEV)
    pools = (prefix_keys, prefix_values, suffix_keys, suffix_values)
    weights = (w_query, w_key, w_value)
    far = [swapped(pool, "side") for pool in pools[2:]]
    gain_row = gain[None, :]
    query_width = w_query.shape[1] // 2
    hops = lax.axis_size("seq") - 1

    state = hidden
    update = jnp.zeros(hidden.shape, F32)
    rest = ()
    old = []
    for step in range(STEPS):
        if rest:
            give, scaled, state, update = give_project(state, gain_row, weights, rest)
            got_sum = swapped(give, "side")
            keep = keep_project(scaled, give, weights)
            total, *sent = pair_sum(keep, got_sum, query_width, hops)
        else:
            keep, give = first_project(state, gain_row, weights)
            got_sum = swapped(give, "side")
            got_sum, *far, keys, values = lax.optimization_barrier((got_sum, *far, *pools[:2]))
            far = [swapped(keys, "side"), *far]
            total, *sent = pair_sum(keep, got_sum, query_width, hops)
            *sent, lengths, table, values = lax.optimization_barrier(
                (*sent, suffix_lengths, page_table, values)
            )
            values = cut(values, sent[0])
            after, values = lax.optimization_barrier((sent[0], values))
            far.insert(1, swapped(values, "side"))
            turning = rotations(lengths, base)
            *own, out_weight, bias = load_caches(lengths, table, pools, w_out, after)
        got = from_others(sent, "seq")
        tables = (*[each[step] for each in turning], bias)
        sent, stat, *kept = attend(
            features, step, total, got, tables, (own, far), old
        )
        far = kept[1:] or far
        got = from_others([sent] * hops, "seq")
        if not rest:
            weights = load(weights, stat)
            got, weights = lax.optimization_barrier((got, weights))
        old += kept[:1]
        mixed = merge(sent, stat, got)
        part = output(mixed, out_weight)
        rest = (update, part, swapped(part, "head"))
    delta = rest[1].astype(F32) + rest[2].astype(F32)
    return ((state.astype(F32) + delta).astype(BF16), update + delta)


def fits(mesh, args):
    heads = args[4].shape[1] // HD // mesh.shape["head"]
    return (
        mesh.shape["head"] == 2
        and mesh.shape["side"] == 2
        and heads % 2 == 0
        and args[6].shape[0] == mesh.shape["groups"]
        and heads // 2 * GROUP * 6 <= LANES
        and mesh.shape["seq"] == heads
        and args[0].shape[0] // mesh.shape["groups"] * STEPS <= LANES
    )


def solution(mesh):
    placed = (
        P("groups", ("seq", "side")),
        P(("seq", "side")),
        P(("seq", "side"), "head"),
        P(("seq", "side"), "head"),
        P(("seq", "side"), "head"),
        P("head", ("seq", "side")),
        P("groups", "head", ("seq", "side"), None),
        P("groups", "head", ("seq", "side"), None),
        P(("groups", "seq", "side"), "head", None, None),
        P(("groups", "seq", "side"), "head", None, None),
        P("groups"),
        P("groups", None),
    )

    def whole(*args):
        return jax.shard_map(
            local_split if fits(mesh, args) else local_any,
            mesh=mesh,
            in_specs=placed,
            out_specs=(P("groups", ("seq", "side")), P("groups", ("seq", "side"))),
            check_vma=False,
        )(*args)

    return whole
```

```python
import functools
import math

import jax
import jax.numpy as jnp
from jax import lax
from jax.experimental import pallas as pl
from jax.experimental.pallas import tpu as pltpu
from jax.sharding import PartitionSpec as P

D = 8192
HD = 128
GROUP = 8
SAMP_DEV = 2
PREFIX = 32768
STEPS = 3


def combined_all(array, axis, combine):
    everything = jax.tree.map(lambda part: lax.all_gather(part, axis), array)
    first = jax.tree.map(lambda part: part[0], everything)

    def lap(k, so_far):
        return combine(so_far, jax.tree.map(lambda part: part[k], everything))

    return lax.fori_loop(1, lax.axis_size(axis), lap, first)


def rotate(vectors, position):
    half = vectors.shape[-1] // 2
    freq = 500000.0 ** (-(jnp.arange(half, dtype=jnp.float32) * 2.0 / vectors.shape[-1]))
    angle = position[..., None] * freq
    cosine = jnp.cos(angle)
    sine = jnp.sin(angle)
    lower = vectors[..., :half]
    upper = vectors[..., half:]
    return jnp.concatenate([lower * cosine - upper * sine, upper * cosine + lower * sine], axis=-1)


def combine(first, second):
    acc_a, top_a, total_a = first
    acc_b, top_b, total_b = second
    top = jnp.maximum(top_a, top_b)
    weight_a = jnp.exp(top_a - top)
    weight_b = jnp.exp(top_b - top)
    return (
        acc_a * weight_a[..., None] + acc_b * weight_b[..., None],
        top,
        total_a * weight_a + total_b * weight_b,
    )


def local_any(
    hidden,
    gain,
    w_query,
    w_key,
    w_value,
    w_out,
    prefix_keys,
    prefix_values,
    suffix_keys,
    suffix_values,
    suffix_lengths,
    page_table,
):
    samples = hidden.shape[0]
    kv_local = w_key.shape[1] // HD
    query_width = kv_local * GROUP * HD
    key_width = kv_local * HD
    prompts = prefix_keys.shape[0]
    scale = 1.0 / math.sqrt(HD)
    rank = lax.axis_index(("seq", "side"))
    w_proj = jnp.concatenate([w_query, w_key, w_value], axis=1)
    pool_keys, pool_values = (suffix_keys, suffix_values)
    start = jnp.bitwise_xor(rank, 1) * SAMP_DEV
    table_rows = lax.dynamic_slice_in_dim(page_table, start, SAMP_DEV, 0)
    page_keys = pool_keys[table_rows]
    page_values = pool_values[table_rows]
    length_rows = lax.dynamic_slice_in_dim(suffix_lengths, start, SAMP_DEV, 0)
    page_count = page_keys.shape[1]
    page_size = page_keys.shape[3]
    suffix_span = page_count * page_size
    live = (jnp.arange(suffix_span, dtype=jnp.int32)[None, :] < length_rows[:, None])[
        :, None, None, :
    ]
    state = hidden
    update = jnp.zeros(hidden.shape, jnp.float32)
    new_keys = []
    new_values = []
    for step in range(STEPS):
        wide = state.astype(jnp.float32)
        scaled = (wide * gain).astype(jnp.bfloat16)
        partial_value = jnp.dot(scaled, w_proj, preferred_element_type=jnp.float32)
        squares = jnp.sum(wide * wide, axis=1)
        proj, total_sq = lax.psum((partial_value, squares), ("seq", "side"))
        inverse = lax.rsqrt(total_sq / D + 1e-05)[:, None]
        position = (PREFIX + suffix_lengths + step).astype(jnp.float32)
        query = rotate(
            (proj[:, :query_width] * inverse).reshape(samples, kv_local, GROUP, HD),
            position[:, None, None],
        ).astype(jnp.bfloat16)
        new_keys.append(
            rotate(
                (proj[:, query_width : query_width + key_width] * inverse).reshape(
                    samples, kv_local, HD
                ),
                position[:, None],
            ).astype(jnp.bfloat16)
        )
        new_values.append(
            (proj[:, query_width + key_width :] * inverse)
            .reshape(samples, kv_local, HD)
            .astype(jnp.bfloat16)
        )
        stacked_keys = jnp.stack(new_keys, axis=1)
        stacked_values = jnp.stack(new_values, axis=1)
        grouped = query.reshape(prompts, samples // prompts, kv_local, GROUP, HD)
        scores = (
            jnp.einsum(
                "pgkhd,pkld->pgkhl", grouped, prefix_keys, preferred_element_type=jnp.float32
            )
            * scale
        )
        top = jnp.max(scores, axis=-1)
        expo = jnp.exp(scores - top[..., None])
        total = jnp.sum(expo, axis=-1)
        acc = jnp.einsum(
            "pgkhl,pkld->pgkhd",
            expo.astype(jnp.bfloat16),
            prefix_values,
            preferred_element_type=jnp.float32,
        )
        acc = acc.reshape(samples, kv_local, GROUP, HD)
        top = top.reshape(samples, kv_local, GROUP)
        total = total.reshape(samples, kv_local, GROUP)
        own_query = lax.dynamic_slice_in_dim(query, start, SAMP_DEV, 0)
        own_keys = lax.dynamic_slice_in_dim(stacked_keys, start, SAMP_DEV, 0)
        own_values = lax.dynamic_slice_in_dim(stacked_values, start, SAMP_DEV, 0)
        suffix_scores = jnp.einsum(
            "skhd,spkjd->skhpj", own_query, page_keys, preferred_element_type=jnp.float32
        )
        suffix_scores = suffix_scores.reshape(SAMP_DEV, kv_local, GROUP, suffix_span) * scale
        suffix_scores = jnp.where(live, suffix_scores, -jnp.inf)
        fresh_scores = (
            jnp.einsum("skhd,sukd->skhu", own_query, own_keys, preferred_element_type=jnp.float32)
            * scale
        )
        peak = jnp.maximum(jnp.max(suffix_scores, axis=-1), jnp.max(fresh_scores, axis=-1))
        suffix_expo = jnp.exp(suffix_scores - peak[..., None])
        fresh_expo = jnp.exp(fresh_scores - peak[..., None])
        near_total = jnp.sum(suffix_expo, axis=-1) + jnp.sum(fresh_expo, axis=-1)
        near_acc = jnp.einsum(
            "skhpj,spkjd->skhd",
            suffix_expo.astype(jnp.bfloat16).reshape(
                SAMP_DEV, kv_local, GROUP, page_count, page_size
            ),
            page_values,
            preferred_element_type=jnp.float32,
        )
        near_acc = near_acc + jnp.einsum(
            "skhu,sukd->skhd",
            fresh_expo.astype(jnp.bfloat16),
            own_values,
            preferred_element_type=jnp.float32,
        )
        rows_now = (
            lax.dynamic_slice_in_dim(acc, start, SAMP_DEV, 0),
            lax.dynamic_slice_in_dim(top, start, SAMP_DEV, 0),
            lax.dynamic_slice_in_dim(total, start, SAMP_DEV, 0),
        )
        joined = combine(rows_now, (near_acc, peak, near_total))
        acc = lax.dynamic_update_slice_in_dim(acc, joined[0], start, 0)
        top = lax.dynamic_update_slice_in_dim(top, joined[1], start, 0)
        total = lax.dynamic_update_slice_in_dim(total, joined[2], start, 0)
        acc, top, total = combined_all((acc, top, total), ("seq", "side"), combine)
        mixed = (acc / total[..., None]).astype(jnp.bfloat16).reshape(samples, query_width)
        part = jnp.dot(mixed, w_out, preferred_element_type=jnp.float32)
        delta = lax.psum(part, "head")
        update = update + delta
        state = (wide + delta).astype(jnp.bfloat16)
    return (state, update)


LANES = 128
LOG2E = 1.4426950408889634
BF16 = jnp.bfloat16
F32 = jnp.float32
VMEM_SPEC = pl.BlockSpec(memory_space=pltpu.VMEM)
SMEM_SPEC = pl.BlockSpec(memory_space=pltpu.SMEM)
HBM_SPEC = pl.BlockSpec(memory_space=pltpu.HBM)
PARAMS = pltpu.CompilerParams(vmem_limit_bytes=4 * 1024 * 1024)
LARGE_PARAMS = pltpu.CompilerParams(vmem_limit_bytes=13 * 1024 * 1024)
COST = pl.CostEstimate(flops=1 << 28, bytes_accessed=1 << 22, transcendentals=0)


def resident(array):
    return pltpu.with_memory_space_constraint(array, pltpu.VMEM)


def in_hbm(array):
    return pltpu.with_memory_space_constraint(array, pltpu.HBM)


def whereabouts():
    seq, side = lax.axis_index("seq"), lax.axis_index("side")
    base = seq * (2 * SAMP_DEV)
    return side, base, base + (1 - side) * SAMP_DEV, base + side * SAMP_DEV, seq


def lanes(rows):
    return lax.broadcasted_iota(jnp.int32, (rows, LANES), 1)


def pieces(values):
    high = values.astype(BF16).astype(F32)
    middle = (values - high).astype(BF16).astype(F32)
    return high, middle, values - high - middle


def move(copies):
    for copy in copies:
        copy.start()
    for copy in copies:
        copy.wait()


def copied(pairs, sems):
    copies = [
        pltpu.make_async_copy(source, target, sems.at[n])
        for n, (source, target) in enumerate(pairs)
    ]
    for copy in copies:
        copy.start()
    return copies


def halves(place, pools, prefix, suffix):
    heads = prefix.shape[1]
    part = pl.ds(place[0] * heads, heads)
    pk, pv, sk, sv = pools
    return [
        (sk.at[:, part], suffix.at[0]),
        (pk.at[0, part], prefix.at[0]),
        (sv.at[:, part], suffix.at[1]),
        (pv.at[0, part], prefix.at[1]),
    ]


def half_shapes(pools):
    pk, sk = pools[0], pools[2]
    return [
        pltpu.VMEM((2, pk.shape[1] // 2) + pk.shape[2:], pk.dtype),
        pltpu.VMEM((2, sk.shape[0], sk.shape[1] // 2) + sk.shape[2:], sk.dtype),
    ]


def live_bias(place, lengths, table, bias):
    pages = table.shape[1]
    page = bias.shape[2] // (SAMP_DEV * pages)
    row = lax.broadcasted_iota(jnp.int32, (bias.shape[1], page), 0)
    column = lax.broadcasted_iota(jnp.int32, (bias.shape[1], page), 1)
    for pool in range(2):
        for j in range(SAMP_DEV):
            sample = place[2 + pool] + j
            mine = row % SAMP_DEV == j
            for p in range(pages):
                live = mine & (column < lengths[sample] - p * page)
                spot = pl.ds(pl.multiple_of(table[sample, p] * page, page), page)
                bias[pool, :, spot] = jnp.where(live, 0.0, -jnp.inf)


def load_caches_kernel(
    lengths, table, pk, pv, sk, sv, w_out, after, prefix, suffix, kept_out, bias, sems
):
    place = whereabouts()
    pairs = halves(place, (pk, pv, sk, sv), prefix, suffix) + [(w_out, kept_out)]
    copies = copied(pairs, sems)
    live_bias(place, lengths, table, bias)
    for copy in copies:
        copy.wait()


def load_caches(lengths, table, pools, w_out, after):
    page = pools[2].shape[2]
    tokens = SAMP_DEV * table.shape[1] * page
    sources = [in_hbm(array) for array in (*pools, w_out)]
    return pl.pallas_call(
        load_caches_kernel,
        out_shape=half_shapes(pools)
        + [
            pltpu.VMEM(w_out.shape, w_out.dtype),
            jax.ShapeDtypeStruct((2, SAMP_DEV * GROUP, tokens), F32),
        ],
        in_specs=[SMEM_SPEC] * 2 + [HBM_SPEC] * 5 + [VMEM_SPEC],
        out_specs=[VMEM_SPEC] * 4,
        scratch_shapes=[pltpu.SemaphoreType.DMA((5,))],
        compiler_params=PARAMS,
        cost_estimate=pl.CostEstimate(flops=0, bytes_accessed=1 << 25, transcendentals=0),
    )(lengths, table, *sources, after)


def load_kernel(*refs):
    count = len(refs) // 2 - 1
    for copy in copied(zip(refs[:count], refs[count + 1 : -1]), refs[-1]):
        copy.wait()


def load(weights, after):
    return pl.pallas_call(
        load_kernel,
        out_shape=[pltpu.VMEM(w.shape, w.dtype) for w in weights],
        in_specs=[HBM_SPEC] * len(weights) + [VMEM_SPEC],
        out_specs=[VMEM_SPEC] * len(weights),
        scratch_shapes=[pltpu.SemaphoreType.DMA((len(weights),))],
        compiler_params=PARAMS,
        cost_estimate=pl.CostEstimate(flops=0, bytes_accessed=1 << 25, transcendentals=0),
    )(*[in_hbm(weight) for weight in weights], after)


def column_tiles(place, weights, who):
    tiles, at = [], 0
    for index, weight in enumerate(weights):
        half = weight.shape[1] // 2
        tile = min(1024, half)
        for begin in range(0, half, tile):
            columns = pl.ds(pl.multiple_of(who * half + begin, tile), tile)
            tiles.append((index, columns, slice(at + begin, at + begin + tile)))
        at += half
    return tiles


def project_half(scaled, weights, tiles, out, arrive=lambda: None):
    vectors, width = [], 0
    for index, columns, to in tiles:
        arrive()
        part = jnp.dot(scaled, weights[index][:, columns], preferred_element_type=F32)
        if index == 0:
            out[:, to] = part.astype(out.dtype)
            width = to.stop
        else:
            vectors += [part[:, at : at + HD] for at in range(0, part.shape[1], HD)]
    span = 2 * SAMP_DEV
    for chip in range(scaled.shape[0] // span):
        part = slice(chip * span, (chip + 1) * span)
        out[:, width + chip * HD : width + (chip + 1) * HD] = jnp.concatenate(
            [vector[part] for vector in vectors], axis=0
        ).astype(out.dtype)


def first_project_kernel(*refs):
    place = whereabouts()
    sources, (keep, give, *buffers, sems) = refs[:5], refs[5:]
    weights, (x_ref, gain) = buffers[:3], buffers[3:]
    outs = ((give, 1 - place[0]), (keep, place[0]))
    halves_of = [(out, column_tiles(place, weights, who)) for out, who in outs]
    pairs = list(zip(sources[3:], buffers[3:]))
    for _, tiles in halves_of:
        for index, columns, _ in tiles:
            pairs.append((sources[index].at[:, columns], weights[index].at[:, columns]))
    copies = copied(pairs, sems)
    copies[0].wait()
    copies[1].wait()
    wide = x_ref[...].astype(F32)
    scaled = (wide * gain[...]).astype(BF16)
    squares = jnp.sum(wide * wide, axis=1, keepdims=True)
    column = lanes(wide.shape[0])
    for out in (give, keep):
        out[:, out.shape[1] - LANES :] = jnp.where(column == 0, squares, 0.0)
    waiting = iter(copies[2:])
    for out, tiles in halves_of:
        project_half(scaled, weights, tiles, out, lambda: next(waiting).wait())


def first_project(x, gain, weights):
    rows = x.shape[0]
    width = sum(w.shape[1] for w in weights) // 2 + LANES
    sources = [in_hbm(array) for array in (*weights, x, gain)]
    count = 2 + 2 * sum(max(1, w.shape[1] // 2048) for w in weights)
    return pl.pallas_call(
        first_project_kernel,
        out_shape=[jax.ShapeDtypeStruct((rows, width), F32)] * 2,
        in_specs=[HBM_SPEC] * 5,
        out_specs=[VMEM_SPEC] * 2,
        scratch_shapes=[pltpu.VMEM(array.shape, array.dtype) for array in sources]
        + [pltpu.SemaphoreType.DMA((count,))],
        compiler_params=LARGE_PARAMS,
    )(*sources)


def give_kernel(x_ref, gain, sum_ref, mine, other, *refs):
    place = whereabouts()
    weights, (give, scaled_ref, new_x, new_sum) = refs[:3], refs[3:]
    delta = mine[...].astype(F32) + other[...].astype(F32)
    new_sum[...] = sum_ref[...] + delta
    state = (x_ref[...].astype(F32) + delta).astype(BF16)
    new_x[...] = state
    wide = state.astype(F32)
    scaled = (wide * gain[...]).astype(BF16)
    scaled_ref[...] = scaled
    squares = jnp.sum(wide * wide, axis=1, keepdims=True)
    give[:, give.shape[1] - LANES :] = in_lanes(squares)
    project_half(scaled, weights, column_tiles(place, weights, 1 - place[0]), give)


def give_project(x, gain, weights, rest):
    rows = x.shape[0]
    width = sum(w.shape[1] for w in weights) // 2 + LANES
    return pl.pallas_call(
        give_kernel,
        out_shape=[
            jax.ShapeDtypeStruct((rows, width), BF16),
            jax.ShapeDtypeStruct(x.shape, BF16),
            jax.ShapeDtypeStruct(x.shape, BF16),
            jax.ShapeDtypeStruct(x.shape, F32),
        ],
        in_specs=[VMEM_SPEC] * 8,
        out_specs=[VMEM_SPEC] * 4,
        compiler_params=PARAMS,
        cost_estimate=COST,
    )(x, gain, *rest, *[resident(weight) for weight in weights])


def keep_kernel(scaled_ref, give, *refs):
    place = whereabouts()
    weights, keep = refs[:3], refs[3]
    scaled = scaled_ref[...]
    main = keep.shape[1] - LANES
    squares = jnp.sum(give[:, main:].astype(F32), axis=1, keepdims=True)
    keep[:, main:] = jnp.broadcast_to(squares, (keep.shape[0], LANES))
    project_half(scaled, weights, column_tiles(place, weights, place[0]), keep)


def keep_project(scaled, give, weights):
    return pl.pallas_call(
        keep_kernel,
        out_shape=jax.ShapeDtypeStruct(give.shape, F32),
        in_specs=[VMEM_SPEC] * 5,
        out_specs=VMEM_SPEC,
        compiler_params=PARAMS,
        cost_estimate=COST,
    )(scaled, give, *[resident(weight) for weight in weights])


def in_lanes(values):
    column = lanes(values.shape[0])
    block = jnp.zeros((values.shape[0], LANES), F32)
    for n, piece in enumerate(pieces(values)):
        block = jnp.where(column == n, piece, block)
    return block.astype(BF16)


def pair_sum_kernel(query_width, keep, got, total, *sent):
    place = whereabouts()
    both = keep[...] + got[...].astype(F32)
    total[...] = both
    rows = both.shape[0]
    main = both.shape[1] - LANES
    squares = keep[:, main : main + 1] + jnp.sum(
        got[:, main:].astype(F32), axis=1, keepdims=True
    )
    total[:, main:] = jnp.broadcast_to(squares, (rows, LANES))
    chips = (main - query_width) // HD
    column = lanes(rows)
    stats = in_lanes(squares)
    query = both[:, :query_width].astype(BF16)
    for hop, out in enumerate(sent, 1):
        chip = lax.rem(place[4] + hop, chips)
        block = pl.ds(pl.multiple_of(query_width + chip * HD, HD), HD)
        out[:, :query_width] = query
        out[:, query_width : query_width + HD] = total[:, block].astype(BF16)
        out[:, query_width + HD :] = stats


def pair_sum(keep, got, query_width, hops):
    rows = keep.shape[0]
    sent = jax.ShapeDtypeStruct((rows, query_width + HD + LANES), BF16)
    return pl.pallas_call(
        functools.partial(pair_sum_kernel, query_width),
        out_shape=[jax.ShapeDtypeStruct(keep.shape, F32)] + [sent] * hops,
        in_specs=[VMEM_SPEC] * 2,
        out_specs=[VMEM_SPEC] * (1 + hops),
        compiler_params=PARAMS,
    )(keep, got)


def lane_fold(fold, array):
    parts = [array[:, at : at + LANES] for at in range(0, array.shape[1], LANES)]
    return functools.reduce(fold, parts)


def row_max(arrays):
    folded = [lane_fold(jnp.maximum, array) for array in arrays]
    return jnp.max(functools.reduce(jnp.maximum, folded), axis=1, keepdims=True)


def against(rows, keys):
    return lax.dot_general(
        rows, keys, (((1,), (1,)), ((), ())), preferred_element_type=F32
    )


def weigh(scores, top, values):
    terms = [
        jnp.dot(
            jnp.exp2(score - top).astype(BF16),
            jnp.concatenate([value, jnp.ones_like(value)], axis=1),
            preferred_element_type=F32,
        )
        for score, value in zip(scores, values)
    ]
    both = functools.reduce(jnp.add, terms)
    return both[:, HD : HD + 1], both[:, :HD]


def attend_kernel(features, step, others, *refs):
    place = whereabouts()
    total_ref = refs[0]
    got = refs[1 : 1 + others]
    cos_ref, sin_ref, new_cos, new_sin, bias_ref = refs[1 + others : 6 + others]
    refs = refs[2:]
    own_prefix, own_suffix, *far = refs[4 + others : (10 if step == 0 else 8) + others]
    refs = refs[(10 if step == 0 else 8) + others :]
    old, (sent, stat, fresh) = refs[:step], refs[step : 3 + step]
    heads = own_prefix.shape[1]
    waits = []
    if step == 0:
        got_prefix, got_suffix, sems = refs[3:]
        waits = copied(halves(place, far, got_prefix, got_suffix), sems)
    else:
        got_prefix, got_suffix = far
    prefix = (own_prefix, got_prefix)
    suffix = (own_suffix, got_suffix)
    rows = total_ref.shape[0]
    width = total_ref.shape[1] - LANES
    query_width = width - 2 * heads * HD
    base, starts = place[1], (place[2], place[3])
    scale = LOG2E / math.sqrt(HD)

    stats = total_ref[:, width : width + 1]
    for ref in got:
        stats = stats + jnp.sum(ref[:, query_width + HD :].astype(F32), axis=1, keepdims=True)
    inverse = lax.rsqrt(stats / features + 1e-05)
    cosine = cos_ref[...]
    sine = sin_ref[...]

    def query_block(at):
        value = total_ref[:, at : at + HD]
        for ref in got:
            value = value + ref[:, at : at + HD].astype(F32)
        value = value * (inverse * scale)
        return (value * cosine + pltpu.roll(value, HD // 2, 1) * sine).astype(BF16)

    sample = lax.broadcasted_iota(jnp.int32, (rows, 1), 0)
    few_rows = SAMP_DEV * GROUP
    pick_row = lax.broadcasted_iota(jnp.int32, (few_rows, GROUP * rows), 0)
    pick_column = lax.broadcasted_iota(jnp.int32, (few_rows, GROUP * rows), 1)
    spot = (pick_row // SAMP_DEV) * rows + pick_row % SAMP_DEV
    picks = [(pick_column == spot + start).astype(F32).astype(BF16) for start in starts]
    column = lanes(rows)

    queries = [
        [query_block((head * GROUP + g) * HD) for g in range(GROUP)] for head in range(heads)
    ]
    packed = [jnp.concatenate(query, axis=0) for query in queries]
    span = 2 * SAMP_DEV
    mine = pl.ds(pl.multiple_of(query_width + place[4] * HD, HD), HD)
    new = total_ref[:, mine]
    for ref in got:
        new = new + ref[:, query_width : query_width + HD].astype(F32)
    vector_row = lax.broadcasted_iota(jnp.int32, (rows, 1), 0) % span
    new_inverse = jnp.zeros((rows, 1), F32)
    for i in range(span):
        one = jnp.sum(jnp.where(sample == base + i, inverse, 0.0), axis=0, keepdims=True)
        new_inverse = jnp.where(vector_row == i, one, new_inverse)
    new = new * new_inverse
    new = new * new_cos[...] + pltpu.roll(new, HD // 2, 1) * new_sin[...]
    half = rows // 2
    fresh[:rows] = new.astype(BF16)
    fresh[rows:] = jnp.concatenate([new[half:], new[:half]], axis=0).astype(BF16)
    padding = jnp.zeros((LANES - (step + 1) * rows, HD), BF16)
    new_keys = jnp.concatenate([ref[:rows] for ref in (*old, fresh)] + [padding], axis=0)
    new_values = jnp.concatenate([ref[rows:] for ref in (*old, fresh)] + [padding], axis=0)
    line = lax.broadcasted_iota(jnp.int32, (GROUP * rows, LANES), 0) % rows - base
    token = lax.broadcasted_iota(jnp.int32, (GROUP * rows, LANES), 1)
    new_scores = [
        jnp.where(
            (token < (step + 1) * rows) & (token % rows == line + head * span)
            & (line >= 0) & (line < span),
            against(packed[head], new_keys),
            -jnp.inf,
        )
        for head in range(heads)
    ]
    few = [
        [jnp.dot(pick, packed[head], preferred_element_type=F32).astype(BF16) for pick in picks]
        for head in range(heads)
    ]
    slots, page = own_suffix.shape[1], own_suffix.shape[3]
    length = own_prefix.shape[2]
    chunk = min(2048, length)
    pieces_of = [(src, at) for src in range(2) for at in range(0, length, chunk)]

    def pool(kind, src, head):
        return suffix[src][kind, :, head].reshape(slots * page, HD)

    near_scores = [[None] * 2 for _ in range(heads)]
    far_scores = [[None] * len(pieces_of) for _ in range(heads)]
    for src in range(2):
        if src == 1:
            for copy in waits[:2]:
                copy.wait()
        for head in range(heads):
            near_scores[head][src] = against(few[head][src], pool(0, src, head)) + bias_ref[src]
            for n, (whose, at) in enumerate(pieces_of):
                if whose == src:
                    far_scores[head][n] = against(
                        packed[head], prefix[src][0, head, at : at + chunk]
                    )
    near_tops = [[row_max([score]) for score in scores] for scores in near_scores]
    for head in range(heads):
        far_scores[head].append(new_scores[head])
    far_tops = [row_max(scores) for scores in far_scores]
    for copy in waits[2:]:
        copy.wait()
    near = [
        [
            weigh([near_scores[head][src]], near_tops[head][src], [pool(1, src, head)])
            for src in range(2)
        ]
        for head in range(heads)
    ]

    tops = jnp.zeros((rows, LANES), F32)
    totals = jnp.zeros((rows, LANES), F32)
    for head in range(heads):
        far_total, far_acc = weigh(
            far_scores[head],
            far_tops[head],
            [prefix[src][1, head, at : at + chunk] for src, at in pieces_of] + [new_values],
        )
        for g in range(GROUP):
            part = slice(g * rows, (g + 1) * rows)
            far_top = far_tops[head][part]
            near_top = jnp.full((rows, 1), -1e30, F32)
            total = jnp.zeros((rows, 1), F32)
            acc = jnp.zeros((rows, HD), F32)
            for src in range(2):
                for j in range(SAMP_DEV):
                    line = slice(g * SAMP_DEV + j, g * SAMP_DEV + j + 1)
                    here = sample == starts[src] + j
                    near_top = jnp.where(here, near_tops[head][src][line], near_top)
                    total = jnp.where(here, near[head][src][0][line], total)
                    acc = jnp.where(here, near[head][src][1][line], acc)
            top = jnp.maximum(far_top, near_top)
            far_weight = jnp.exp2(far_top - top)
            near_weight = jnp.exp2(near_top - top)
            total = total * near_weight + far_total[part] * far_weight
            acc = acc * near_weight + far_acc[part] * far_weight
            index = head * GROUP + g
            sent[:, index * HD : (index + 1) * HD] = acc.astype(BF16)
            tops = jnp.where(column == index, top, tops)
            totals = jnp.where(column == index, total, totals)
    many = heads * GROUP
    stat[:, :LANES] = tops
    stat[:, LANES:] = totals
    parts = [*pieces(tops), *pieces(totals)]
    packed_stats = parts[0]
    for n, part in enumerate(parts[1:], 1):
        packed_stats = packed_stats + pltpu.roll(part, n * many, 1)
    sent[:, many * HD :] = packed_stats.astype(BF16)


def attend(features, step, total, got, tables, caches, old):
    rows = total.shape[0]
    own, far = caches
    heads = own[0].shape[1]
    if step == 0:
        inputs = [resident(array) for array in own] + [in_hbm(array) for array in far]
        specs = [VMEM_SPEC] * 2 + [HBM_SPEC] * 4
        out_shape = [pltpu.VMEM(part.shape, BF16) for part in own]
        scratch = [pltpu.SemaphoreType.DMA((4,))]
    else:
        inputs = [resident(array) for array in (*own, *far)]
        specs = [VMEM_SPEC] * 4
        out_shape, scratch = [], []
    small = [total, *got, *tables]
    last = step == STEPS - 1
    if last:
        scratch = [pltpu.VMEM((2 * rows, HD), BF16)]
    else:
        out_shape = [jax.ShapeDtypeStruct((2 * rows, HD), BF16)] + out_shape
    return pl.pallas_call(
        functools.partial(attend_kernel, features, step, len(got)),
        out_shape=[
            jax.ShapeDtypeStruct((rows, heads * GROUP * HD + LANES), BF16),
            jax.ShapeDtypeStruct((rows, 2 * LANES), F32),
            *out_shape,
        ],
        in_specs=[VMEM_SPEC] * len(small) + specs + [VMEM_SPEC] * len(old),
        out_specs=[VMEM_SPEC] * (2 + len(out_shape)),
        scratch_shapes=scratch,
        compiler_params=LARGE_PARAMS,
    )(*small, *inputs, *old)


def merge_kernel(own, stat, *refs):
    got, out = refs[:-1], refs[-1]
    many = out.shape[1] // HD
    tops, totals = [stat[:, :LANES]], [stat[:, LANES:]]
    for ref in got:
        packed = ref[:, many * HD :].astype(F32)
        turns = [packed] + [pltpu.roll(packed, LANES - n * many, 1) for n in range(1, 6)]
        tops.append(turns[0] + turns[1] + turns[2])
        totals.append(turns[3] + turns[4] + turns[5])
    used = lanes(own.shape[0]) < many
    tops = [jnp.where(used, top, 0.0) for top in tops]
    top = functools.reduce(jnp.maximum, tops)
    weights = [jnp.exp2(each - top) for each in tops]
    total = functools.reduce(jnp.add, [w * t for w, t in zip(weights, totals)])
    share = 1.0 / jnp.where(used, total, 1.0)
    weights = [weight * share for weight in weights]
    for index in range(many):
        part = slice(index * HD, (index + 1) * HD)
        value = own[:, part].astype(F32) * weights[0][:, index : index + 1]
        for ref, weight in zip(got, weights[1:]):
            value = value + ref[:, part].astype(F32) * weight[:, index : index + 1]
        out[:, part] = value.astype(BF16)


def merge(own, stat, got):
    return pl.pallas_call(
        merge_kernel,
        out_shape=jax.ShapeDtypeStruct((own.shape[0], own.shape[1] - LANES), BF16),
        in_specs=[VMEM_SPEC] * (2 + len(got)),
        out_specs=VMEM_SPEC,
        compiler_params=PARAMS,
    )(own, stat, *got)


def near_output_kernel(mine, weight, out):
    place = whereabouts()
    half = mine.shape[1]
    rows = pl.ds(pl.multiple_of(place[0] * half, half), half)
    out[...] = jnp.dot(mine[...], weight[rows], preferred_element_type=F32)


def far_output_kernel(other, weight, near, out):
    place = whereabouts()
    half = other.shape[1]
    rows = pl.ds(pl.multiple_of((1 - place[0]) * half, half), half)
    total = near[...] + jnp.dot(other[...], weight[rows], preferred_element_type=F32)
    out[...] = total.astype(BF16)


def output(mine, weight):
    other = swapped(mine, "side")
    shape = (mine.shape[0], weight.shape[1])
    near = pl.pallas_call(
        near_output_kernel,
        out_shape=jax.ShapeDtypeStruct(shape, F32),
        in_specs=[VMEM_SPEC] * 2,
        out_specs=VMEM_SPEC,
        compiler_params=PARAMS,
        cost_estimate=COST,
    )(mine, resident(weight))
    return pl.pallas_call(
        far_output_kernel,
        out_shape=jax.ShapeDtypeStruct(shape, BF16),
        in_specs=[VMEM_SPEC] * 3,
        out_specs=VMEM_SPEC,
        compiler_params=PARAMS,
    )(other, resident(weight), near)


def swapped(array, axis):
    return lax.ppermute(array, axis, [(0, 1), (1, 0)])


def from_others(arrays, axis):
    size = lax.axis_size(axis)
    return [
        lax.ppermute(array, axis, [(i, (i + hop) % size) for i in range(size)])
        for hop, array in enumerate(arrays, 1)
    ]


def rotations(lengths, base):
    half = HD // 2
    freq = 500000.0 ** (-(jnp.arange(half, dtype=F32) * 2.0 / HD))
    position = (
        PREFIX + lengths[None, :] + jnp.arange(STEPS, dtype=jnp.int32)[:, None]
    ).astype(F32)
    angle = position[..., None] * freq
    cosine, sine = jnp.cos(angle), jnp.sin(angle)
    cosine = jnp.concatenate([cosine, cosine], axis=-1)
    sine = jnp.concatenate([-sine, sine], axis=-1)
    span = 2 * SAMP_DEV
    vectors = lengths.shape[0] // span
    new_cosine = lax.dynamic_slice_in_dim(cosine, base, span, 1)
    new_sine = lax.dynamic_slice_in_dim(sine, base, span, 1)
    turns = vectors // 2
    new_cosine = jnp.concatenate(
        [new_cosine] * turns + [jnp.ones_like(new_cosine)] * turns, axis=1
    )
    new_sine = jnp.concatenate([new_sine] * turns + [jnp.zeros_like(new_sine)] * turns, axis=1)
    return cosine, sine, new_cosine, new_sine


def local_split(
    hidden,
    gain,
    w_query,
    w_key,
    w_value,
    w_out,
    prefix_keys,
    prefix_values,
    suffix_keys,
    suffix_values,
    suffix_lengths,
    page_table,
):
    features = hidden.shape[1] * lax.axis_size(("seq", "side"))
    base = lax.axis_index("seq") * (2 * SAMP_DEV)
    pools = (prefix_keys, prefix_values, suffix_keys, suffix_values)
    weights = (w_query, w_key, w_value)
    far = [swapped(pool, "side") for pool in pools[2:]]
    gain_row = gain[None, :]
    query_width = w_query.shape[1] // 2
    hops = lax.axis_size("seq") - 1

    state = hidden
    update = jnp.zeros(hidden.shape, F32)
    rest = ()
    old = []
    for step in range(STEPS):
        if rest:
            give, scaled, state, update = give_project(state, gain_row, weights, rest)
            got_sum = swapped(give, "side")
            keep = keep_project(scaled, give, weights)
            total, *sent = pair_sum(keep, got_sum, query_width, hops)
        else:
            keep, give = first_project(state, gain_row, weights)
            got_sum = swapped(give, "side")
            got_sum, *given = lax.optimization_barrier((got_sum, *far, *pools[:2]))
            far = [swapped(pool, "side") for pool in given[2:]] + given[:2]
            total, *sent = pair_sum(keep, got_sum, query_width, hops)
            *sent, lengths, table = lax.optimization_barrier(
                (*sent, suffix_lengths, page_table)
            )
            turning = rotations(lengths, base)
            *own, out_weight, bias = load_caches(lengths, table, pools, w_out, sent[0])
        got = from_others(sent, "seq")
        tables = (*[each[step] for each in turning], bias)
        sent, stat, *kept = attend(
            features, step, total, got, tables, (own, far), old
        )
        far = kept[1:] or far
        got = from_others([sent] * hops, "seq")
        if not rest:
            weights = load(weights, stat)
            got, weights = lax.optimization_barrier((got, weights))
        old += kept[:1]
        mixed = merge(sent, stat, got)
        part = output(mixed, out_weight)
        rest = (update, part, swapped(part, "head"))
    delta = rest[1].astype(F32) + rest[2].astype(F32)
    return ((state.astype(F32) + delta).astype(BF16), update + delta)


def fits(mesh, args):
    heads = args[4].shape[1] // HD // mesh.shape["head"]
    return (
        mesh.shape["head"] == 2
        and mesh.shape["side"] == 2
        and heads % 2 == 0
        and args[6].shape[0] == mesh.shape["groups"]
        and heads // 2 * GROUP * 6 <= LANES
        and mesh.shape["seq"] == heads
        and args[0].shape[0] // mesh.shape["groups"] * STEPS <= LANES
    )


def solution(mesh):
    placed = (
        P("groups", ("seq", "side")),
        P(("seq", "side")),
        P(("seq", "side"), "head"),
        P(("seq", "side"), "head"),
        P(("seq", "side"), "head"),
        P("head", ("seq", "side")),
        P("groups", "head", ("seq", "side"), None),
        P("groups", "head", ("seq", "side"), None),
        P(("groups", "seq", "side"), "head", None, None),
        P(("groups", "seq", "side"), "head", None, None),
        P("groups"),
        P("groups", None),
    )

    def whole(*args):
        return jax.shard_map(
            local_split if fits(mesh, args) else local_any,
            mesh=mesh,
            in_specs=placed,
            out_specs=(P("groups", ("seq", "side")), P("groups", ("seq", "side"))),
            check_vma=False,
        )(*args)

    return whole
```

```python
import functools
import math

import jax
import jax.numpy as jnp
from jax import lax
from jax.experimental import pallas as pl
from jax.experimental.pallas import tpu as pltpu
from jax.sharding import PartitionSpec as P

D = 8192
HD = 128
GROUP = 8
SAMP_DEV = 2
PREFIX = 32768
STEPS = 3


def combined_all(array, axis, combine):
    everything = jax.tree.map(lambda part: lax.all_gather(part, axis), array)
    first = jax.tree.map(lambda part: part[0], everything)

    def lap(k, so_far):
        return combine(so_far, jax.tree.map(lambda part: part[k], everything))

    return lax.fori_loop(1, lax.axis_size(axis), lap, first)


def rotate(vectors, position):
    half = vectors.shape[-1] // 2
    freq = 500000.0 ** (-(jnp.arange(half, dtype=jnp.float32) * 2.0 / vectors.shape[-1]))
    angle = position[..., None] * freq
    cosine = jnp.cos(angle)
    sine = jnp.sin(angle)
    lower = vectors[..., :half]
    upper = vectors[..., half:]
    return jnp.concatenate([lower * cosine - upper * sine, upper * cosine + lower * sine], axis=-1)


def combine(first, second):
    acc_a, top_a, total_a = first
    acc_b, top_b, total_b = second
    top = jnp.maximum(top_a, top_b)
    weight_a = jnp.exp(top_a - top)
    weight_b = jnp.exp(top_b - top)
    return (
        acc_a * weight_a[..., None] + acc_b * weight_b[..., None],
        top,
        total_a * weight_a + total_b * weight_b,
    )


def local_any(
    hidden,
    gain,
    w_query,
    w_key,
    w_value,
    w_out,
    prefix_keys,
    prefix_values,
    suffix_keys,
    suffix_values,
    suffix_lengths,
    page_table,
):
    samples = hidden.shape[0]
    kv_local = w_key.shape[1] // HD
    query_width = kv_local * GROUP * HD
    key_width = kv_local * HD
    prompts = prefix_keys.shape[0]
    scale = 1.0 / math.sqrt(HD)
    rank = lax.axis_index(("seq", "side"))
    w_proj = jnp.concatenate([w_query, w_key, w_value], axis=1)
    pool_keys, pool_values = (suffix_keys, suffix_values)
    start = jnp.bitwise_xor(rank, 1) * SAMP_DEV
    table_rows = lax.dynamic_slice_in_dim(page_table, start, SAMP_DEV, 0)
    page_keys = pool_keys[table_rows]
    page_values = pool_values[table_rows]
    length_rows = lax.dynamic_slice_in_dim(suffix_lengths, start, SAMP_DEV, 0)
    page_count = page_keys.shape[1]
    page_size = page_keys.shape[3]
    suffix_span = page_count * page_size
    live = (jnp.arange(suffix_span, dtype=jnp.int32)[None, :] < length_rows[:, None])[
        :, None, None, :
    ]
    state = hidden
    update = jnp.zeros(hidden.shape, jnp.float32)
    new_keys = []
    new_values = []
    for step in range(STEPS):
        wide = state.astype(jnp.float32)
        scaled = (wide * gain).astype(jnp.bfloat16)
        partial_value = jnp.dot(scaled, w_proj, preferred_element_type=jnp.float32)
        squares = jnp.sum(wide * wide, axis=1)
        proj, total_sq = lax.psum((partial_value, squares), ("seq", "side"))
        inverse = lax.rsqrt(total_sq / D + 1e-05)[:, None]
        position = (PREFIX + suffix_lengths + step).astype(jnp.float32)
        query = rotate(
            (proj[:, :query_width] * inverse).reshape(samples, kv_local, GROUP, HD),
            position[:, None, None],
        ).astype(jnp.bfloat16)
        new_keys.append(
            rotate(
                (proj[:, query_width : query_width + key_width] * inverse).reshape(
                    samples, kv_local, HD
                ),
                position[:, None],
            ).astype(jnp.bfloat16)
        )
        new_values.append(
            (proj[:, query_width + key_width :] * inverse)
            .reshape(samples, kv_local, HD)
            .astype(jnp.bfloat16)
        )
        stacked_keys = jnp.stack(new_keys, axis=1)
        stacked_values = jnp.stack(new_values, axis=1)
        grouped = query.reshape(prompts, samples // prompts, kv_local, GROUP, HD)
        scores = (
            jnp.einsum(
                "pgkhd,pkld->pgkhl", grouped, prefix_keys, preferred_element_type=jnp.float32
            )
            * scale
        )
        top = jnp.max(scores, axis=-1)
        expo = jnp.exp(scores - top[..., None])
        total = jnp.sum(expo, axis=-1)
        acc = jnp.einsum(
            "pgkhl,pkld->pgkhd",
            expo.astype(jnp.bfloat16),
            prefix_values,
            preferred_element_type=jnp.float32,
        )
        acc = acc.reshape(samples, kv_local, GROUP, HD)
        top = top.reshape(samples, kv_local, GROUP)
        total = total.reshape(samples, kv_local, GROUP)
        own_query = lax.dynamic_slice_in_dim(query, start, SAMP_DEV, 0)
        own_keys = lax.dynamic_slice_in_dim(stacked_keys, start, SAMP_DEV, 0)
        own_values = lax.dynamic_slice_in_dim(stacked_values, start, SAMP_DEV, 0)
        suffix_scores = jnp.einsum(
            "skhd,spkjd->skhpj", own_query, page_keys, preferred_element_type=jnp.float32
        )
        suffix_scores = suffix_scores.reshape(SAMP_DEV, kv_local, GROUP, suffix_span) * scale
        suffix_scores = jnp.where(live, suffix_scores, -jnp.inf)
        fresh_scores = (
            jnp.einsum("skhd,sukd->skhu", own_query, own_keys, preferred_element_type=jnp.float32)
            * scale
        )
        peak = jnp.maximum(jnp.max(suffix_scores, axis=-1), jnp.max(fresh_scores, axis=-1))
        suffix_expo = jnp.exp(suffix_scores - peak[..., None])
        fresh_expo = jnp.exp(fresh_scores - peak[..., None])
        near_total = jnp.sum(suffix_expo, axis=-1) + jnp.sum(fresh_expo, axis=-1)
        near_acc = jnp.einsum(
            "skhpj,spkjd->skhd",
            suffix_expo.astype(jnp.bfloat16).reshape(
                SAMP_DEV, kv_local, GROUP, page_count, page_size
            ),
            page_values,
            preferred_element_type=jnp.float32,
        )
        near_acc = near_acc + jnp.einsum(
            "skhu,sukd->skhd",
            fresh_expo.astype(jnp.bfloat16),
            own_values,
            preferred_element_type=jnp.float32,
        )
        rows_now = (
            lax.dynamic_slice_in_dim(acc, start, SAMP_DEV, 0),
            lax.dynamic_slice_in_dim(top, start, SAMP_DEV, 0),
            lax.dynamic_slice_in_dim(total, start, SAMP_DEV, 0),
        )
        joined = combine(rows_now, (near_acc, peak, near_total))
        acc = lax.dynamic_update_slice_in_dim(acc, joined[0], start, 0)
        top = lax.dynamic_update_slice_in_dim(top, joined[1], start, 0)
        total = lax.dynamic_update_slice_in_dim(total, joined[2], start, 0)
        acc, top, total = combined_all((acc, top, total), ("seq", "side"), combine)
        mixed = (acc / total[..., None]).astype(jnp.bfloat16).reshape(samples, query_width)
        part = jnp.dot(mixed, w_out, preferred_element_type=jnp.float32)
        delta = lax.psum(part, "head")
        update = update + delta
        state = (wide + delta).astype(jnp.bfloat16)
    return (state, update)


LANES = 128
LOG2E = 1.4426950408889634
BF16 = jnp.bfloat16
F32 = jnp.float32
VMEM_SPEC = pl.BlockSpec(memory_space=pltpu.VMEM)
SMEM_SPEC = pl.BlockSpec(memory_space=pltpu.SMEM)
HBM_SPEC = pl.BlockSpec(memory_space=pltpu.HBM)
PARAMS = pltpu.CompilerParams(vmem_limit_bytes=4 * 1024 * 1024)
LARGE_PARAMS = pltpu.CompilerParams(vmem_limit_bytes=13 * 1024 * 1024)
COST = pl.CostEstimate(flops=1 << 28, bytes_accessed=1 << 22, transcendentals=0)


def resident(array):
    return pltpu.with_memory_space_constraint(array, pltpu.VMEM)


def in_hbm(array):
    return pltpu.with_memory_space_constraint(array, pltpu.HBM)


def whereabouts():
    seq, side = lax.axis_index("seq"), lax.axis_index("side")
    base = seq * (2 * SAMP_DEV)
    return side, base, base + (1 - side) * SAMP_DEV, base + side * SAMP_DEV, seq


def lanes(rows):
    return lax.broadcasted_iota(jnp.int32, (rows, LANES), 1)


def pieces(values):
    high = values.astype(BF16).astype(F32)
    middle = (values - high).astype(BF16).astype(F32)
    return high, middle, values - high - middle


def move(copies):
    for copy in copies:
        copy.start()
    for copy in copies:
        copy.wait()


def copied(pairs, sems):
    copies = [
        pltpu.make_async_copy(source, target, sems.at[n])
        for n, (source, target) in enumerate(pairs)
    ]
    for copy in copies:
        copy.start()
    return copies


def halves(place, pools, prefix, suffix):
    heads = prefix.shape[1]
    part = pl.ds(place[0] * heads, heads)
    pk, pv, sk, sv = pools
    return [
        (sk.at[:, part], suffix.at[0]),
        (pk.at[0, part], prefix.at[0]),
        (sv.at[:, part], suffix.at[1]),
        (pv.at[0, part], prefix.at[1]),
    ]


def half_shapes(pools):
    pk, sk = pools[0], pools[2]
    return [
        pltpu.VMEM((2, pk.shape[1] // 2) + pk.shape[2:], pk.dtype),
        pltpu.VMEM((2, sk.shape[0], sk.shape[1] // 2) + sk.shape[2:], sk.dtype),
    ]


def live_bias(place, lengths, table, bias):
    pages = table.shape[1]
    page = bias.shape[2] // (SAMP_DEV * pages)
    row = lax.broadcasted_iota(jnp.int32, (bias.shape[1], page), 0)
    column = lax.broadcasted_iota(jnp.int32, (bias.shape[1], page), 1)
    for pool in range(2):
        for j in range(SAMP_DEV):
            sample = place[2 + pool] + j
            mine = row % SAMP_DEV == j
            for p in range(pages):
                live = mine & (column < lengths[sample] - p * page)
                spot = pl.ds(pl.multiple_of(table[sample, p] * page, page), page)
                bias[pool, :, spot] = jnp.where(live, 0.0, -jnp.inf)


def load_caches_kernel(
    lengths, table, pk, pv, sk, sv, w_out, after, prefix, suffix, kept_out, bias, sems
):
    place = whereabouts()
    pairs = halves(place, (pk, pv, sk, sv), prefix, suffix) + [(w_out, kept_out)]
    copies = copied(pairs, sems)
    live_bias(place, lengths, table, bias)
    for copy in copies:
        copy.wait()


def load_caches(lengths, table, pools, w_out, after):
    page = pools[2].shape[2]
    tokens = SAMP_DEV * table.shape[1] * page
    sources = [in_hbm(array) for array in (*pools, w_out)]
    return pl.pallas_call(
        load_caches_kernel,
        out_shape=half_shapes(pools)
        + [
            pltpu.VMEM(w_out.shape, w_out.dtype),
            jax.ShapeDtypeStruct((2, SAMP_DEV * GROUP, tokens), F32),
        ],
        in_specs=[SMEM_SPEC] * 2 + [HBM_SPEC] * 5 + [VMEM_SPEC],
        out_specs=[VMEM_SPEC] * 4,
        scratch_shapes=[pltpu.SemaphoreType.DMA((5,))],
        compiler_params=PARAMS,
        cost_estimate=pl.CostEstimate(flops=0, bytes_accessed=1 << 25, transcendentals=0),
    )(lengths, table, *sources, after)


def load_kernel(*refs):
    count = len(refs) // 2 - 1
    for copy in copied(zip(refs[:count], refs[count + 1 : -1]), refs[-1]):
        copy.wait()


def load(weights, after):
    return pl.pallas_call(
        load_kernel,
        out_shape=[pltpu.VMEM(w.shape, w.dtype) for w in weights],
        in_specs=[HBM_SPEC] * len(weights) + [VMEM_SPEC],
        out_specs=[VMEM_SPEC] * len(weights),
        scratch_shapes=[pltpu.SemaphoreType.DMA((len(weights),))],
        compiler_params=PARAMS,
        cost_estimate=pl.CostEstimate(flops=0, bytes_accessed=1 << 25, transcendentals=0),
    )(*[in_hbm(weight) for weight in weights], after)


def column_tiles(weights, who, most):
    tiles, at = [], 0
    for index, weight in enumerate(weights):
        half = weight.shape[1] // 2
        tile = min(most, half)
        for begin in range(0, half, tile):
            columns = pl.ds(pl.multiple_of(who * half + begin, tile), tile)
            tiles.append((index, columns, slice(at + begin, at + begin + tile)))
        at += half
    return tiles


def project_half(scaled, weights, tiles, out, arrive=lambda: None):
    vectors, width = [], 0
    for index, columns, to in tiles:
        arrive()
        part = jnp.dot(scaled, weights[index][:, columns], preferred_element_type=F32)
        if index == 0:
            out[:, to] = part.astype(out.dtype)
            width = to.stop
        else:
            vectors += [part[:, at : at + HD] for at in range(0, part.shape[1], HD)]
    span = 2 * SAMP_DEV
    for chip in range(scaled.shape[0] // span):
        part = slice(chip * span, (chip + 1) * span)
        out[:, width + chip * HD : width + (chip + 1) * HD] = jnp.concatenate(
            [vector[part] for vector in vectors], axis=0
        ).astype(out.dtype)


def first_project_kernel(*refs):
    place = whereabouts()
    sources, (keep, give, *buffers, sems) = refs[:5], refs[5:]
    weights, (x_ref, gain) = buffers[:3], buffers[3:]
    outs = ((give, 1 - place[0]), (keep, place[0]))
    halves_of = [(out, column_tiles(weights, who, 1024)) for out, who in outs]
    pairs = list(zip(sources[3:], buffers[3:]))
    for _, tiles in halves_of:
        for index, columns, _ in tiles:
            pairs.append((sources[index].at[:, columns], weights[index].at[:, columns]))
    copies = copied(pairs, sems)
    copies[0].wait()
    copies[1].wait()
    wide = x_ref[...].astype(F32)
    scaled = (wide * gain[...]).astype(BF16)
    squares = jnp.sum(wide * wide, axis=1, keepdims=True)
    column = lanes(wide.shape[0])
    for out in (give, keep):
        out[:, out.shape[1] - LANES :] = jnp.where(column == 0, squares, 0.0)
    waiting = iter(copies[2:])
    for out, tiles in halves_of:
        project_half(scaled, weights, tiles, out, lambda: next(waiting).wait())


def first_project(x, gain, weights):
    rows = x.shape[0]
    width = sum(w.shape[1] for w in weights) // 2 + LANES
    sources = [in_hbm(array) for array in (*weights, x, gain)]
    count = 2 + 2 * sum(max(1, w.shape[1] // 2048) for w in weights)
    return pl.pallas_call(
        first_project_kernel,
        out_shape=[jax.ShapeDtypeStruct((rows, width), F32)] * 2,
        in_specs=[HBM_SPEC] * 5,
        out_specs=[VMEM_SPEC] * 2,
        scratch_shapes=[pltpu.VMEM(array.shape, array.dtype) for array in sources]
        + [pltpu.SemaphoreType.DMA((count,))],
        compiler_params=LARGE_PARAMS,
    )(*sources)


def give_kernel(x_ref, gain, sum_ref, mine, other, *refs):
    place = whereabouts()
    weights, (give, scaled_ref, new_x, new_sum) = refs[:3], refs[3:]
    delta = mine[...].astype(F32) + other[...].astype(F32)
    new_sum[...] = sum_ref[...] + delta
    state = (x_ref[...].astype(F32) + delta).astype(BF16)
    new_x[...] = state
    wide = state.astype(F32)
    scaled = (wide * gain[...]).astype(BF16)
    scaled_ref[...] = scaled
    squares = jnp.sum(wide * wide, axis=1, keepdims=True)
    give[:, give.shape[1] - LANES :] = in_lanes(squares)
    project_half(scaled, weights, column_tiles(weights, 1 - place[0], 2048), give)


def give_project(x, gain, weights, rest):
    rows = x.shape[0]
    width = sum(w.shape[1] for w in weights) // 2 + LANES
    return pl.pallas_call(
        give_kernel,
        out_shape=[
            jax.ShapeDtypeStruct((rows, width), BF16),
            jax.ShapeDtypeStruct(x.shape, BF16),
            jax.ShapeDtypeStruct(x.shape, BF16),
            jax.ShapeDtypeStruct(x.shape, F32),
        ],
        in_specs=[VMEM_SPEC] * 8,
        out_specs=[VMEM_SPEC] * 4,
        compiler_params=PARAMS,
        cost_estimate=COST,
    )(x, gain, *rest, *[resident(weight) for weight in weights])


def keep_kernel(scaled_ref, give, *refs):
    place = whereabouts()
    weights, keep = refs[:3], refs[3]
    scaled = scaled_ref[...]
    main = keep.shape[1] - LANES
    squares = jnp.sum(give[:, main:].astype(F32), axis=1, keepdims=True)
    keep[:, main:] = jnp.broadcast_to(squares, (keep.shape[0], LANES))
    project_half(scaled, weights, column_tiles(weights, place[0], 2048), keep)


def keep_project(scaled, give, weights):
    return pl.pallas_call(
        keep_kernel,
        out_shape=jax.ShapeDtypeStruct(give.shape, F32),
        in_specs=[VMEM_SPEC] * 5,
        out_specs=VMEM_SPEC,
        compiler_params=PARAMS,
        cost_estimate=COST,
    )(scaled, give, *[resident(weight) for weight in weights])


def in_lanes(values):
    column = lanes(values.shape[0])
    block = jnp.zeros((values.shape[0], LANES), F32)
    for n, piece in enumerate(pieces(values)):
        block = jnp.where(column == n, piece, block)
    return block.astype(BF16)


def pair_sum_kernel(query_width, keep, got, total, *sent):
    place = whereabouts()
    both = keep[...] + got[...].astype(F32)
    total[...] = both
    rows = both.shape[0]
    main = both.shape[1] - LANES
    squares = keep[:, main : main + 1] + jnp.sum(
        got[:, main:].astype(F32), axis=1, keepdims=True
    )
    total[:, main:] = jnp.broadcast_to(squares, (rows, LANES))
    chips = (main - query_width) // HD
    column = lanes(rows)
    stats = in_lanes(squares)
    query = both[:, :query_width].astype(BF16)
    for hop, out in enumerate(sent, 1):
        chip = lax.rem(place[4] + hop, chips)
        block = pl.ds(pl.multiple_of(query_width + chip * HD, HD), HD)
        out[:, :query_width] = query
        out[:, query_width : query_width + HD] = total[:, block].astype(BF16)
        out[:, query_width + HD :] = stats


def pair_sum(keep, got, query_width, hops):
    rows = keep.shape[0]
    sent = jax.ShapeDtypeStruct((rows, query_width + HD + LANES), BF16)
    return pl.pallas_call(
        functools.partial(pair_sum_kernel, query_width),
        out_shape=[jax.ShapeDtypeStruct(keep.shape, F32)] + [sent] * hops,
        in_specs=[VMEM_SPEC] * 2,
        out_specs=[VMEM_SPEC] * (1 + hops),
        compiler_params=PARAMS,
    )(keep, got)


def lane_fold(fold, array):
    parts = [array[:, at : at + LANES] for at in range(0, array.shape[1], LANES)]
    return functools.reduce(fold, parts)


def row_max(arrays):
    folded = [lane_fold(jnp.maximum, array) for array in arrays]
    return jnp.max(functools.reduce(jnp.maximum, folded), axis=1, keepdims=True)


def against(rows, keys):
    return lax.dot_general(
        rows, keys, (((1,), (1,)), ((), ())), preferred_element_type=F32
    )


def weigh(scores, top, values):
    terms = [
        jnp.dot(
            jnp.exp2(score - top).astype(BF16),
            jnp.concatenate([value, jnp.ones_like(value)], axis=1),
            preferred_element_type=F32,
        )
        for score, value in zip(scores, values)
    ]
    both = functools.reduce(jnp.add, terms)
    return both[:, HD : HD + 1], both[:, :HD]


def attend_kernel(features, step, others, *refs):
    place = whereabouts()
    total_ref = refs[0]
    got = refs[1 : 1 + others]
    cos_ref, sin_ref, new_cos, new_sin, bias_ref = refs[1 + others : 6 + others]
    refs = refs[2:]
    own_prefix, own_suffix, *far = refs[4 + others : (10 if step == 0 else 8) + others]
    refs = refs[(10 if step == 0 else 8) + others :]
    old, (sent, stat, fresh) = refs[:step], refs[step : 3 + step]
    heads = own_prefix.shape[1]
    waits = []
    if step == 0:
        got_prefix, got_suffix, sems = refs[3:]
        waits = copied(halves(place, far, got_prefix, got_suffix), sems)
    else:
        got_prefix, got_suffix = far
    prefix = (own_prefix, got_prefix)
    suffix = (own_suffix, got_suffix)
    rows = total_ref.shape[0]
    width = total_ref.shape[1] - LANES
    query_width = width - 2 * heads * HD
    base, starts = place[1], (place[2], place[3])
    scale = LOG2E / math.sqrt(HD)

    stats = total_ref[:, width : width + 1]
    for ref in got:
        stats = stats + jnp.sum(ref[:, query_width + HD :].astype(F32), axis=1, keepdims=True)
    inverse = lax.rsqrt(stats / features + 1e-05)
    cosine = cos_ref[...]
    sine = sin_ref[...]

    def query_block(at):
        value = total_ref[:, at : at + HD]
        for ref in got:
            value = value + ref[:, at : at + HD].astype(F32)
        value = value * (inverse * scale)
        return (value * cosine + pltpu.roll(value, HD // 2, 1) * sine).astype(BF16)

    sample = lax.broadcasted_iota(jnp.int32, (rows, 1), 0)
    few_rows = SAMP_DEV * GROUP
    pick_row = lax.broadcasted_iota(jnp.int32, (few_rows, GROUP * rows), 0)
    pick_column = lax.broadcasted_iota(jnp.int32, (few_rows, GROUP * rows), 1)
    spot = (pick_row // SAMP_DEV) * rows + pick_row % SAMP_DEV
    picks = [(pick_column == spot + start).astype(F32).astype(BF16) for start in starts]
    column = lanes(rows)

    queries = [
        [query_block((head * GROUP + g) * HD) for g in range(GROUP)] for head in range(heads)
    ]
    packed = [jnp.concatenate(query, axis=0) for query in queries]
    span = 2 * SAMP_DEV
    mine = pl.ds(pl.multiple_of(query_width + place[4] * HD, HD), HD)
    new = total_ref[:, mine]
    for ref in got:
        new = new + ref[:, query_width : query_width + HD].astype(F32)
    vector_row = lax.broadcasted_iota(jnp.int32, (rows, 1), 0) % span
    new_inverse = jnp.zeros((rows, 1), F32)
    for i in range(span):
        one = jnp.sum(jnp.where(sample == base + i, inverse, 0.0), axis=0, keepdims=True)
        new_inverse = jnp.where(vector_row == i, one, new_inverse)
    new = new * new_inverse
    new = new * new_cos[...] + pltpu.roll(new, HD // 2, 1) * new_sin[...]
    half = rows // 2
    fresh[:rows] = new.astype(BF16)
    fresh[rows:] = jnp.concatenate([new[half:], new[:half]], axis=0).astype(BF16)
    padding = jnp.zeros((LANES - (step + 1) * rows, HD), BF16)
    new_keys = jnp.concatenate([ref[:rows] for ref in (*old, fresh)] + [padding], axis=0)
    new_values = jnp.concatenate([ref[rows:] for ref in (*old, fresh)] + [padding], axis=0)
    line = lax.broadcasted_iota(jnp.int32, (GROUP * rows, LANES), 0) % rows - base
    token = lax.broadcasted_iota(jnp.int32, (GROUP * rows, LANES), 1)
    new_scores = [
        jnp.where(
            (token < (step + 1) * rows) & (token % rows == line + head * span)
            & (line >= 0) & (line < span),
            against(packed[head], new_keys),
            -jnp.inf,
        )
        for head in range(heads)
    ]
    few = [
        [jnp.dot(pick, packed[head], preferred_element_type=F32).astype(BF16) for pick in picks]
        for head in range(heads)
    ]
    slots, page = own_suffix.shape[1], own_suffix.shape[3]
    length = own_prefix.shape[2]
    chunk = min(2048, length)
    pieces_of = [(src, at) for src in range(2) for at in range(0, length, chunk)]

    def pool(kind, src, head):
        return suffix[src][kind, :, head].reshape(slots * page, HD)

    near_scores = [[None] * 2 for _ in range(heads)]
    far_scores = [[None] * len(pieces_of) for _ in range(heads)]
    for src in range(2):
        if src == 1:
            for copy in waits[:2]:
                copy.wait()
        for head in range(heads):
            near_scores[head][src] = against(few[head][src], pool(0, src, head)) + bias_ref[src]
            for n, (whose, at) in enumerate(pieces_of):
                if whose == src:
                    far_scores[head][n] = against(
                        packed[head], prefix[src][0, head, at : at + chunk]
                    )
    near_tops = [[row_max([score]) for score in scores] for scores in near_scores]
    for head in range(heads):
        far_scores[head].append(new_scores[head])
    far_tops = [row_max(scores) for scores in far_scores]
    for copy in waits[2:]:
        copy.wait()
    near = [
        [
            weigh([near_scores[head][src]], near_tops[head][src], [pool(1, src, head)])
            for src in range(2)
        ]
        for head in range(heads)
    ]

    tops = jnp.zeros((rows, LANES), F32)
    totals = jnp.zeros((rows, LANES), F32)
    for head in range(heads):
        far_total, far_acc = weigh(
            far_scores[head],
            far_tops[head],
            [prefix[src][1, head, at : at + chunk] for src, at in pieces_of] + [new_values],
        )
        for g in range(GROUP):
            part = slice(g * rows, (g + 1) * rows)
            far_top = far_tops[head][part]
            near_top = jnp.full((rows, 1), -1e30, F32)
            total = jnp.zeros((rows, 1), F32)
            acc = jnp.zeros((rows, HD), F32)
            for src in range(2):
                for j in range(SAMP_DEV):
                    line = slice(g * SAMP_DEV + j, g * SAMP_DEV + j + 1)
                    here = sample == starts[src] + j
                    near_top = jnp.where(here, near_tops[head][src][line], near_top)
                    total = jnp.where(here, near[head][src][0][line], total)
                    acc = jnp.where(here, near[head][src][1][line], acc)
            top = jnp.maximum(far_top, near_top)
            far_weight = jnp.exp2(far_top - top)
            near_weight = jnp.exp2(near_top - top)
            total = total * near_weight + far_total[part] * far_weight
            acc = acc * near_weight + far_acc[part] * far_weight
            index = head * GROUP + g
            sent[:, index * HD : (index + 1) * HD] = acc.astype(BF16)
            tops = jnp.where(column == index, top, tops)
            totals = jnp.where(column == index, total, totals)
    many = heads * GROUP
    stat[:, :LANES] = tops
    stat[:, LANES:] = totals
    parts = [*pieces(tops), *pieces(totals)]
    packed_stats = parts[0]
    for n, part in enumerate(parts[1:], 1):
        packed_stats = packed_stats + pltpu.roll(part, n * many, 1)
    sent[:, many * HD :] = packed_stats.astype(BF16)


def attend(features, step, total, got, tables, caches, old):
    rows = total.shape[0]
    own, far = caches
    heads = own[0].shape[1]
    if step == 0:
        inputs = [resident(array) for array in own] + [in_hbm(array) for array in far]
        specs = [VMEM_SPEC] * 2 + [HBM_SPEC] * 4
        out_shape = [pltpu.VMEM(part.shape, BF16) for part in own]
        scratch = [pltpu.SemaphoreType.DMA((4,))]
    else:
        inputs = [resident(array) for array in (*own, *far)]
        specs = [VMEM_SPEC] * 4
        out_shape, scratch = [], []
    small = [total, *got, *tables]
    last = step == STEPS - 1
    if last:
        scratch = [pltpu.VMEM((2 * rows, HD), BF16)]
    else:
        out_shape = [jax.ShapeDtypeStruct((2 * rows, HD), BF16)] + out_shape
    return pl.pallas_call(
        functools.partial(attend_kernel, features, step, len(got)),
        out_shape=[
            jax.ShapeDtypeStruct((rows, heads * GROUP * HD + LANES), BF16),
            jax.ShapeDtypeStruct((rows, 2 * LANES), F32),
            *out_shape,
        ],
        in_specs=[VMEM_SPEC] * len(small) + specs + [VMEM_SPEC] * len(old),
        out_specs=[VMEM_SPEC] * (2 + len(out_shape)),
        scratch_shapes=scratch,
        compiler_params=LARGE_PARAMS,
    )(*small, *inputs, *old)


def merge_kernel(own, stat, *refs):
    got, out = refs[:-1], refs[-1]
    many = out.shape[1] // HD
    tops, totals = [stat[:, :LANES]], [stat[:, LANES:]]
    for ref in got:
        packed = ref[:, many * HD :].astype(F32)
        turns = [packed] + [pltpu.roll(packed, LANES - n * many, 1) for n in range(1, 6)]
        tops.append(turns[0] + turns[1] + turns[2])
        totals.append(turns[3] + turns[4] + turns[5])
    used = lanes(own.shape[0]) < many
    tops = [jnp.where(used, top, 0.0) for top in tops]
    top = functools.reduce(jnp.maximum, tops)
    weights = [jnp.exp2(each - top) for each in tops]
    total = functools.reduce(jnp.add, [w * t for w, t in zip(weights, totals)])
    share = 1.0 / jnp.where(used, total, 1.0)
    weights = [weight * share for weight in weights]
    for index in range(many):
        part = slice(index * HD, (index + 1) * HD)
        value = own[:, part].astype(F32) * weights[0][:, index : index + 1]
        for ref, weight in zip(got, weights[1:]):
            value = value + ref[:, part].astype(F32) * weight[:, index : index + 1]
        out[:, part] = value.astype(BF16)


def merge(own, stat, got):
    return pl.pallas_call(
        merge_kernel,
        out_shape=jax.ShapeDtypeStruct((own.shape[0], own.shape[1] - LANES), BF16),
        in_specs=[VMEM_SPEC] * (2 + len(got)),
        out_specs=VMEM_SPEC,
        compiler_params=PARAMS,
    )(own, stat, *got)


def near_output_kernel(mine, weight, out):
    place = whereabouts()
    half = mine.shape[1]
    rows = pl.ds(pl.multiple_of(place[0] * half, half), half)
    out[...] = jnp.dot(mine[...], weight[rows], preferred_element_type=F32)


def far_output_kernel(other, weight, near, out):
    place = whereabouts()
    half = other.shape[1]
    rows = pl.ds(pl.multiple_of((1 - place[0]) * half, half), half)
    total = near[...] + jnp.dot(other[...], weight[rows], preferred_element_type=F32)
    out[...] = total.astype(BF16)


def output(mine, weight):
    other = swapped(mine, "side")
    shape = (mine.shape[0], weight.shape[1])
    near = pl.pallas_call(
        near_output_kernel,
        out_shape=jax.ShapeDtypeStruct(shape, F32),
        in_specs=[VMEM_SPEC] * 2,
        out_specs=VMEM_SPEC,
        compiler_params=PARAMS,
        cost_estimate=COST,
    )(mine, resident(weight))
    return pl.pallas_call(
        far_output_kernel,
        out_shape=jax.ShapeDtypeStruct(shape, BF16),
        in_specs=[VMEM_SPEC] * 3,
        out_specs=VMEM_SPEC,
        compiler_params=PARAMS,
    )(other, resident(weight), near)


def swapped(array, axis):
    return lax.ppermute(array, axis, [(0, 1), (1, 0)])


def from_others(arrays, axis):
    size = lax.axis_size(axis)
    return [
        lax.ppermute(array, axis, [(i, (i + hop) % size) for i in range(size)])
        for hop, array in enumerate(arrays, 1)
    ]


def rotations(lengths, base):
    half = HD // 2
    freq = 500000.0 ** (-(jnp.arange(half, dtype=F32) * 2.0 / HD))
    position = (
        PREFIX + lengths[None, :] + jnp.arange(STEPS, dtype=jnp.int32)[:, None]
    ).astype(F32)
    angle = position[..., None] * freq
    cosine, sine = jnp.cos(angle), jnp.sin(angle)
    cosine = jnp.concatenate([cosine, cosine], axis=-1)
    sine = jnp.concatenate([-sine, sine], axis=-1)
    span = 2 * SAMP_DEV
    vectors = lengths.shape[0] // span
    new_cosine = lax.dynamic_slice_in_dim(cosine, base, span, 1)
    new_sine = lax.dynamic_slice_in_dim(sine, base, span, 1)
    turns = vectors // 2
    new_cosine = jnp.concatenate(
        [new_cosine] * turns + [jnp.ones_like(new_cosine)] * turns, axis=1
    )
    new_sine = jnp.concatenate([new_sine] * turns + [jnp.zeros_like(new_sine)] * turns, axis=1)
    return cosine, sine, new_cosine, new_sine


def local_split(
    hidden,
    gain,
    w_query,
    w_key,
    w_value,
    w_out,
    prefix_keys,
    prefix_values,
    suffix_keys,
    suffix_values,
    suffix_lengths,
    page_table,
):
    features = hidden.shape[1] * lax.axis_size(("seq", "side"))
    base = lax.axis_index("seq") * (2 * SAMP_DEV)
    pools = (prefix_keys, prefix_values, suffix_keys, suffix_values)
    weights = (w_query, w_key, w_value)
    far = [swapped(pool, "side") for pool in pools[2:]]
    gain_row = gain[None, :]
    query_width = w_query.shape[1] // 2
    hops = lax.axis_size("seq") - 1

    state = hidden
    update = jnp.zeros(hidden.shape, F32)
    rest = ()
    old = []
    for step in range(STEPS):
        if rest:
            give, scaled, state, update = give_project(state, gain_row, weights, rest)
            got_sum = swapped(give, "side")
            keep = keep_project(scaled, give, weights)
            total, *sent = pair_sum(keep, got_sum, query_width, hops)
        else:
            keep, give = first_project(state, gain_row, weights)
            got_sum = swapped(give, "side")
            got_sum, *given = lax.optimization_barrier((got_sum, *far, *pools[:2]))
            far = [swapped(pool, "side") for pool in given[2:]] + given[:2]
            total, *sent = pair_sum(keep, got_sum, query_width, hops)
            *sent, lengths, table = lax.optimization_barrier(
                (*sent, suffix_lengths, page_table)
            )
            turning = rotations(lengths, base)
            *own, out_weight, bias = load_caches(lengths, table, pools, w_out, sent[0])
        got = from_others(sent, "seq")
        tables = (*[each[step] for each in turning], bias)
        sent, stat, *kept = attend(
            features, step, total, got, tables, (own, far), old
        )
        far = kept[1:] or far
        got = from_others([sent] * hops, "seq")
        if not rest:
            weights = load(weights, stat)
            got, weights = lax.optimization_barrier((got, weights))
        old += kept[:1]
        mixed = merge(sent, stat, got)
        part = output(mixed, out_weight)
        rest = (update, part, swapped(part, "head"))
    delta = rest[1].astype(F32) + rest[2].astype(F32)
    return ((state.astype(F32) + delta).astype(BF16), update + delta)


def fits(mesh, args):
    heads = args[4].shape[1] // HD // mesh.shape["head"]
    return (
        mesh.shape["head"] == 2
        and mesh.shape["side"] == 2
        and heads % 2 == 0
        and args[6].shape[0] == mesh.shape["groups"]
        and heads // 2 * GROUP * 6 <= LANES
        and mesh.shape["seq"] == heads
        and args[0].shape[0] // mesh.shape["groups"] * STEPS <= LANES
    )


def solution(mesh):
    placed = (
        P("groups", ("seq", "side")),
        P(("seq", "side")),
        P(("seq", "side"), "head"),
        P(("seq", "side"), "head"),
        P(("seq", "side"), "head"),
        P("head", ("seq", "side")),
        P("groups", "head", ("seq", "side"), None),
        P("groups", "head", ("seq", "side"), None),
        P(("groups", "seq", "side"), "head", None, None),
        P(("groups", "seq", "side"), "head", None, None),
        P("groups"),
        P("groups", None),
    )

    def whole(*args):
        return jax.shard_map(
            local_split if fits(mesh, args) else local_any,
            mesh=mesh,
            in_specs=placed,
            out_specs=(P("groups", ("seq", "side")), P("groups", ("seq", "side"))),
            check_vma=False,
        )(*args)

    return whole
```
